512 devices in a mesh: ctx: 64 (over y, x, core), head: 8 (over z).
Axes of the slice: x: 4, y: 8, z: 8, core: 2. Of those that a mesh axis runs over, the one named last changes fastest.
Arguments:
- queries: bfloat16 [4096, 12288], P(('ctx', 'head')), may hold values from -8 to 8
- latent: bfloat16 [4096, 512], P(('ctx', 'head')), may hold values from -6 to 6
- rope_key: bfloat16 [4096, 64], P(('ctx', 'head')), may hold values from -8 to 8
- w_uk: bfloat16 [64, 512, 128], P('head'), may hold values from -0.25 to 0.25
- w_uv: bfloat16 [64, 512, 128], P('head'), may hold values from -0.25 to 0.25
- block_order: int32 [128], replicated, may hold values from 0 to 127, each once
Outputs:
- out: bfloat16 [4096, 8192], P(('ctx', 'head'))
The draws below stay inside these ranges and needn't reach their ends.
Inputs may be any that keep to these rules, and one draw needn't show every extreme that they name: `block_order`: each of 0 to 127 appears once.
All inputs are finite; a program needn't handle non-finite values.
Results may differ from the reference program's by a relative error of at most 0.009.
Values may be sent and summed in bfloat16 or wider, within the bound.
No kernel may reach another device: no remote copies, remote signals or barrier semaphores. Data moves between devices by JAX's collectives and lax.ppermute only.
A program may use at most 64 MiB of HBM per device.

```python
import jax
import jax.numpy as jnp
from jax import lax

HALF = 32
TOKENS = 4096
H = 64
DL = 512
DR = 64
DN = 128
DV = 128
N_CTX = 64


def draw_queries(key, part):
    key = jax.random.fold_in(key, 1)
    base = jnp.clip(jax.random.normal(key, (TOKENS, H, DN + DR)), -8.0, 8.0)
    return base.reshape(TOKENS, H * (DN + DR)).astype(jnp.bfloat16)


def draw_rope_key(key, part):
    key = jax.random.fold_in(key, 2)
    base = jnp.clip(jax.random.normal(key, (TOKENS, DR)), -8.0, 8.0)
    return base.astype(jnp.bfloat16)


def level_of(stream_key, dims, shards, smallest, top_value):
    def one(dim, parts):
        draws = jax.random.uniform(jax.random.fold_in(jax.random.fold_in(stream_key, 6), dim), (parts,), jnp.float32, smallest / len(shards), top_value / len(shards))
        return jnp.repeat(jnp.exp(draws), dims[dim] // parts).reshape((-1,) + (1,) * (len(dims) - dim - 1))

    factor_of = one(*shards[0])
    for cut in shards[1:]:
        factor_of = factor_of * one(*cut)
    return factor_of


def centred(key, dims, width, limit, shards=(), kind=jnp.bfloat16):
    values = jax.random.normal(key, dims, jnp.float32) * width
    if len(shards) > 0:
        values = level_of(key, dims, shards, -0.22, 0.18) * values
    return jnp.clip(values, min=-limit, max=limit).astype(kind)


def setup_inputs(seed: int = 0) -> dict:
    key_of = jax.random.split(jax.random.key(seed), 7)
    return {
        "queries": draw_queries(jax.random.fold_in(key_of[6], 71), 0),
        "latent": centred(key_of[1], (TOKENS, DL), 1.0, 6.0, ((0, 512),)),
        "rope_key": draw_rope_key(jax.random.fold_in(key_of[6], 71), 0),
        "w_uk": centred(key_of[3], (H, DL, DN), DL ** -0.5, 0.25, ((0, 8),)),
        "w_uv": centred(key_of[4], (H, DL, DV), DL ** -0.5, 0.25, ((0, 8),)),
        "block_order": jax.random.permutation(key_of[5], 2 * N_CTX).astype(jnp.int32),
    }


def reference(queries, latent, rope_key, w_uk, w_uv, block_order):
    block_count = 2 * N_CTX
    slot_ids = jnp.arange(block_count, dtype=jnp.int32)
    inverse = jnp.sum(jnp.where(block_order[None, :] == slot_ids[:, None], slot_ids[None, :], 0), axis=1).astype(jnp.int32)
    score_scale = (DN + DR) ** -0.5
    k_pos = jnp.arange(TOKENS, dtype=jnp.int32)
    k_row = (inverse[k_pos // HALF] * HALF + k_pos % HALF).astype(jnp.int32)
    k_lat = latent.astype(jnp.float32)[k_row]
    k_rope = rope_key.astype(jnp.float32)[k_row]
    absorb_wide = w_uk.astype(jnp.float32)
    value_wide = w_uv.astype(jnp.float32)

    def one_block(block_id):
        seq_block = jnp.sum(jnp.where(slot_ids == block_id, block_order, 0)).astype(jnp.int32)
        q_pos = seq_block * HALF + jnp.arange(HALF, dtype=jnp.int32)
        q_rows = lax.dynamic_slice_in_dim(queries, (block_id * HALF).astype(jnp.int32), HALF, 0)
        q_rows = q_rows.reshape(HALF, H, DN + DR).astype(jnp.float32)
        q_lat = jnp.einsum("thd,hld->thl", q_rows[:, :, :DN], absorb_wide).astype(jnp.bfloat16)
        q_lat = lax.optimization_barrier(q_lat).astype(jnp.float32)
        scores = jnp.einsum("thl,ul->thu", q_lat, k_lat) + jnp.einsum("thr,ur->thu", q_rows[:, :, DN:], k_rope)
        scores = scores * score_scale
        visible = (k_pos[None, :] <= q_pos[:, None])[:, None, :]
        row_max = jnp.max(jnp.where(visible, scores, -jnp.inf), axis=2, keepdims=True)
        exponent = jnp.where(visible, jnp.exp(scores - row_max), 0.0)
        row_total = jnp.sum(exponent, axis=2, keepdims=True)
        rounded = lax.optimization_barrier(exponent.astype(jnp.bfloat16)).astype(jnp.float32)
        o_lat = (jnp.einsum("thu,ul->thl", rounded, k_lat) / row_total).astype(jnp.bfloat16)
        o_lat = lax.optimization_barrier(o_lat).astype(jnp.float32)
        projected = jnp.einsum("thl,hlv->thv", o_lat, value_wide).astype(jnp.bfloat16)
        return projected.reshape(HALF, H * DV)

    result = lax.map(one_block, jnp.arange(block_count, dtype=jnp.int32))
    return result.reshape(TOKENS, H * DV)
```

```python
import functools

import jax
import jax.numpy as jnp
from jax import lax
from jax.experimental import pallas as pl
from jax.experimental.pallas import tpu as pltpu
from jax.sharding import PartitionSpec as P

HALF = 32
DL = 512
DR = 64
DN = 128
DV = 128
DQ = DN + DR
WIDE = 640
STAT = 128
NX = 4
NY = 8
NZ = 8
HEADS = 8
SPAN = 64
FLOOR_SCORE = -1e30
LOG2E = 1.4426950408889634
SCALE2 = DQ ** (-0.5) * LOG2E


def ctx_of(y, x, core):
    return ((y % NY) * NX + (x % NX)) * 2 + core


def along_x(step):
    return [
        (ctx_of(y, x, c), ctx_of(y, x + step, c))
        for y in range(NY)
        for x in range(NX)
        for c in range(2)
    ]


CORE_SWAP = [(i, i ^ 1) for i in range(NX * NY * 2)]
Y_GROUPS = [[ctx_of(y, x, c) for y in range(NY)] for x in range(NX) for c in range(2)]


def attend_kernel(place_ref, order_ref, q0, q1, q2, q3, kv_own, kv_sib, w_uk, w_uv, out_ref, keys, qs, mask, stat):
    me = place_ref[0]
    core = me % 2
    x = (me // 2) % NX
    y = me // (2 * NX)
    rows = NX * SPAN
    key_count = 2 * NY * SPAN
    keys[: NY * SPAN] = kv_own[...]
    keys[NY * SPAN :] = kv_sib[...]
    lane = lax.broadcasted_iota(jnp.int32, (1, key_count), 1)
    key_pos = lane % HALF
    for side in range(2):
        side_core = core if side == 0 else 1 - core
        for yy in range(NY):
            slot = (yy * NX + x) * 2 + side_core
            for half in range(2):
                which = (side * NY + yy) * 2 + half
                key_pos = key_pos + jnp.where(lane // HALF == which, order_ref[2 * slot + half] * HALF, 0)
    row = lax.broadcasted_iota(jnp.int32, (rows, 1), 0)
    q_pos = row % HALF
    for step in range(NX):
        slot = (y * NX + (x - step + NX) % NX) * 2 + core
        for half in range(2):
            q_pos = q_pos + jnp.where(row // HALF == 2 * step + half, order_ref[2 * slot + half] * HALF, 0)
    mask[...] = jnp.where(key_pos <= q_pos, 0.0, FLOOR_SCORE)
    for step, q in enumerate((q0, q1, q2, q3)):
        for h in range(HEADS):
            here = slice(step * SPAN, (step + 1) * SPAN)
            qs[h, here, :DN] = q[:, h * DQ : h * DQ + DN]
            qs[h, here, DN : DN + DR] = q[:, h * DQ + DN : (h + 1) * DQ]
            qs[h, here, DN + DR :] = jnp.zeros((SPAN, DR), jnp.bfloat16)
    stat[...] = jnp.zeros_like(stat)
    lanes = lax.broadcasted_iota(jnp.int32, (rows, STAT), 1)

    def head(h, carry):
        q_lat = lax.dot_general(
            qs[h, :, :DN], w_uk[h], (((1,), (1,)), ((), ())), preferred_element_type=jnp.float32
        ).astype(jnp.bfloat16)
        q_all = jnp.concatenate([q_lat, qs[h, :, DN:]], axis=1)
        scores = lax.dot_general(
            q_all, keys[...], (((1,), (1,)), ((), ())), preferred_element_type=jnp.float32
        )
        scores = scores * SCALE2 + mask[...]
        top = jnp.max(scores, axis=1, keepdims=True)
        weight = jnp.exp2(scores - top)
        total = jnp.sum(weight, axis=1, keepdims=True)
        lat = jnp.dot(weight.astype(jnp.bfloat16), keys[:, :DL], preferred_element_type=jnp.float32)
        o_lat = (lat / total).astype(jnp.bfloat16)
        proj = jnp.dot(o_lat, w_uv[h], preferred_element_type=jnp.float32).astype(jnp.bfloat16)
        for step in range(NX):
            out_ref[step, :, pl.ds(pl.multiple_of(h * DV, DV), DV)] = proj[step * SPAN : (step + 1) * SPAN]
        level = top + jnp.log2(total)
        stat[...] = jnp.where(lanes % HEADS == h, level, stat[...])
        return carry

    lax.fori_loop(0, HEADS, head, 0)
    level = stat[...]
    high = level.astype(jnp.bfloat16)
    rest = level - high.astype(jnp.float32)
    middle = rest.astype(jnp.bfloat16)
    low = (rest - middle.astype(jnp.float32)).astype(jnp.bfloat16)
    part = lanes // HEADS
    packed = jnp.where(
        part == 0,
        high.astype(jnp.float32),
        jnp.where(part == 1, middle.astype(jnp.float32), jnp.where(part == 2, low.astype(jnp.float32), 0.0)),
    ).astype(jnp.bfloat16)
    for step in range(NX):
        out_ref[step, :, HEADS * DV :] = packed[step * SPAN : (step + 1) * SPAN]


def attend(place, order, qs, kv_own, kv_sib, w_uk, w_uv):
    vmem = pl.BlockSpec(memory_space=pltpu.VMEM)
    smem = pl.BlockSpec(memory_space=pltpu.SMEM)
    rows = NX * SPAN
    key_count = 2 * NY * SPAN
    return pl.pallas_call(
        attend_kernel,
        out_shape=jax.ShapeDtypeStruct((NX, SPAN, HEADS * DV + STAT), jnp.bfloat16),
        in_specs=[smem, smem] + [vmem] * 8,
        out_specs=vmem,
        scratch_shapes=[
            pltpu.VMEM((key_count, WIDE), jnp.bfloat16),
            pltpu.VMEM((HEADS, rows, DN + 2 * DR), jnp.bfloat16),
            pltpu.VMEM((rows, key_count), jnp.float32),
            pltpu.VMEM((rows, STAT), jnp.float32),
        ],
        compiler_params=pltpu.CompilerParams(vmem_limit_bytes=32 * 1024 * 1024),
        cost_estimate=pl.CostEstimate(flops=6_000_000_000, bytes_accessed=5_000_000, transcendentals=2_000_000),
    )(place, order, *qs, kv_own, kv_sib, w_uk, w_uv)


def merge_kernel(p0, p1, p2, p3, out_ref):
    parts = (p0, p1, p2, p3)
    levels = []
    for p in parts:
        pieces = p[:, HEADS * DV :].astype(jnp.float32)
        levels.append(pieces[:, :HEADS] + pieces[:, HEADS : 2 * HEADS] + pieces[:, 2 * HEADS : 3 * HEADS])
    top = functools.reduce(jnp.maximum, levels)
    shares = [jnp.exp2(level - top) for level in levels]
    whole = functools.reduce(jnp.add, shares)
    shares = [share / whole for share in shares]
    for h in range(HEADS):
        cols = slice(h * DV, (h + 1) * DV)
        acc = jnp.zeros((SPAN, DV), jnp.float32)
        for p, share in zip(parts, shares):
            acc = acc + share[:, h : h + 1] * p[:, cols].astype(jnp.float32)
        out_ref[:, cols] = acc.astype(jnp.bfloat16)


def merge(parts):
    vmem = pl.BlockSpec(memory_space=pltpu.VMEM)
    return pl.pallas_call(
        merge_kernel,
        out_shape=jax.ShapeDtypeStruct((SPAN, HEADS * DV), jnp.bfloat16),
        in_specs=[vmem] * NX,
        out_specs=vmem,
        cost_estimate=pl.CostEstimate(flops=1_000_000, bytes_accessed=800_000, transcendentals=2000),
    )(*parts)


def copies(value, count):
    return jnp.broadcast_to(value[None], (count,) + value.shape)


def on_device(queries, latent, rope_key, w_uk, w_uv, block_order):
    place = lax.axis_index("ctx").astype(jnp.int32).reshape(1)
    kv = jnp.concatenate([latent, rope_key, jnp.zeros_like(rope_key)], axis=1)
    kv = lax.all_to_all(copies(kv, NZ), "head", split_axis=0, concat_axis=0, tiled=True)
    kv = kv.reshape(SPAN, WIDE)
    kv = lax.all_to_all(
        copies(kv, NY), "ctx", split_axis=0, concat_axis=0, tiled=True, axis_index_groups=Y_GROUPS
    )
    kv_own = kv.reshape(NY * SPAN, WIDE)
    kv_sib = lax.ppermute(kv_own, "ctx", CORE_SWAP)
    q_own = lax.all_to_all(queries, "head", split_axis=1, concat_axis=0, tiled=True)
    qs = [q_own] + [lax.ppermute(q_own, "ctx", along_x(step)) for step in range(1, NX)]
    partial = attend(place, block_order, qs, kv_own, kv_sib, w_uk, w_uv)
    parts = [partial[0]] + [lax.ppermute(partial[step], "ctx", along_x(-step)) for step in range(1, NX)]
    merged = merge(parts)
    return lax.all_to_all(merged, "head", split_axis=0, concat_axis=1, tiled=True)


def solution(mesh):
    in_specs = (
        P(("ctx", "head"), None),
        P(("ctx", "head"), None),
        P(("ctx", "head"), None),
        P("head", None, None),
        P("head", None, None),
        P(),
    )
    out_specs = P(("ctx", "head"), None)
    return jax.shard_map(
        on_device, mesh=mesh, in_specs=in_specs, out_specs=out_specs, check_vma=False
    )
```

```python
import functools

import jax
import jax.numpy as jnp
from jax import lax
from jax.experimental import pallas as pl
from jax.experimental.pallas import tpu as pltpu
from jax.sharding import PartitionSpec as P

HALF = 32
DL = 512
DR = 64
DN = 128
DV = 128
DQ = DN + DR
WIDE = 640
STAT = 128
EXTRA = 128
NX = 4
NY = 8
NZ = 8
HEADS = 8
SPAN = 64
FLOOR_SCORE = -1e30
LOG2E = 1.4426950408889634
SCALE2 = DQ ** (-0.5) * LOG2E


def ctx_of(y, x, core):
    return ((y % NY) * NX + (x % NX)) * 2 + core


def along_x(step):
    return [
        (ctx_of(y, x, c), ctx_of(y, x + step, c))
        for y in range(NY)
        for x in range(NX)
        for c in range(2)
    ]


CORE_SWAP = [(i, i ^ 1) for i in range(NX * NY * 2)]
Y_GROUPS = [[ctx_of(y, x, c) for y in range(NY)] for x in range(NX) for c in range(2)]


def prepare_kernel(place_ref, order_ref, q0, q1, q2, q3, w_uk, out_ref, nope):
    me = place_ref[0]
    core = me % 2
    x = (me // 2) % NX
    y = me // (2 * NX)
    blocks = 2 * NY * SPAN // HALF
    lane = lax.broadcasted_iota(jnp.int32, (HALF, EXTRA), 1)
    token = lax.broadcasted_iota(jnp.int32, (HALF, EXTRA), 0)
    key_block = jnp.zeros((HALF, EXTRA), jnp.int32)
    for which in range(blocks):
        side_core = core if which < blocks // 2 else 1 - core
        slot = (((which // 2) % NY) * NX + x) * 2 + side_core
        key_block = jnp.where(lane == which, order_ref[2 * slot + which % 2], key_block)
    for step, q in enumerate((q0, q1, q2, q3)):
        slot = (y * NX + (x - step + NX) % NX) * 2 + core
        here = slice(step * SPAN, (step + 1) * SPAN)
        floors = []
        for half in range(2):
            ahead = (lane < blocks) & (key_block > order_ref[2 * slot + half])
            if step == 0:
                own = lane - blocks - half * HALF
                ahead = ahead | ((own >= 0) & (own < HALF) & (own > token))
            floors.append(jnp.where(ahead, FLOOR_SCORE, 0.0))
        floor = jnp.concatenate(floors, axis=0).astype(jnp.bfloat16)
        for h in range(HEADS):
            nope[h, here] = q[:, h * DQ : h * DQ + DN]
            out_ref[h, here, DL : DL + DR] = q[:, h * DQ + DN : (h + 1) * DQ]
            out_ref[h, here, DL + DR : WIDE] = jnp.zeros((SPAN, DR), jnp.bfloat16)
            out_ref[h, here, WIDE:] = floor
    for h in range(HEADS):
        out_ref[h, :, :DL] = lax.dot_general(
            nope[h], w_uk[h], (((1,), (1,)), ((), ())), preferred_element_type=jnp.float32
        ).astype(jnp.bfloat16)


def prepare(place, order, qs, w_uk):
    vmem = pl.BlockSpec(memory_space=pltpu.VMEM)
    smem = pl.BlockSpec(memory_space=pltpu.SMEM)
    rows = NX * SPAN
    return pl.pallas_call(
        prepare_kernel,
        out_shape=jax.ShapeDtypeStruct((HEADS, rows, WIDE + EXTRA), jnp.bfloat16),
        in_specs=[smem, smem] + [vmem] * 5,
        out_specs=vmem,
        scratch_shapes=[pltpu.VMEM((HEADS, rows, DN), jnp.bfloat16)],
        compiler_params=pltpu.CompilerParams(vmem_limit_bytes=16 * 1024 * 1024),
        cost_estimate=pl.CostEstimate(flops=4_000_000_000, bytes_accessed=6_000_000, transcendentals=0),
    )(place, order, *qs, w_uk)


def attend_kernel(place_ref, q_ref, kv_own, kv_sib, w_uv, out0, out1, out2, out3, keys, stat):
    outs = (out0, out1, out2, out3)
    y = place_ref[0] // (2 * NX)
    rows = NX * SPAN
    key_count = 2 * NY * SPAN
    blocks = key_count // HALF
    keys[: NY * SPAN, :WIDE] = kv_own[...]
    keys[NY * SPAN :, :WIDE] = kv_sib[...]
    key = lax.broadcasted_iota(jnp.int32, (key_count, EXTRA), 0)
    col = lax.broadcasted_iota(jnp.int32, (key_count, EXTRA), 1)
    own_first = 2 * y
    own_col = blocks + key - own_first * HALF
    in_own = (key // HALF == own_first) | (key // HALF == own_first + 1)
    ones = (col == key // HALF) | (in_own & (col == own_col))
    keys[:, WIDE:] = jnp.where(ones, 1.0, 0.0).astype(jnp.bfloat16)
    stat[...] = jnp.zeros_like(stat)
    lanes = lax.broadcasted_iota(jnp.int32, (rows, STAT), 1)

    def pair(p, carry):
        heads = [2 * p, 2 * p + 1]
        scores = [
            lax.dot_general(q_ref[h], keys[...], (((1,), (1,)), ((), ())), preferred_element_type=jnp.float32)
            for h in heads
        ]
        levels = []
        for h, s in zip(heads, scores):
            top = jnp.max(s, axis=1, keepdims=True)
            weight = jnp.exp2((s - top) * SCALE2)
            total = jnp.sum(weight, axis=1, keepdims=True)
            lat = jnp.dot(weight.astype(jnp.bfloat16), keys[:, :DL], preferred_element_type=jnp.float32)
            o_lat = (lat * (1.0 / total)).astype(jnp.bfloat16)
            proj = jnp.dot(o_lat, w_uv[h], preferred_element_type=jnp.float32).astype(jnp.bfloat16)
            for step in range(NX):
                outs[step][:, pl.ds(pl.multiple_of(h * DV, DV), DV)] = proj[step * SPAN : (step + 1) * SPAN]
            levels.append(top * SCALE2 + jnp.log2(total))
        held = stat[...]
        for h, level in zip(heads, levels):
            held = jnp.where(lanes % HEADS == h, level, held)
        stat[...] = held
        return carry

    lax.fori_loop(0, HEADS // 2, pair, 0)
    level = stat[...]
    high = level.astype(jnp.bfloat16)
    rest = level - high.astype(jnp.float32)
    middle = rest.astype(jnp.bfloat16)
    low = (rest - middle.astype(jnp.float32)).astype(jnp.bfloat16)
    part = lanes // HEADS
    packed = jnp.where(
        part == 0,
        high.astype(jnp.float32),
        jnp.where(part == 1, middle.astype(jnp.float32), jnp.where(part == 2, low.astype(jnp.float32), 0.0)),
    ).astype(jnp.bfloat16)
    for step in range(NX):
        outs[step][:, HEADS * DV :] = packed[step * SPAN : (step + 1) * SPAN]


def attend(place, q_all, kv_own, kv_sib, w_uv):
    vmem = pl.BlockSpec(memory_space=pltpu.VMEM)
    smem = pl.BlockSpec(memory_space=pltpu.SMEM)
    rows = NX * SPAN
    key_count = 2 * NY * SPAN
    return pl.pallas_call(
        attend_kernel,
        out_shape=[jax.ShapeDtypeStruct((SPAN, HEADS * DV + STAT), jnp.bfloat16)] * NX,
        in_specs=[smem] + [vmem] * 4,
        out_specs=[vmem] * NX,
        scratch_shapes=[
            pltpu.VMEM((key_count, WIDE + EXTRA), jnp.bfloat16),
            pltpu.VMEM((rows, STAT), jnp.float32),
        ],
        compiler_params=pltpu.CompilerParams(vmem_limit_bytes=24 * 1024 * 1024),
        cost_estimate=pl.CostEstimate(flops=6_000_000_000, bytes_accessed=5_000_000, transcendentals=2_000_000),
    )(place, q_all, kv_own, kv_sib, w_uv)


def merge_kernel(p0, p1, p2, p3, out_ref):
    parts = (p0, p1, p2, p3)
    levels = []
    for p in parts:
        pieces = p[:, HEADS * DV :].astype(jnp.float32)
        levels.append(pieces[:, :HEADS] + pieces[:, HEADS : 2 * HEADS] + pieces[:, 2 * HEADS : 3 * HEADS])
    top = functools.reduce(jnp.maximum, levels)
    shares = [jnp.exp2(level - top) for level in levels]
    whole = functools.reduce(jnp.add, shares)
    shares = [share / whole for share in shares]
    for h in range(HEADS):
        cols = slice(h * DV, (h + 1) * DV)
        acc = jnp.zeros((SPAN, DV), jnp.float32)
        for p, share in zip(parts, shares):
            acc = acc + share[:, h : h + 1] * p[:, cols].astype(jnp.float32)
        out_ref[:, cols] = acc.astype(jnp.bfloat16)


def merge(parts):
    vmem = pl.BlockSpec(memory_space=pltpu.VMEM)
    return pl.pallas_call(
        merge_kernel,
        out_shape=jax.ShapeDtypeStruct((SPAN, HEADS * DV), jnp.bfloat16),
        in_specs=[vmem] * NX,
        out_specs=vmem,
        cost_estimate=pl.CostEstimate(flops=1_000_000, bytes_accessed=800_000, transcendentals=2000),
    )(*parts)


def copies(value, count):
    return jnp.broadcast_to(value[None], (count,) + value.shape)


def on_device(queries, latent, rope_key, w_uk, w_uv, block_order):
    place = lax.axis_index("ctx").astype(jnp.int32).reshape(1)
    kv = jnp.concatenate([latent, rope_key, jnp.zeros_like(rope_key)], axis=1)
    both = jnp.concatenate([queries.reshape(8, NZ, HEADS * DQ).swapaxes(0, 1), copies(kv, NZ)], axis=2)
    both = lax.all_to_all(both, "head", split_axis=0, concat_axis=0, tiled=True).reshape(SPAN, HEADS * DQ + WIDE)
    q_own = both[:, : HEADS * DQ]
    kv = lax.all_to_all(
        copies(both[:, HEADS * DQ :], NY), "ctx", split_axis=0, concat_axis=0, tiled=True, axis_index_groups=Y_GROUPS
    )
    kv_own = kv.reshape(NY * SPAN, WIDE)
    kv_sib = lax.ppermute(kv_own, "ctx", CORE_SWAP)
    qs = [q_own] + [lax.ppermute(q_own, "ctx", along_x(step)) for step in range(1, NX)]
    q_all = prepare(place, block_order, qs, w_uk)
    partial = attend(place, q_all, kv_own, kv_sib, w_uv)
    parts = [partial[0]] + [lax.ppermute(partial[step], "ctx", along_x(-step)) for step in range(1, NX)]
    merged = merge(parts)
    return lax.all_to_all(merged, "head", split_axis=0, concat_axis=1, tiled=True)


def solution(mesh):
    in_specs = (
        P(("ctx", "head"), None),
        P(("ctx", "head"), None),
        P(("ctx", "head"), None),
        P("head", None, None),
        P("head", None, None),
        P(),
    )
    out_specs = P(("ctx", "head"), None)
    return jax.shard_map(
        on_device, mesh=mesh, in_specs=in_specs, out_specs=out_specs, check_vma=False
    )
```

```python
import functools

import jax
import jax.numpy as jnp
from jax import lax
from jax.experimental import pallas as pl
from jax.experimental.pallas import tpu as pltpu
from jax.sharding import PartitionSpec as P

HALF = 32
DL = 512
DR = 64
DN = 128
DV = 128
DQ = DN + DR
WIDE = 640
STAT = 128
EXTRA = 128
NX = 4
NY = 8
NZ = 8
HEADS = 8
SPAN = 64
LANES = 128
PACKED = DL // LANES * SPAN + HALF
FLOOR_SCORE = -1e30
LOG2E = 1.4426950408889634
SCALE2 = DQ ** (-0.5) * LOG2E


def ctx_of(y, x, core):
    return ((y % NY) * NX + (x % NX)) * 2 + core


def along_x(step):
    return [
        (ctx_of(y, x, c), ctx_of(y, x + step, c))
        for y in range(NY)
        for x in range(NX)
        for c in range(2)
    ]


CORE_SWAP = [(i, i ^ 1) for i in range(NX * NY * 2)]
XZ_GROUPS = [
    [ctx_of(y, x, c) * NZ + z for x in range(NX) for z in range(NZ)] for y in range(NY) for c in range(2)
]
Y_GROUPS = [[ctx_of(y, x, c) for y in range(NY)] for x in range(NX) for c in range(2)]


def pack_kernel(both_ref, q_ref, kv_ref):
    q_ref[...] = both_ref[:, : HEADS * DQ]
    rope = both_ref[:, HEADS * DQ + DL : HEADS * DQ + DL + DR]
    for to in range(NY):
        for j in range(DL // LANES):
            col = HEADS * DQ + j * LANES
            kv_ref[to, j * SPAN : (j + 1) * SPAN] = both_ref[:, col : col + LANES]
        kv_ref[to, PACKED - HALF :, :DR] = rope[:HALF]
        kv_ref[to, PACKED - HALF :, DR:] = rope[HALF:]


def pack(both):
    vmem = pl.BlockSpec(memory_space=pltpu.VMEM)
    return pl.pallas_call(
        pack_kernel,
        out_shape=[
            jax.ShapeDtypeStruct((SPAN, HEADS * DQ), jnp.bfloat16),
            jax.ShapeDtypeStruct((NY, PACKED, LANES), jnp.bfloat16),
        ],
        in_specs=[vmem],
        out_specs=[vmem] * 2,
        compiler_params=pltpu.CompilerParams(vmem_limit_bytes=8 * 1024 * 1024),
        cost_estimate=pl.CostEstimate(flops=4_000_000_000, bytes_accessed=1_000_000, transcendentals=0),
    )(both)


def prepare_kernel(info_ref, q0, q1, q2, q3, w_uk, out_ref, nope):
    me = info_ref[0]
    core = me % 2
    x = (me // 2) % NX
    y = me // (2 * NX)
    blocks = 2 * NY * SPAN // HALF
    lane = lax.broadcasted_iota(jnp.int32, (HALF, EXTRA), 1)
    token = lax.broadcasted_iota(jnp.int32, (HALF, EXTRA), 0)
    key_block = jnp.zeros((HALF, EXTRA), jnp.int32)
    for which in range(blocks):
        side_core = core if which < blocks // 2 else 1 - core
        slot = (((which // 2) % NY) * NX + x) * 2 + side_core
        key_block = jnp.where(lane == which, info_ref[1 + 2 * slot + which % 2], key_block)
    for step, q in enumerate((q0, q1, q2, q3)):
        slot = (y * NX + (x - step + NX) % NX) * 2 + core
        here = slice(step * SPAN, (step + 1) * SPAN)
        floors = []
        for half in range(2):
            ahead = (lane < blocks) & (key_block > info_ref[1 + 2 * slot + half])
            if step == 0:
                own = lane - blocks - half * HALF
                ahead = ahead | ((own >= 0) & (own < HALF) & (own > token))
            floors.append(jnp.where(ahead, FLOOR_SCORE, 0.0))
        floor = jnp.concatenate(floors, axis=0).astype(jnp.bfloat16)
        for h in range(HEADS):
            nope[h, here] = q[:, h * DQ : h * DQ + DN]
            out_ref[h, here, DL : DL + DR] = q[:, h * DQ + DN : (h + 1) * DQ]
            out_ref[h, here, DL + DR : WIDE] = jnp.zeros((SPAN, DR), jnp.bfloat16)
            out_ref[h, here, WIDE:] = floor
    for h in range(HEADS):
        out_ref[h, :, :DL] = lax.dot_general(
            nope[h], w_uk[h], (((1,), (1,)), ((), ())), preferred_element_type=jnp.float32
        ).astype(jnp.bfloat16)


def prepare(info, qs, w_uk):
    vmem = pl.BlockSpec(memory_space=pltpu.VMEM)
    smem = pl.BlockSpec(memory_space=pltpu.SMEM)
    rows = NX * SPAN
    return pl.pallas_call(
        prepare_kernel,
        out_shape=jax.ShapeDtypeStruct((HEADS, rows, WIDE + EXTRA), jnp.bfloat16),
        in_specs=[smem] + [vmem] * 5,
        out_specs=vmem,
        scratch_shapes=[pltpu.VMEM((HEADS, rows, DN), jnp.bfloat16)],
        compiler_params=pltpu.CompilerParams(vmem_limit_bytes=16 * 1024 * 1024),
        cost_estimate=pl.CostEstimate(flops=4_000_000_000, bytes_accessed=6_000_000, transcendentals=0),
    )(info, *qs, w_uk)


def fill_keys(keys, kv, first, own_block):
    count = NY * SPAN
    blocks = 2 * count // HALF
    for b in range(NY):
        here = slice(b * SPAN, (b + 1) * SPAN)
        for j in range(DL // LANES):
            keys[here, j * LANES : (j + 1) * LANES] = kv[b, j * SPAN : (j + 1) * SPAN]
        keys[b * SPAN : b * SPAN + HALF, DL : DL + DR] = kv[b, PACKED - HALF :, :DR]
        keys[b * SPAN + HALF : (b + 1) * SPAN, DL : DL + DR] = kv[b, PACKED - HALF :, DR:]
    keys[:, DL + DR : WIDE] = jnp.zeros((count, WIDE - DL - DR), jnp.bfloat16)
    key = lax.broadcasted_iota(jnp.int32, (count, EXTRA), 0)
    col = lax.broadcasted_iota(jnp.int32, (count, EXTRA), 1)
    ones = col == key // HALF + first
    if own_block is not None:
        in_own = (key // HALF == own_block) | (key // HALF == own_block + 1)
        ones = ones | (in_own & (col == blocks + key - own_block * HALF))
    keys[:, WIDE:] = jnp.where(ones, 1.0, 0.0).astype(jnp.bfloat16)


def scores_of(q, keys):
    return lax.dot_general(q, keys[...], (((1,), (1,)), ((), ())), preferred_element_type=jnp.float32)


def own_kernel(place_ref, q_ref, kv, lat_ref, top_ref, total_ref, keys):
    y = place_ref[0] // (2 * NX)
    rows = NX * SPAN
    fill_keys(keys, kv, 0, 2 * y)

    def pair(p, carry):
        heads = [2 * p, 2 * p + 1]
        scores = [scores_of(q_ref[h], keys) for h in heads]
        for h, s in zip(heads, scores):
            top = jnp.max(s, axis=1, keepdims=True)
            weight = jnp.exp2((s - top) * SCALE2)
            total = jnp.sum(weight, axis=1, keepdims=True)
            lat_ref[h] = jnp.dot(weight.astype(jnp.bfloat16), keys[:, :DL], preferred_element_type=jnp.float32)
            top_ref[h] = jnp.broadcast_to(top, (rows, STAT))
            total_ref[h] = jnp.broadcast_to(total, (rows, STAT))
        return carry

    lax.fori_loop(0, HEADS // 2, pair, 0)


def attend_own(place, q_all, kv):
    vmem = pl.BlockSpec(memory_space=pltpu.VMEM)
    smem = pl.BlockSpec(memory_space=pltpu.SMEM)
    rows = NX * SPAN
    return pl.pallas_call(
        own_kernel,
        out_shape=[
            jax.ShapeDtypeStruct((HEADS, rows, DL), jnp.float32),
            jax.ShapeDtypeStruct((HEADS, rows, STAT), jnp.float32),
            jax.ShapeDtypeStruct((HEADS, rows, STAT), jnp.float32),
        ],
        in_specs=[smem] + [vmem] * 2,
        out_specs=[vmem] * 3,
        scratch_shapes=[pltpu.VMEM((NY * SPAN, WIDE + EXTRA), jnp.bfloat16)],
        compiler_params=pltpu.CompilerParams(vmem_limit_bytes=20 * 1024 * 1024),
        cost_estimate=pl.CostEstimate(flops=20_000_000_000, bytes_accessed=5_000_000, transcendentals=1_000_000),
    )(place, q_all, kv)


def other_kernel(place_ref, q_ref, kv, lat_ref, top_ref, total_ref, w_uv, out_ref, keys, stat):
    x = (place_ref[0] // 2) % NX
    rows = NX * SPAN
    fill_keys(keys, kv, NY * SPAN // HALF, None)
    stat[...] = jnp.zeros_like(stat)
    lanes = lax.broadcasted_iota(jnp.int32, (rows, STAT), 1)

    def pair(p, carry):
        heads = [2 * p, 2 * p + 1]
        scores = [scores_of(q_ref[h], keys) for h in heads]
        levels = []
        for h, s in zip(heads, scores):
            old_top = top_ref[h, :, :1]
            old_total = total_ref[h, :, :1]
            top = jnp.maximum(old_top, jnp.max(s, axis=1, keepdims=True))
            shrink = jnp.exp2((old_top - top) * SCALE2)
            weight = jnp.exp2((s - top) * SCALE2)
            total = old_total * shrink + jnp.sum(weight, axis=1, keepdims=True)
            lat = jnp.dot(weight.astype(jnp.bfloat16), keys[:, :DL], preferred_element_type=jnp.float32)
            share = 1.0 / total
            o_lat = (lat * share + lat_ref[h] * (shrink * share)).astype(jnp.bfloat16)
            proj = jnp.dot(o_lat, w_uv[h], preferred_element_type=jnp.float32).astype(jnp.bfloat16)
            for step in range(NX):
                to = (x + NX - step) % NX
                out_ref[to, :, pl.ds(pl.multiple_of(h * DV, DV), DV)] = proj[step * SPAN : (step + 1) * SPAN]
            levels.append(top * SCALE2 + jnp.log2(total))
        held = stat[...]
        for h, level in zip(heads, levels):
            held = jnp.where(lanes % HEADS == h, level, held)
        stat[...] = held
        return carry

    lax.fori_loop(0, HEADS // 2, pair, 0)
    level = stat[...]
    high = level.astype(jnp.bfloat16)
    rest = level - high.astype(jnp.float32)
    middle = rest.astype(jnp.bfloat16)
    low = (rest - middle.astype(jnp.float32)).astype(jnp.bfloat16)
    part = lanes // HEADS
    packed = jnp.where(
        part == 0,
        high.astype(jnp.float32),
        jnp.where(part == 1, middle.astype(jnp.float32), jnp.where(part == 2, low.astype(jnp.float32), 0.0)),
    ).astype(jnp.bfloat16)
    for step in range(NX):
        to = (x + NX - step) % NX
        out_ref[to, :, HEADS * DV :] = packed[step * SPAN : (step + 1) * SPAN]


def attend_other(place, q_all, kv, state, w_uv):
    vmem = pl.BlockSpec(memory_space=pltpu.VMEM)
    smem = pl.BlockSpec(memory_space=pltpu.SMEM)
    rows = NX * SPAN
    return pl.pallas_call(
        other_kernel,
        out_shape=jax.ShapeDtypeStruct((NX, SPAN, HEADS * DV + STAT), jnp.bfloat16),
        in_specs=[smem] + [vmem] * 6,
        out_specs=vmem,
        scratch_shapes=[
            pltpu.VMEM((NY * SPAN, WIDE + EXTRA), jnp.bfloat16),
            pltpu.VMEM((rows, STAT), jnp.float32),
        ],
        compiler_params=pltpu.CompilerParams(vmem_limit_bytes=20 * 1024 * 1024),
        cost_estimate=pl.CostEstimate(flops=4_000_000_000, bytes_accessed=5_000_000, transcendentals=1_000_000),
    )(place, q_all, kv, *state, w_uv)


def merge_kernel(p_ref, out_ref):
    for z in range(NZ):
        levels = []
        for x in range(NX):
            pieces = p_ref[x, z, :, HEADS * DV :].astype(jnp.float32)
            levels.append(pieces[:, :HEADS] + pieces[:, HEADS : 2 * HEADS] + pieces[:, 2 * HEADS : 3 * HEADS])
        top = functools.reduce(jnp.maximum, levels)
        shares = [jnp.exp2(level - top) for level in levels]
        whole = functools.reduce(jnp.add, shares)
        shares = [share / whole for share in shares]
        for h in range(HEADS):
            acc = jnp.zeros((SPAN // NZ, DV), jnp.float32)
            for x in range(NX):
                acc = acc + shares[x][:, h : h + 1] * p_ref[x, z, :, h * DV : (h + 1) * DV].astype(jnp.float32)
            out_ref[:, (z * HEADS + h) * DV : (z * HEADS + h + 1) * DV] = acc.astype(jnp.bfloat16)


def merge(parts):
    vmem = pl.BlockSpec(memory_space=pltpu.VMEM)
    return pl.pallas_call(
        merge_kernel,
        out_shape=jax.ShapeDtypeStruct((SPAN // NZ, NZ * HEADS * DV), jnp.bfloat16),
        in_specs=[vmem],
        out_specs=vmem,
        cost_estimate=pl.CostEstimate(flops=1_000_000, bytes_accessed=800_000, transcendentals=2000),
    )(parts)


def copies(value, count):
    return jnp.broadcast_to(value[None], (count,) + value.shape)


def on_device(queries, latent, rope_key, w_uk, w_uv, block_order):
    place = lax.axis_index("ctx").astype(jnp.int32).reshape(1)
    info = jnp.concatenate([place, block_order])
    kv = jnp.concatenate([latent, rope_key, jnp.zeros_like(rope_key)], axis=1)
    both = jnp.concatenate([queries.reshape(8, NZ, HEADS * DQ).swapaxes(0, 1), copies(kv, NZ)], axis=2)
    both = lax.all_to_all(both, "head", split_axis=0, concat_axis=0, tiled=True).reshape(SPAN, HEADS * DQ + WIDE)
    q_own, kv = pack(both)
    kv_own = lax.all_to_all(kv, "ctx", split_axis=0, concat_axis=0, tiled=True, axis_index_groups=Y_GROUPS)
    kv_sib = lax.ppermute(kv_own, "ctx", CORE_SWAP)
    qs = [q_own] + [lax.ppermute(q_own, "ctx", along_x(step)) for step in range(1, NX)]
    q_all = prepare(info, qs, w_uk)
    state = attend_own(place, q_all, kv_own)
    partial = attend_other(place, q_all, kv_sib, state, w_uv)
    rows = SPAN // NZ
    partial = partial.reshape(NX * NZ, rows, HEADS * DV + STAT)
    parts = lax.all_to_all(
        partial, ("ctx", "head"), split_axis=0, concat_axis=0, tiled=True, axis_index_groups=XZ_GROUPS
    )
    return merge(parts.reshape(NX, NZ, rows, HEADS * DV + STAT))


def solution(mesh):
    in_specs = (
        P(("ctx", "head"), None),
        P(("ctx", "head"), None),
        P(("ctx", "head"), None),
        P("head", None, None),
        P("head", None, None),
        P(),
    )
    out_specs = P(("ctx", "head"), None)
    return jax.shard_map(
        on_device, mesh=mesh, in_specs=in_specs, out_specs=out_specs, check_vma=False
    )
```

```python
import functools

import jax
import jax.numpy as jnp
from jax import lax
from jax.experimental import pallas as pl
from jax.experimental.pallas import tpu as pltpu
from jax.sharding import PartitionSpec as P

HALF = 32
DL = 512
DR = 64
DN = 128
DV = 128
DQ = DN + DR
WIDE = 640
STAT = 128
EXTRA = 128
NX = 4
NY = 8
NZ = 8
HEADS = 8
SPAN = 64
LANES = 128
PACKED = DL // LANES * SPAN + HALF
FLOOR_SCORE = -1e30
LOG2E = 1.4426950408889634
SCALE2 = DQ ** (-0.5) * LOG2E


def ctx_of(y, x, core):
    return ((y % NY) * NX + (x % NX)) * 2 + core


def along_x(step):
    return [
        (ctx_of(y, x, c), ctx_of(y, x + step, c))
        for y in range(NY)
        for x in range(NX)
        for c in range(2)
    ]


CORE_SWAP = [(i, i ^ 1) for i in range(NX * NY * 2)]
XZ_GROUPS = [
    [ctx_of(y, x, c) * NZ + z for x in range(NX) for z in range(NZ)] for y in range(NY) for c in range(2)
]
Y_GROUPS = [[ctx_of(y, x, c) for y in range(NY)] for x in range(NX) for c in range(2)]


def spread_kernel(q_ref, lat_ref, rope_ref, out_ref):
    end = HEADS * DQ
    for z in range(NZ):
        out_ref[z, :, :end] = q_ref[:, z * end : (z + 1) * end]
        out_ref[z, :, end : end + DL] = lat_ref[...]
        out_ref[z, :, end + DL : end + DL + DR] = rope_ref[...]
        out_ref[z, :, end + DL + DR :] = jnp.zeros_like(rope_ref)


def spread(queries, latent, rope_key):
    vmem = pl.BlockSpec(memory_space=pltpu.VMEM)
    return pl.pallas_call(
        spread_kernel,
        out_shape=jax.ShapeDtypeStruct((NZ, SPAN // NZ, HEADS * DQ + WIDE), jnp.bfloat16),
        in_specs=[vmem] * 3,
        out_specs=vmem,
        compiler_params=pltpu.CompilerParams(vmem_limit_bytes=60 * 1024 * 1024),
        cost_estimate=pl.CostEstimate(flops=1_000_000, bytes_accessed=500_000, transcendentals=0),
    )(queries, latent, rope_key)


def pack_kernel(both_ref, q_ref, kv_ref):
    q_ref[...] = both_ref[:, : HEADS * DQ]
    rope = both_ref[:, HEADS * DQ + DL : HEADS * DQ + DL + DR]
    for to in range(NY):
        for j in range(DL // LANES):
            col = HEADS * DQ + j * LANES
            kv_ref[to, j * SPAN : (j + 1) * SPAN] = both_ref[:, col : col + LANES]
        kv_ref[to, PACKED - HALF :, :DR] = rope[:HALF]
        kv_ref[to, PACKED - HALF :, DR:] = rope[HALF:]


def pack(both):
    vmem = pl.BlockSpec(memory_space=pltpu.VMEM)
    return pl.pallas_call(
        pack_kernel,
        out_shape=[
            jax.ShapeDtypeStruct((SPAN, HEADS * DQ), jnp.bfloat16),
            jax.ShapeDtypeStruct((NY, PACKED, LANES), jnp.bfloat16),
        ],
        in_specs=[vmem],
        out_specs=[vmem] * 2,
        compiler_params=pltpu.CompilerParams(vmem_limit_bytes=8 * 1024 * 1024),
        cost_estimate=pl.CostEstimate(flops=4_000_000_000, bytes_accessed=1_000_000, transcendentals=0),
    )(both)


def fill_keys(keys, kv, first, own_block):
    count = NY * SPAN
    blocks = 2 * count // HALF
    for b in range(NY):
        here = slice(b * SPAN, (b + 1) * SPAN)
        for j in range(DL // LANES):
            keys[here, j * LANES : (j + 1) * LANES] = kv[b, j * SPAN : (j + 1) * SPAN]
        keys[b * SPAN : b * SPAN + HALF, DL : DL + DR] = kv[b, PACKED - HALF :, :DR]
        keys[b * SPAN + HALF : (b + 1) * SPAN, DL : DL + DR] = kv[b, PACKED - HALF :, DR:]
    keys[:, DL + DR : WIDE] = jnp.zeros((count, WIDE - DL - DR), jnp.bfloat16)
    key = lax.broadcasted_iota(jnp.int32, (count, EXTRA), 0)
    col = lax.broadcasted_iota(jnp.int32, (count, EXTRA), 1)
    ones = col == key // HALF + first
    if own_block is not None:
        in_own = (key // HALF == own_block) | (key // HALF == own_block + 1)
        ones = ones | (in_own & (col == blocks + key - own_block * HALF))
    keys[:, WIDE:] = jnp.where(ones, 1.0, 0.0).astype(jnp.bfloat16)


def pair_scores(q_ref, keys, p):
    q = q_ref[2 * p : 2 * p + 2].reshape(2 * NX * SPAN, WIDE + EXTRA)
    return lax.dot_general(q, keys[...], (((1,), (1,)), ((), ())), preferred_element_type=jnp.float32)


def wide(value, count):
    return jnp.concatenate([value] * count, axis=1)


def floors_of(info_ref):
    me = info_ref[0]
    core = me % 2
    x = (me // 2) % NX
    y = me // (2 * NX)
    blocks = 2 * NY * SPAN // HALF
    lane = lax.broadcasted_iota(jnp.int32, (HALF, EXTRA), 1)
    token = lax.broadcasted_iota(jnp.int32, (HALF, EXTRA), 0)
    key_block = jnp.zeros((HALF, EXTRA), jnp.int32)
    for which in range(blocks):
        side_core = core if which < blocks // 2 else 1 - core
        slot = (((which // 2) % NY) * NX + x) * 2 + side_core
        key_block = jnp.where(lane == which, info_ref[1 + 2 * slot + which % 2], key_block)
    floors = []
    for step in range(NX):
        slot = (y * NX + (x - step + NX) % NX) * 2 + core
        for half in range(2):
            ahead = (lane < blocks) & (key_block > info_ref[1 + 2 * slot + half])
            if step == 0:
                own = lane - blocks - half * HALF
                ahead = ahead | ((own >= 0) & (own < HALF) & (own > token))
            floors.append(jnp.where(ahead, FLOOR_SCORE, 0.0))
    return jnp.concatenate(floors, axis=0).astype(jnp.bfloat16)


def own_kernel(info_ref, q0, q1, q2, q3, w_uk, kv, q_ref, lat_ref, top_ref, total_ref, keys):
    y = info_ref[0] // (2 * NX)
    rows = NX * SPAN
    floor = floors_of(info_ref)
    none = jnp.zeros((rows, WIDE - DL - DR), jnp.bfloat16)

    def fill_queries(h):
        here = slice(h * DQ, (h + 1) * DQ)
        q = jnp.concatenate([q0[:, here], q1[:, here], q2[:, here], q3[:, here]], axis=0)
        q_lat = lax.dot_general(
            q[:, :DN], w_uk[h], (((1,), (1,)), ((), ())), preferred_element_type=jnp.float32
        )
        q_ref[h, :, :DL] = q_lat.astype(jnp.bfloat16)
        q_ref[h, :, DL : DL + DR] = q[:, DN:]
        q_ref[h, :, DL + DR : WIDE] = none
        q_ref[h, :, WIDE:] = floor

    fill_queries(0)
    fill_queries(1)
    fill_keys(keys, kv, 0, 2 * y)
    ahead = pair_scores(q_ref, keys, 0)
    for p in range(HEADS // 2):
        s = ahead
        if p + 1 < HEADS // 2:
            fill_queries(2 * p + 2)
            fill_queries(2 * p + 3)
            ahead = pair_scores(q_ref, keys, p + 1)
        top = jnp.max(s, axis=1, keepdims=True)
        weight = jnp.exp2((s - top) * SCALE2)
        total = jnp.sum(weight, axis=1, keepdims=True)
        lat = jnp.dot(weight.astype(jnp.bfloat16), keys[:, :DL], preferred_element_type=jnp.float32)
        pair = slice(2 * p, 2 * p + 2)
        lat_ref[pair] = lat.reshape(2, rows, DL)
        top_ref[pair] = jnp.broadcast_to(top, (2 * rows, STAT)).reshape(2, rows, STAT)
        total_ref[pair] = jnp.broadcast_to(total, (2 * rows, STAT)).reshape(2, rows, STAT)


def attend_own(info, qs, w_uk, kv):
    vmem = pl.BlockSpec(memory_space=pltpu.VMEM)
    smem = pl.BlockSpec(memory_space=pltpu.SMEM)
    rows = NX * SPAN
    return pl.pallas_call(
        own_kernel,
        out_shape=[
            jax.ShapeDtypeStruct((HEADS, rows, WIDE + EXTRA), jnp.bfloat16),
            jax.ShapeDtypeStruct((HEADS, rows, DL), jnp.float32),
            jax.ShapeDtypeStruct((HEADS, rows, STAT), jnp.float32),
            jax.ShapeDtypeStruct((HEADS, rows, STAT), jnp.float32),
        ],
        in_specs=[smem] + [vmem] * 6,
        out_specs=[vmem] * 4,
        scratch_shapes=[pltpu.VMEM((NY * SPAN, WIDE + EXTRA), jnp.bfloat16)],
        compiler_params=pltpu.CompilerParams(vmem_limit_bytes=20 * 1024 * 1024),
        cost_estimate=pl.CostEstimate(flops=6_000_000_000, bytes_accessed=5_000_000, transcendentals=1_000_000),
    )(info, *qs, w_uk, kv)


def other_kernel(place_ref, q_ref, kv, lat_ref, top_ref, total_ref, w_uv, out_ref, keys):
    x = (place_ref[0] // 2) % NX
    rows = NX * SPAN
    fill_keys(keys, kv, NY * SPAN // HALF, None)
    lanes = lax.broadcasted_iota(jnp.int32, (rows, STAT), 1)
    level = jnp.zeros((rows, STAT), jnp.float32)
    ahead = pair_scores(q_ref, keys, 0)
    for p in range(HEADS // 2):
        s = ahead
        if p + 1 < HEADS // 2:
            ahead = pair_scores(q_ref, keys, p + 1)
        pair = slice(2 * p, 2 * p + 2)
        old_top = top_ref[pair].reshape(2 * rows, STAT)
        old_total = total_ref[pair].reshape(2 * rows, STAT)
        top = jnp.maximum(old_top, jnp.max(s, axis=1, keepdims=True))
        shrink = jnp.exp2((old_top - top) * SCALE2)
        weight = jnp.exp2((s - wide(top, NY * SPAN // STAT)) * SCALE2)
        total = old_total * shrink + jnp.sum(weight, axis=1, keepdims=True)
        lat = jnp.dot(weight.astype(jnp.bfloat16), keys[:, :DL], preferred_element_type=jnp.float32)
        share = 1.0 / total
        old_lat = lat_ref[pair].reshape(2 * rows, DL)
        o_lat = (lat * wide(share, DL // STAT) + old_lat * wide(shrink * share, DL // STAT)).astype(jnp.bfloat16)
        here = top * SCALE2 + jnp.log2(total)
        for i in range(2):
            h = 2 * p + i
            proj = jnp.dot(o_lat[i * rows : (i + 1) * rows], w_uv[h], preferred_element_type=jnp.float32)
            proj = proj.astype(jnp.bfloat16)
            for step in range(NX):
                to = (x + NX - step) % NX
                out_ref[to, :, h * DV : (h + 1) * DV] = proj[step * SPAN : (step + 1) * SPAN]
            level = jnp.where(lanes % HEADS == h, here[i * rows : (i + 1) * rows], level)
    high = level.astype(jnp.bfloat16)
    rest = level - high.astype(jnp.float32)
    middle = rest.astype(jnp.bfloat16)
    low = (rest - middle.astype(jnp.float32)).astype(jnp.bfloat16)
    part = lanes // HEADS
    packed = jnp.where(
        part == 0,
        high.astype(jnp.float32),
        jnp.where(part == 1, middle.astype(jnp.float32), jnp.where(part == 2, low.astype(jnp.float32), 0.0)),
    ).astype(jnp.bfloat16)
    for step in range(NX):
        to = (x + NX - step) % NX
        out_ref[to, :, HEADS * DV :] = packed[step * SPAN : (step + 1) * SPAN]


def attend_other(place, q_all, kv, state, w_uv):
    vmem = pl.BlockSpec(memory_space=pltpu.VMEM)
    smem = pl.BlockSpec(memory_space=pltpu.SMEM)
    rows = NX * SPAN
    return pl.pallas_call(
        other_kernel,
        out_shape=jax.ShapeDtypeStruct((NX, SPAN, HEADS * DV + STAT), jnp.bfloat16),
        in_specs=[smem] + [vmem] * 6,
        out_specs=vmem,
        scratch_shapes=[pltpu.VMEM((NY * SPAN, WIDE + EXTRA), jnp.bfloat16)],
        compiler_params=pltpu.CompilerParams(vmem_limit_bytes=20 * 1024 * 1024),
        cost_estimate=pl.CostEstimate(flops=4_000_000_000, bytes_accessed=5_000_000, transcendentals=1_000_000),
    )(place, q_all, kv, *state, w_uv)


def merge_kernel(p_ref, out_ref):
    levels = []
    for x in range(NX):
        pieces = p_ref[x, :, :, HEADS * DV :].astype(jnp.float32).reshape(SPAN, STAT)
        rest = pltpu.roll(pieces, STAT - HEADS, 1) + pltpu.roll(pieces, STAT - 2 * HEADS, 1)
        levels.append(pieces + rest)
    top = functools.reduce(jnp.maximum, levels)
    shares = [jnp.exp2(level - top) for level in levels]
    whole = functools.reduce(jnp.add, shares)
    shares = [share / whole for share in shares]
    tokens = SPAN // NZ
    for z in range(NZ):
        here = slice(z * tokens, (z + 1) * tokens)
        for h in range(HEADS):
            acc = jnp.zeros((tokens, DV), jnp.float32)
            for x in range(NX):
                acc = acc + shares[x][here, h : h + 1] * p_ref[x, z, :, h * DV : (h + 1) * DV].astype(jnp.float32)
            out_ref[:, (z * HEADS + h) * DV : (z * HEADS + h + 1) * DV] = acc.astype(jnp.bfloat16)


def merge(parts):
    vmem = pl.BlockSpec(memory_space=pltpu.VMEM)
    return pl.pallas_call(
        merge_kernel,
        out_shape=jax.ShapeDtypeStruct((SPAN // NZ, NZ * HEADS * DV), jnp.bfloat16),
        in_specs=[vmem],
        out_specs=vmem,
        compiler_params=pltpu.CompilerParams(vmem_limit_bytes=8 * 1024 * 1024),
        cost_estimate=pl.CostEstimate(flops=1_000_000, bytes_accessed=800_000, transcendentals=2000),
    )(parts)


def on_device(queries, latent, rope_key, w_uk, w_uv, block_order):
    place = lax.axis_index("ctx").astype(jnp.int32).reshape(1)
    info = jnp.concatenate([place, block_order])
    both = spread(queries, latent, rope_key)
    both = lax.all_to_all(both, "head", split_axis=0, concat_axis=0, tiled=True).reshape(SPAN, HEADS * DQ + WIDE)
    q_own, kv = pack(both)
    kv_own = lax.all_to_all(kv, "ctx", split_axis=0, concat_axis=0, tiled=True, axis_index_groups=Y_GROUPS)
    kv_sib = lax.ppermute(kv_own, "ctx", CORE_SWAP)
    qs = [q_own] + [lax.ppermute(q_own, "ctx", along_x(step)) for step in range(1, NX)]
    q_all, *state = attend_own(info, qs, w_uk, kv_own)
    partial = attend_other(place, q_all, kv_sib, state, w_uv)
    rows = SPAN // NZ
    partial = partial.reshape(NX * NZ, rows, HEADS * DV + STAT)
    parts = lax.all_to_all(
        partial, ("ctx", "head"), split_axis=0, concat_axis=0, tiled=True, axis_index_groups=XZ_GROUPS
    )
    return merge(parts.reshape(NX, NZ, rows, HEADS * DV + STAT))


def solution(mesh):
    in_specs = (
        P(("ctx", "head"), None),
        P(("ctx", "head"), None),
        P(("ctx", "head"), None),
        P("head", None, None),
        P("head", None, None),
        P(),
    )
    out_specs = P(("ctx", "head"), None)
    return jax.shard_map(
        on_device, mesh=mesh, in_specs=in_specs, out_specs=out_specs, check_vma=False
    )
```

```python
import functools

import jax
import jax.numpy as jnp
from jax import lax
from jax.experimental import pallas as pl
from jax.experimental.pallas import tpu as pltpu
from jax.sharding import PartitionSpec as P

HALF = 32
DL = 512
DR = 64
DN = 128
DV = 128
DQ = DN + DR
WIDE = 640
STAT = 128
EXTRA = 128
NX = 4
NY = 8
NZ = 8
HEADS = 8
SPAN = 64
LANES = 128
PACKED = DL // LANES * HALF + HALF // 2
PIECE = NY * HALF
PIECES = 4
BLOCKS = PIECES * NY
FLOOR_SCORE = -1e30
LOG2E = 1.4426950408889634
SCALE2 = DQ ** (-0.5) * LOG2E


def ctx_of(y, x, core):
    return ((y % NY) * NX + (x % NX)) * 2 + core


def along_x(step):
    return [
        (ctx_of(y, x, c), ctx_of(y, x + step, c))
        for y in range(NY)
        for x in range(NX)
        for c in range(2)
    ]


Z_SWAP = [(i, i ^ 1) for i in range(NZ)]
CORE_SWAP = [(i, i ^ 1) for i in range(NX * NY * 2)]
XZ_GROUPS = [
    [ctx_of(y, x, c) * NZ + z for x in range(NX) for z in range(NZ)] for y in range(NY) for c in range(2)
]
Y_GROUPS = [[ctx_of(y, x, c) for y in range(NY)] for x in range(NX) for c in range(2)]


def spread_kernel(q_ref, lat_ref, rope_ref, out_ref):
    end = HEADS * DQ
    for z in range(NZ):
        out_ref[z, :, :end] = q_ref[:, z * end : (z + 1) * end]
        out_ref[z, :, end : end + DL] = lat_ref[...]
        out_ref[z, :, end + DL : end + DL + DR] = rope_ref[...]
        out_ref[z, :, end + DL + DR :] = jnp.zeros_like(rope_ref)


def spread(queries, latent, rope_key):
    vmem = pl.BlockSpec(memory_space=pltpu.VMEM)
    return pl.pallas_call(
        spread_kernel,
        out_shape=jax.ShapeDtypeStruct((NZ, SPAN // NZ, HEADS * DQ + WIDE), jnp.bfloat16),
        in_specs=[vmem] * 3,
        out_specs=vmem,
        compiler_params=pltpu.CompilerParams(vmem_limit_bytes=60 * 1024 * 1024),
        cost_estimate=pl.CostEstimate(flops=1_000_000, bytes_accessed=500_000, transcendentals=0),
    )(queries, latent, rope_key)


def pack_kernel(info_ref, both_ref, q_ref, kv_ref):
    q_ref[...] = both_ref[:, : HEADS * DQ]
    rows = pl.ds(pl.multiple_of(info_ref[1] * HALF, HALF), HALF)
    kept = both_ref[rows, HEADS * DQ : HEADS * DQ + DL + DR]
    for to in range(NY):
        for j in range(DL // LANES):
            kv_ref[to, j * HALF : (j + 1) * HALF] = kept[:, j * LANES : (j + 1) * LANES]
        kv_ref[to, DL // LANES * HALF :, :DR] = kept[: HALF // 2, DL:]
        kv_ref[to, DL // LANES * HALF :, DR:] = kept[HALF // 2 :, DL:]


def pack(info, both):
    vmem = pl.BlockSpec(memory_space=pltpu.VMEM)
    smem = pl.BlockSpec(memory_space=pltpu.SMEM)
    return pl.pallas_call(
        pack_kernel,
        out_shape=[
            jax.ShapeDtypeStruct((SPAN, HEADS * DQ), jnp.bfloat16),
            jax.ShapeDtypeStruct((NY, PACKED, LANES), jnp.bfloat16),
        ],
        in_specs=[smem, vmem],
        out_specs=[vmem] * 2,
        compiler_params=pltpu.CompilerParams(vmem_limit_bytes=8 * 1024 * 1024),
        cost_estimate=pl.CostEstimate(flops=4_000_000_000, bytes_accessed=1_000_000, transcendentals=0),
    )(info, both)


def fill_keys(keys, kv, piece, info_ref):
    lat_rows = DL // LANES * HALF
    for b in range(NY):
        here = slice(b * HALF, (b + 1) * HALF)
        for j in range(DL // LANES):
            keys[here, j * LANES : (j + 1) * LANES] = kv[b, j * HALF : (j + 1) * HALF]
        keys[b * HALF : b * HALF + HALF // 2, DL : DL + DR] = kv[b, lat_rows:, :DR]
        keys[b * HALF + HALF // 2 : (b + 1) * HALF, DL : DL + DR] = kv[b, lat_rows:, DR:]
    keys[:, DL + DR : WIDE] = jnp.zeros((PIECE, WIDE - DL - DR), jnp.bfloat16)
    key = lax.broadcasted_iota(jnp.int32, (PIECE, EXTRA), 0)
    col = lax.broadcasted_iota(jnp.int32, (PIECE, EXTRA), 1)
    ones = col == key // HALF + piece * NY
    if piece % 2 == 0:
        y = info_ref[0] // (2 * NX)
        ones = ones | ((key // HALF == y) & (col == BLOCKS + piece // 2 * HALF + key - y * HALF))
    keys[:, WIDE:] = jnp.where(ones, 1.0, 0.0).astype(jnp.bfloat16)


def pair_scores(q_ref, keys, p):
    q = q_ref[2 * p : 2 * p + 2].reshape(2 * NX * SPAN, WIDE + EXTRA)
    return lax.dot_general(q, keys[...], (((1,), (1,)), ((), ())), preferred_element_type=jnp.float32)


def wide(value, count):
    return jnp.concatenate([value] * count, axis=1)


def floors_of(info_ref):
    me, parity = info_ref[0], info_ref[1]
    core = me % 2
    x = (me // 2) % NX
    y = me // (2 * NX)
    lane = lax.broadcasted_iota(jnp.int32, (HALF, EXTRA), 1)
    token = lax.broadcasted_iota(jnp.int32, (HALF, EXTRA), 0)
    key_block = jnp.zeros((HALF, EXTRA), jnp.int32)
    for which in range(BLOCKS):
        piece = which // NY
        key_core = (core + piece) % 2
        key_half = (parity + piece // 2) % 2
        slot = ((which % NY) * NX + x) * 2 + key_core
        key_block = jnp.where(lane == which, info_ref[2 + 2 * slot + key_half], key_block)
    floors = []
    for step in range(NX):
        slot = (y * NX + (x - step + NX) % NX) * 2 + core
        for half in range(2):
            ahead = (lane < BLOCKS) & (key_block > info_ref[2 + 2 * slot + half])
            if step == 0:
                own = lane - BLOCKS - (parity + half) % 2 * HALF
                ahead = ahead | ((own >= 0) & (own < HALF) & (own > token))
            floors.append(jnp.where(ahead, FLOOR_SCORE, 0.0))
    return jnp.concatenate(floors, axis=0).astype(jnp.bfloat16)


def first_kernel(info_ref, q0, q1, q2, q3, w_uk, kv, q_ref, lat_ref, top_ref, total_ref, keys):
    rows = NX * SPAN
    floor = floors_of(info_ref)
    none = jnp.zeros((rows, WIDE - DL - DR), jnp.bfloat16)

    def fill_queries(h):
        here = slice(h * DQ, (h + 1) * DQ)
        q = jnp.concatenate([q0[:, here], q1[:, here], q2[:, here], q3[:, here]], axis=0)
        q_lat = lax.dot_general(
            q[:, :DN], w_uk[h], (((1,), (1,)), ((), ())), preferred_element_type=jnp.float32
        )
        q_ref[h, :, :DL] = q_lat.astype(jnp.bfloat16)
        q_ref[h, :, DL : DL + DR] = q[:, DN:]
        q_ref[h, :, DL + DR : WIDE] = none
        q_ref[h, :, WIDE:] = floor

    fill_queries(0)
    fill_queries(1)
    fill_keys(keys, kv, 0, info_ref)
    ahead = pair_scores(q_ref, keys, 0)
    for p in range(HEADS // 2):
        s = ahead
        if p + 1 < HEADS // 2:
            fill_queries(2 * p + 2)
            fill_queries(2 * p + 3)
            ahead = pair_scores(q_ref, keys, p + 1)
        top = jnp.max(s, axis=1, keepdims=True)
        weight = jnp.exp2((s - top) * SCALE2)
        total = jnp.sum(weight, axis=1, keepdims=True)
        lat = jnp.dot(weight.astype(jnp.bfloat16), keys[:, :DL], preferred_element_type=jnp.float32)
        pair = slice(2 * p, 2 * p + 2)
        lat_ref[pair] = lat.reshape(2, rows, DL)
        top_ref[pair] = jnp.broadcast_to(top, (2 * rows, STAT)).reshape(2, rows, STAT)
        total_ref[pair] = jnp.broadcast_to(total, (2 * rows, STAT)).reshape(2, rows, STAT)


def attend_first(info, qs, w_uk, kv):
    vmem = pl.BlockSpec(memory_space=pltpu.VMEM)
    smem = pl.BlockSpec(memory_space=pltpu.SMEM)
    rows = NX * SPAN
    return pl.pallas_call(
        first_kernel,
        out_shape=[
            jax.ShapeDtypeStruct((HEADS, rows, WIDE + EXTRA), jnp.bfloat16),
            jax.ShapeDtypeStruct((HEADS, rows, DL), jnp.float32),
            jax.ShapeDtypeStruct((HEADS, rows, STAT), jnp.float32),
            jax.ShapeDtypeStruct((HEADS, rows, STAT), jnp.float32),
        ],
        in_specs=[smem] + [vmem] * 6,
        out_specs=[vmem] * 4,
        scratch_shapes=[pltpu.VMEM((PIECE, WIDE + EXTRA), jnp.bfloat16)],
        compiler_params=pltpu.CompilerParams(vmem_limit_bytes=20 * 1024 * 1024),
        cost_estimate=pl.CostEstimate(flops=6_000_000_000, bytes_accessed=5_000_000, transcendentals=1_000_000),
    )(info, *qs, w_uk, kv)


def advance(s, keys, lat_ref, top_ref, total_ref, pair):
    rows = 2 * NX * SPAN
    old_top = top_ref[pair].reshape(rows, STAT)
    top = jnp.maximum(old_top, jnp.max(s, axis=1, keepdims=True))
    shrink = jnp.exp2((old_top - top) * SCALE2)
    weight = jnp.exp2((s - wide(top, PIECE // STAT)) * SCALE2)
    total = total_ref[pair].reshape(rows, STAT) * shrink + jnp.sum(weight, axis=1, keepdims=True)
    lat = jnp.dot(weight.astype(jnp.bfloat16), keys[:, :DL], preferred_element_type=jnp.float32)
    return top, total, shrink, lat, lat_ref[pair].reshape(rows, DL)


def middle_kernel(piece, info_ref, q_ref, kv, old_lat, old_top, old_total, lat_ref, top_ref, total_ref, keys):
    rows = NX * SPAN
    fill_keys(keys, kv, piece, info_ref)
    ahead = pair_scores(q_ref, keys, 0)
    for p in range(HEADS // 2):
        s = ahead
        if p + 1 < HEADS // 2:
            ahead = pair_scores(q_ref, keys, p + 1)
        pair = slice(2 * p, 2 * p + 2)
        top, total, shrink, lat, held = advance(s, keys, old_lat, old_top, old_total, pair)
        lat_ref[pair] = (lat + held * wide(shrink, DL // STAT)).reshape(2, rows, DL)
        top_ref[pair] = top.reshape(2, rows, STAT)
        total_ref[pair] = total.reshape(2, rows, STAT)


def attend_middle(piece, info, q_all, kv, state):
    vmem = pl.BlockSpec(memory_space=pltpu.VMEM)
    smem = pl.BlockSpec(memory_space=pltpu.SMEM)
    rows = NX * SPAN
    return pl.pallas_call(
        functools.partial(middle_kernel, piece),
        out_shape=[
            jax.ShapeDtypeStruct((HEADS, rows, DL), jnp.float32),
            jax.ShapeDtypeStruct((HEADS, rows, STAT), jnp.float32),
            jax.ShapeDtypeStruct((HEADS, rows, STAT), jnp.float32),
        ],
        in_specs=[smem] + [vmem] * 5,
        out_specs=[vmem] * 3,
        scratch_shapes=[pltpu.VMEM((PIECE, WIDE + EXTRA), jnp.bfloat16)],
        compiler_params=pltpu.CompilerParams(vmem_limit_bytes=16 * 1024 * 1024),
        cost_estimate=pl.CostEstimate(flops=2_500_000_000, bytes_accessed=5_000_000, transcendentals=500_000),
    )(info, q_all, kv, *state)


def last_kernel(info_ref, q_ref, kv, old_lat, old_top, old_total, w_uv, out_ref, keys):
    x = (info_ref[0] // 2) % NX
    rows = NX * SPAN
    fill_keys(keys, kv, PIECES - 1, info_ref)
    lanes = lax.broadcasted_iota(jnp.int32, (rows, STAT), 1)
    level = jnp.zeros((rows, STAT), jnp.float32)
    ahead = pair_scores(q_ref, keys, 0)
    for p in range(HEADS // 2):
        s = ahead
        if p + 1 < HEADS // 2:
            ahead = pair_scores(q_ref, keys, p + 1)
        pair = slice(2 * p, 2 * p + 2)
        top, total, shrink, lat, held = advance(s, keys, old_lat, old_top, old_total, pair)
        share = 1.0 / total
        o_lat = (lat * wide(share, DL // STAT) + held * wide(shrink * share, DL // STAT)).astype(jnp.bfloat16)
        here = top * SCALE2 + jnp.log2(total)
        for i in range(2):
            h = 2 * p + i
            proj = jnp.dot(o_lat[i * rows : (i + 1) * rows], w_uv[h], preferred_element_type=jnp.float32)
            proj = proj.astype(jnp.bfloat16)
            for step in range(NX):
                to = (x + NX - step) % NX
                out_ref[to, :, h * DV : (h + 1) * DV] = proj[step * SPAN : (step + 1) * SPAN]
            level = jnp.where(lanes % HEADS == h, here[i * rows : (i + 1) * rows], level)
    high = level.astype(jnp.bfloat16)
    rest = level - high.astype(jnp.float32)
    middle = rest.astype(jnp.bfloat16)
    low = (rest - middle.astype(jnp.float32)).astype(jnp.bfloat16)
    part = lanes // HEADS
    packed = jnp.where(
        part == 0,
        high.astype(jnp.float32),
        jnp.where(part == 1, middle.astype(jnp.float32), jnp.where(part == 2, low.astype(jnp.float32), 0.0)),
    ).astype(jnp.bfloat16)
    for step in range(NX):
        to = (x + NX - step) % NX
        out_ref[to, :, HEADS * DV :] = packed[step * SPAN : (step + 1) * SPAN]


def attend_last(info, q_all, kv, state, w_uv):
    vmem = pl.BlockSpec(memory_space=pltpu.VMEM)
    smem = pl.BlockSpec(memory_space=pltpu.SMEM)
    rows = NX * SPAN
    return pl.pallas_call(
        last_kernel,
        out_shape=jax.ShapeDtypeStruct((NX, SPAN, HEADS * DV + STAT), jnp.bfloat16),
        in_specs=[smem] + [vmem] * 6,
        out_specs=vmem,
        scratch_shapes=[pltpu.VMEM((PIECE, WIDE + EXTRA), jnp.bfloat16)],
        compiler_params=pltpu.CompilerParams(vmem_limit_bytes=20 * 1024 * 1024),
        cost_estimate=pl.CostEstimate(flops=4_000_000_000, bytes_accessed=5_000_000, transcendentals=1_000_000),
    )(info, q_all, kv, *state, w_uv)


def merge_kernel(p_ref, out_ref):
    levels = []
    for x in range(NX):
        pieces = p_ref[x, :, :, HEADS * DV :].astype(jnp.float32).reshape(SPAN, STAT)
        rest = pltpu.roll(pieces, STAT - HEADS, 1) + pltpu.roll(pieces, STAT - 2 * HEADS, 1)
        levels.append(pieces + rest)
    top = functools.reduce(jnp.maximum, levels)
    shares = [jnp.exp2(level - top) for level in levels]
    whole = functools.reduce(jnp.add, shares)
    shares = [share / whole for share in shares]
    tokens = SPAN // NZ
    for z in range(NZ):
        here = slice(z * tokens, (z + 1) * tokens)
        for h in range(HEADS):
            acc = jnp.zeros((tokens, DV), jnp.float32)
            for x in range(NX):
                acc = acc + shares[x][here, h : h + 1] * p_ref[x, z, :, h * DV : (h + 1) * DV].astype(jnp.float32)
            out_ref[:, (z * HEADS + h) * DV : (z * HEADS + h + 1) * DV] = acc.astype(jnp.bfloat16)


def merge(parts):
    vmem = pl.BlockSpec(memory_space=pltpu.VMEM)
    return pl.pallas_call(
        merge_kernel,
        out_shape=jax.ShapeDtypeStruct((SPAN // NZ, NZ * HEADS * DV), jnp.bfloat16),
        in_specs=[vmem],
        out_specs=vmem,
        compiler_params=pltpu.CompilerParams(vmem_limit_bytes=8 * 1024 * 1024),
        cost_estimate=pl.CostEstimate(flops=1_000_000, bytes_accessed=800_000, transcendentals=2000),
    )(parts)


def on_device(queries, latent, rope_key, w_uk, w_uv, block_order):
    place = jnp.stack([lax.axis_index("ctx"), lax.axis_index("head") % 2]).astype(jnp.int32)
    info = jnp.concatenate([place, block_order])
    both = spread(queries, latent, rope_key)
    both = lax.all_to_all(both, "head", split_axis=0, concat_axis=0, tiled=True).reshape(SPAN, HEADS * DQ + WIDE)
    q_own, kv = pack(info, both)
    near = lax.all_to_all(kv, "ctx", split_axis=0, concat_axis=0, tiled=True, axis_index_groups=Y_GROUPS)
    far = lax.ppermute(near, "head", Z_SWAP)
    near_core = lax.ppermute(near, "ctx", CORE_SWAP)
    far_core = lax.ppermute(far, "ctx", CORE_SWAP)
    qs = [q_own] + [lax.ppermute(q_own, "ctx", along_x(step)) for step in range(1, NX)]
    q_all, *state = attend_first(info, qs, w_uk, near)
    state = attend_middle(1, info, q_all, near_core, state)
    state = attend_middle(2, info, q_all, far, state)
    partial = attend_last(info, q_all, far_core, state, w_uv)
    rows = SPAN // NZ
    partial = partial.reshape(NX * NZ, rows, HEADS * DV + STAT)
    parts = lax.all_to_all(
        partial, ("ctx", "head"), split_axis=0, concat_axis=0, tiled=True, axis_index_groups=XZ_GROUPS
    )
    return merge(parts.reshape(NX, NZ, rows, HEADS * DV + STAT))


def solution(mesh):
    in_specs = (
        P(("ctx", "head"), None),
        P(("ctx", "head"), None),
        P(("ctx", "head"), None),
        P("head", None, None),
        P("head", None, None),
        P(),
    )
    out_specs = P(("ctx", "head"), None)
    return jax.shard_map(
        on_device, mesh=mesh, in_specs=in_specs, out_specs=out_specs, check_vma=False
    )
```

```python
import functools

import jax
import jax.numpy as jnp
from jax import lax
from jax.experimental import pallas as pl
from jax.experimental.pallas import tpu as pltpu
from jax.sharding import PartitionSpec as P

HALF = 32
DL = 512
DR = 64
DN = 128
DV = 128
DQ = DN + DR
WIDE = 640
STAT = 128
EXTRA = 128
NX = 4
NY = 8
NZ = 8
HEADS = 8
SPAN = 64
LANES = 128
PACKED = DL // LANES * SPAN + HALF
FLOOR_SCORE = -1e30
LOG2E = 1.4426950408889634
SCALE2 = DQ ** (-0.5) * LOG2E


def along_x(step):
    return [(x, (x + step) % NX) for x in range(NX)]


CORE_SWAP = [(0, 1), (1, 0)]
CTX = ("y", "x", "core")


def spread_kernel(q_ref, lat_ref, rope_ref, out_ref):
    end = HEADS * DQ
    for z in range(NZ):
        out_ref[z, :, :end] = q_ref[:, z * end : (z + 1) * end]
        out_ref[z, :, end : end + DL] = lat_ref[...]
        out_ref[z, :, end + DL : end + DL + DR] = rope_ref[...]
        out_ref[z, :, end + DL + DR :] = jnp.zeros_like(rope_ref)


def spread(queries, latent, rope_key):
    vmem = pl.BlockSpec(memory_space=pltpu.VMEM)
    return pl.pallas_call(
        spread_kernel,
        out_shape=jax.ShapeDtypeStruct((NZ, SPAN // NZ, HEADS * DQ + WIDE), jnp.bfloat16),
        in_specs=[vmem] * 3,
        out_specs=vmem,
        compiler_params=pltpu.CompilerParams(vmem_limit_bytes=60 * 1024 * 1024),
        cost_estimate=pl.CostEstimate(flops=1_000_000, bytes_accessed=500_000, transcendentals=0),
    )(queries, latent, rope_key)


def pack_kernel(both_ref, q_ref, kv_ref):
    q_ref[...] = both_ref[:, : HEADS * DQ]
    rope = both_ref[:, HEADS * DQ + DL : HEADS * DQ + DL + DR]
    for to in range(NY):
        for j in range(DL // LANES):
            col = HEADS * DQ + j * LANES
            kv_ref[to, j * SPAN : (j + 1) * SPAN] = both_ref[:, col : col + LANES]
        kv_ref[to, PACKED - HALF :, :DR] = rope[:HALF]
        kv_ref[to, PACKED - HALF :, DR:] = rope[HALF:]


def pack(both):
    vmem = pl.BlockSpec(memory_space=pltpu.VMEM)
    return pl.pallas_call(
        pack_kernel,
        out_shape=[
            jax.ShapeDtypeStruct((SPAN, HEADS * DQ), jnp.bfloat16),
            jax.ShapeDtypeStruct((NY, PACKED, LANES), jnp.bfloat16),
        ],
        in_specs=[vmem],
        out_specs=[vmem] * 2,
        compiler_params=pltpu.CompilerParams(vmem_limit_bytes=8 * 1024 * 1024),
        cost_estimate=pl.CostEstimate(flops=4_000_000_000, bytes_accessed=1_000_000, transcendentals=0),
    )(both)


def fill_keys(keys, kv, first, own_block):
    count = NY * SPAN
    blocks = 2 * count // HALF
    for b in range(NY):
        here = slice(b * SPAN, (b + 1) * SPAN)
        for j in range(DL // LANES):
            keys[here, j * LANES : (j + 1) * LANES] = kv[b, j * SPAN : (j + 1) * SPAN]
        keys[b * SPAN : b * SPAN + HALF, DL : DL + DR] = kv[b, PACKED - HALF :, :DR]
        keys[b * SPAN + HALF : (b + 1) * SPAN, DL : DL + DR] = kv[b, PACKED - HALF :, DR:]
    keys[:, DL + DR : WIDE] = jnp.zeros((count, WIDE - DL - DR), jnp.bfloat16)
    key = lax.broadcasted_iota(jnp.int32, (count, EXTRA), 0)
    col = lax.broadcasted_iota(jnp.int32, (count, EXTRA), 1)
    ones = col == key // HALF + first
    if own_block is not None:
        in_own = (key // HALF == own_block) | (key // HALF == own_block + 1)
        ones = ones | (in_own & (col == blocks + key - own_block * HALF))
    keys[:, WIDE:] = jnp.where(ones, 1.0, 0.0).astype(jnp.bfloat16)


def pair_scores(q_ref, keys, p):
    q = q_ref[2 * p : 2 * p + 2].reshape(2 * NX * SPAN, WIDE + EXTRA)
    return lax.dot_general(q, keys[...], (((1,), (1,)), ((), ())), preferred_element_type=jnp.float32)


def wide(value, count):
    return jnp.concatenate([value] * count, axis=1)


def floors_of(info_ref):
    me = info_ref[0]
    core = me % 2
    x = (me // 2) % NX
    y = me // (2 * NX)
    blocks = 2 * NY * SPAN // HALF
    lane = lax.broadcasted_iota(jnp.int32, (HALF, EXTRA), 1)
    token = lax.broadcasted_iota(jnp.int32, (HALF, EXTRA), 0)
    key_block = jnp.zeros((HALF, EXTRA), jnp.int32)
    for which in range(blocks):
        side_core = core if which < blocks // 2 else 1 - core
        slot = (((which // 2) % NY) * NX + x) * 2 + side_core
        key_block = jnp.where(lane == which, info_ref[1 + 2 * slot + which % 2], key_block)
    floors = []
    for step in range(NX):
        slot = (y * NX + (x - step + NX) % NX) * 2 + core
        for half in range(2):
            ahead = (lane < blocks) & (key_block > info_ref[1 + 2 * slot + half])
            if step == 0:
                own = lane - blocks - half * HALF
                ahead = ahead | ((own >= 0) & (own < HALF) & (own > token))
            floors.append(jnp.where(ahead, FLOOR_SCORE, 0.0))
    return jnp.concatenate(floors, axis=0).astype(jnp.bfloat16)


def own_kernel(info_ref, q0, q1, q2, q3, w_uk, kv, q_ref, lat_ref, top_ref, total_ref, keys):
    y = info_ref[0] // (2 * NX)
    rows = NX * SPAN
    floor = floors_of(info_ref)
    none = jnp.zeros((rows, WIDE - DL - DR), jnp.bfloat16)

    def fill_queries(h):
        here = slice(h * DQ, (h + 1) * DQ)
        q = jnp.concatenate([q0[:, here], q1[:, here], q2[:, here], q3[:, here]], axis=0)
        q_lat = lax.dot_general(
            q[:, :DN], w_uk[h], (((1,), (1,)), ((), ())), preferred_element_type=jnp.float32
        )
        q_ref[h, :, :DL] = q_lat.astype(jnp.bfloat16)
        q_ref[h, :, DL : DL + DR] = q[:, DN:]
        q_ref[h, :, DL + DR : WIDE] = none
        q_ref[h, :, WIDE:] = floor

    fill_queries(0)
    fill_queries(1)
    fill_keys(keys, kv, 0, 2 * y)
    ahead = pair_scores(q_ref, keys, 0)
    for p in range(HEADS // 2):
        s = ahead
        if p + 1 < HEADS // 2:
            fill_queries(2 * p + 2)
            fill_queries(2 * p + 3)
            ahead = pair_scores(q_ref, keys, p + 1)
        top = jnp.max(s, axis=1, keepdims=True)
        weight = jnp.exp2((s - top) * SCALE2)
        total = jnp.sum(weight, axis=1, keepdims=True)
        lat = jnp.dot(weight.astype(jnp.bfloat16), keys[:, :DL], preferred_element_type=jnp.float32)
        pair = slice(2 * p, 2 * p + 2)
        lat_ref[pair] = lat.reshape(2, rows, DL)
        top_ref[pair] = jnp.broadcast_to(top, (2 * rows, STAT)).reshape(2, rows, STAT)
        total_ref[pair] = jnp.broadcast_to(total, (2 * rows, STAT)).reshape(2, rows, STAT)


def attend_own(info, qs, w_uk, kv):
    vmem = pl.BlockSpec(memory_space=pltpu.VMEM)
    smem = pl.BlockSpec(memory_space=pltpu.SMEM)
    rows = NX * SPAN
    return pl.pallas_call(
        own_kernel,
        out_shape=[
            jax.ShapeDtypeStruct((HEADS, rows, WIDE + EXTRA), jnp.bfloat16),
            jax.ShapeDtypeStruct((HEADS, rows, DL), jnp.float32),
            jax.ShapeDtypeStruct((HEADS, rows, STAT), jnp.float32),
            jax.ShapeDtypeStruct((HEADS, rows, STAT), jnp.float32),
        ],
        in_specs=[smem] + [vmem] * 6,
        out_specs=[vmem] * 4,
        scratch_shapes=[pltpu.VMEM((NY * SPAN, WIDE + EXTRA), jnp.bfloat16)],
        compiler_params=pltpu.CompilerParams(vmem_limit_bytes=20 * 1024 * 1024),
        cost_estimate=pl.CostEstimate(flops=6_000_000_000, bytes_accessed=5_000_000, transcendentals=1_000_000),
    )(info, *qs, w_uk, kv)


def other_kernel(place_ref, q_ref, kv, lat_ref, top_ref, total_ref, w_uv, out_ref, keys):
    x = (place_ref[0] // 2) % NX
    rows = NX * SPAN
    fill_keys(keys, kv, NY * SPAN // HALF, None)
    lanes = lax.broadcasted_iota(jnp.int32, (rows, STAT), 1)
    level = jnp.zeros((rows, STAT), jnp.float32)
    ahead = pair_scores(q_ref, keys, 0)
    for p in range(HEADS // 2):
        s = ahead
        if p + 1 < HEADS // 2:
            ahead = pair_scores(q_ref, keys, p + 1)
        pair = slice(2 * p, 2 * p + 2)
        old_top = top_ref[pair].reshape(2 * rows, STAT)
        old_total = total_ref[pair].reshape(2 * rows, STAT)
        top = jnp.maximum(old_top, jnp.max(s, axis=1, keepdims=True))
        shrink = jnp.exp2((old_top - top) * SCALE2)
        weight = jnp.exp2((s - wide(top, NY * SPAN // STAT)) * SCALE2)
        total = old_total * shrink + jnp.sum(weight, axis=1, keepdims=True)
        lat = jnp.dot(weight.astype(jnp.bfloat16), keys[:, :DL], preferred_element_type=jnp.float32)
        share = 1.0 / total
        old_lat = lat_ref[pair].reshape(2 * rows, DL)
        o_lat = (lat * wide(share, DL // STAT) + old_lat * wide(shrink * share, DL // STAT)).astype(jnp.bfloat16)
        here = top * SCALE2 + jnp.log2(total)
        for i in range(2):
            h = 2 * p + i
            proj = jnp.dot(o_lat[i * rows : (i + 1) * rows], w_uv[h], preferred_element_type=jnp.float32)
            proj = proj.astype(jnp.bfloat16)
            for step in range(NX):
                to = (x + NX - step) % NX
                out_ref[to, :, h * DV : (h + 1) * DV] = proj[step * SPAN : (step + 1) * SPAN]
            level = jnp.where(lanes % HEADS == h, here[i * rows : (i + 1) * rows], level)
    high = level.astype(jnp.bfloat16)
    rest = level - high.astype(jnp.float32)
    middle = rest.astype(jnp.bfloat16)
    low = (rest - middle.astype(jnp.float32)).astype(jnp.bfloat16)
    part = lanes // HEADS
    packed = jnp.where(
        part == 0,
        high.astype(jnp.float32),
        jnp.where(part == 1, middle.astype(jnp.float32), jnp.where(part == 2, low.astype(jnp.float32), 0.0)),
    ).astype(jnp.bfloat16)
    for step in range(NX):
        to = (x + NX - step) % NX
        out_ref[to, :, HEADS * DV :] = packed[step * SPAN : (step + 1) * SPAN]


def attend_other(place, q_all, kv, state, w_uv):
    vmem = pl.BlockSpec(memory_space=pltpu.VMEM)
    smem = pl.BlockSpec(memory_space=pltpu.SMEM)
    rows = NX * SPAN
    return pl.pallas_call(
        other_kernel,
        out_shape=jax.ShapeDtypeStruct((NX, SPAN, HEADS * DV + STAT), jnp.bfloat16),
        in_specs=[smem] + [vmem] * 6,
        out_specs=vmem,
        scratch_shapes=[pltpu.VMEM((NY * SPAN, WIDE + EXTRA), jnp.bfloat16)],
        compiler_params=pltpu.CompilerParams(vmem_limit_bytes=20 * 1024 * 1024),
        cost_estimate=pl.CostEstimate(flops=4_000_000_000, bytes_accessed=5_000_000, transcendentals=1_000_000),
    )(place, q_all, kv, *state, w_uv)


def merge_kernel(p_ref, out_ref):
    levels = []
    for x in range(NX):
        pieces = p_ref[x, :, :, HEADS * DV :].astype(jnp.float32).reshape(SPAN, STAT)
        rest = pltpu.roll(pieces, STAT - HEADS, 1) + pltpu.roll(pieces, STAT - 2 * HEADS, 1)
        levels.append(pieces + rest)
    top = functools.reduce(jnp.maximum, levels)
    shares = [jnp.exp2(level - top) for level in levels]
    whole = functools.reduce(jnp.add, shares)
    shares = [share / whole for share in shares]
    tokens = SPAN // NZ
    for z in range(NZ):
        here = slice(z * tokens, (z + 1) * tokens)
        for h in range(HEADS):
            acc = jnp.zeros((tokens, DV), jnp.float32)
            for x in range(NX):
                acc = acc + shares[x][here, h : h + 1] * p_ref[x, z, :, h * DV : (h + 1) * DV].astype(jnp.float32)
            out_ref[:, (z * HEADS + h) * DV : (z * HEADS + h + 1) * DV] = acc.astype(jnp.bfloat16)


def merge(parts):
    vmem = pl.BlockSpec(memory_space=pltpu.VMEM)
    return pl.pallas_call(
        merge_kernel,
        out_shape=jax.ShapeDtypeStruct((SPAN // NZ, NZ * HEADS * DV), jnp.bfloat16),
        in_specs=[vmem],
        out_specs=vmem,
        compiler_params=pltpu.CompilerParams(vmem_limit_bytes=8 * 1024 * 1024),
        cost_estimate=pl.CostEstimate(flops=1_000_000, bytes_accessed=800_000, transcendentals=2000),
    )(parts)


def on_device(queries, latent, rope_key, w_uk, w_uv, block_order):
    place = lax.axis_index(CTX).astype(jnp.int32).reshape(1)
    info = jnp.concatenate([place, block_order])
    both = spread(queries, latent, rope_key)
    both = lax.all_to_all(both, "z", split_axis=0, concat_axis=0, tiled=True).reshape(SPAN, HEADS * DQ + WIDE)
    q_own, kv = pack(both)
    kv_own = lax.all_to_all(kv, "y", split_axis=0, concat_axis=0, tiled=True)
    kv_sib = lax.ppermute(kv_own, "core", CORE_SWAP)
    qs = [q_own] + [lax.ppermute(q_own, "x", along_x(step)) for step in range(1, NX)]
    q_all, *state = attend_own(info, qs, w_uk, kv_own)
    partial = attend_other(place, q_all, kv_sib, state, w_uv)
    rows = SPAN // NZ
    partial = partial.reshape(NX * NZ, rows, HEADS * DV + STAT)
    parts = lax.all_to_all(partial, ("x", "z"), split_axis=0, concat_axis=0, tiled=True)
    return merge(parts.reshape(NX, NZ, rows, HEADS * DV + STAT))


def solution(mesh):
    fine = jax.sharding.Mesh(mesh.devices.reshape(NY, NX, 2, NZ), ("y", "x", "core", "z"))
    tokens = P(("y", "x", "core", "z"), None)
    in_specs = (tokens, tokens, tokens, P("z", None, None), P("z", None, None), P())
    return jax.shard_map(on_device, mesh=fine, in_specs=in_specs, out_specs=tokens, check_vma=False)
```

```python
import functools

import jax
import jax.numpy as jnp
from jax import lax
from jax.experimental import pallas as pl
from jax.experimental.pallas import tpu as pltpu
from jax.sharding import PartitionSpec as P

HALF = 32
DL = 512
DR = 64
DN = 128
DV = 128
DQ = DN + DR
WIDE = 640
STAT = 128
EXTRA = 128
NX = 4
NY = 8
NZ = 8
HEADS = 8
SPAN = 64
LANES = 128
PACKED = DL // LANES * SPAN + HALF
FLOOR_SCORE = -1e30
LOG2E = 1.4426950408889634
SCALE2 = DQ ** (-0.5) * LOG2E


def along_x(step):
    return [(x, (x + step) % NX) for x in range(NX)]


CORE_SWAP = [(0, 1), (1, 0)]
CTX = ("y", "x", "core")


def spread_kernel(q_ref, lat_ref, rope_ref, out_ref):
    end = HEADS * DQ
    for z in range(out_ref.shape[0]):
        out_ref[z, :, :end] = q_ref[:, z * end : (z + 1) * end]
        out_ref[z, :, end : end + DL] = lat_ref[...]
        out_ref[z, :, end + DL : end + DL + DR] = rope_ref[...]
        out_ref[z, :, end + DL + DR :] = jnp.zeros_like(rope_ref)


def spread(queries, latent, rope_key):
    tokens = SPAN // NZ
    steps = 4
    each = NZ // steps
    return pl.pallas_call(
        spread_kernel,
        grid=(steps,),
        out_shape=jax.ShapeDtypeStruct((NZ, tokens, HEADS * DQ + WIDE), jnp.bfloat16),
        in_specs=[
            pl.BlockSpec((tokens, each * HEADS * DQ), lambda i: (0, i)),
            pl.BlockSpec((tokens, DL), lambda i: (0, 0)),
            pl.BlockSpec((tokens, DR), lambda i: (0, 0)),
        ],
        out_specs=pl.BlockSpec((each, tokens, HEADS * DQ + WIDE), lambda i: (i, 0, 0)),
        compiler_params=pltpu.CompilerParams(vmem_limit_bytes=60 * 1024 * 1024),
        cost_estimate=pl.CostEstimate(flops=1_000_000, bytes_accessed=500_000, transcendentals=0),
    )(queries, latent, rope_key)


def pack_kernel(both_ref, q_ref, kv_ref):
    q_ref[...] = both_ref[:, : HEADS * DQ]
    rope = both_ref[:, HEADS * DQ + DL : HEADS * DQ + DL + DR]
    for to in range(NY):
        for j in range(DL // LANES):
            col = HEADS * DQ + j * LANES
            kv_ref[to, j * SPAN : (j + 1) * SPAN] = both_ref[:, col : col + LANES]
        kv_ref[to, PACKED - HALF :, :DR] = rope[:HALF]
        kv_ref[to, PACKED - HALF :, DR:] = rope[HALF:]


def pack(both):
    vmem = pl.BlockSpec(memory_space=pltpu.VMEM)
    return pl.pallas_call(
        pack_kernel,
        out_shape=[
            jax.ShapeDtypeStruct((SPAN, HEADS * DQ), jnp.bfloat16),
            jax.ShapeDtypeStruct((NY, PACKED, LANES), jnp.bfloat16),
        ],
        in_specs=[vmem],
        out_specs=[vmem] * 2,
        compiler_params=pltpu.CompilerParams(vmem_limit_bytes=8 * 1024 * 1024),
        cost_estimate=pl.CostEstimate(flops=4_000_000_000, bytes_accessed=1_000_000, transcendentals=0),
    )(both)


def fill_keys(keys, kv, first, own_block):
    count = NY * SPAN
    blocks = 2 * count // HALF
    for b in range(NY):
        here = slice(b * SPAN, (b + 1) * SPAN)
        for j in range(DL // LANES):
            keys[here, j * LANES : (j + 1) * LANES] = kv[b, j * SPAN : (j + 1) * SPAN]
        keys[b * SPAN : b * SPAN + HALF, DL : DL + DR] = kv[b, PACKED - HALF :, :DR]
        keys[b * SPAN + HALF : (b + 1) * SPAN, DL : DL + DR] = kv[b, PACKED - HALF :, DR:]
    keys[:, DL + DR : WIDE] = jnp.zeros((count, WIDE - DL - DR), jnp.bfloat16)
    key = lax.broadcasted_iota(jnp.int32, (count, EXTRA), 0)
    col = lax.broadcasted_iota(jnp.int32, (count, EXTRA), 1)
    ones = col == key // HALF + first
    if own_block is not None:
        in_own = (key // HALF == own_block) | (key // HALF == own_block + 1)
        ones = ones | (in_own & (col == blocks + key - own_block * HALF))
    keys[:, WIDE:] = jnp.where(ones, 1.0, 0.0).astype(jnp.bfloat16)


def pair_scores(q_ref, floor, keys, p):
    rows = NX * SPAN
    q = jnp.concatenate(
        [q_ref[2 * p : 2 * p + 2].reshape(2 * rows, WIDE), jnp.concatenate([floor, floor], axis=0)], axis=1
    )
    return lax.dot_general(q, keys[...], (((1,), (1,)), ((), ())), preferred_element_type=jnp.float32)


def pair_values(keys, w_uv, p):
    w = jnp.concatenate([w_uv[2 * p], w_uv[2 * p + 1]], axis=1)
    return jnp.dot(keys[:, :DL], w, preferred_element_type=jnp.float32).astype(jnp.bfloat16)


def weigh(weight, values):
    rows = NX * SPAN
    weight = weight.astype(jnp.bfloat16)
    return [
        jnp.dot(weight[i * rows : (i + 1) * rows], values[:, i * DV : (i + 1) * DV], preferred_element_type=jnp.float32)
        for i in range(2)
    ]


def wide(value, count):
    return jnp.concatenate([value] * count, axis=1)


def floors_of(info_ref):
    me = info_ref[0]
    core = me % 2
    x = (me // 2) % NX
    y = me // (2 * NX)
    blocks = 2 * NY * SPAN // HALF
    lane = lax.broadcasted_iota(jnp.int32, (HALF, EXTRA), 1)
    token = lax.broadcasted_iota(jnp.int32, (HALF, EXTRA), 0)
    key_block = jnp.zeros((HALF, EXTRA), jnp.int32)
    for which in range(blocks):
        side_core = core if which < blocks // 2 else 1 - core
        slot = (((which // 2) % NY) * NX + x) * 2 + side_core
        key_block = jnp.where(lane == which, info_ref[1 + 2 * slot + which % 2], key_block)
    floors = []
    for step in range(NX):
        slot = (y * NX + (x - step + NX) % NX) * 2 + core
        for half in range(2):
            ahead = (lane < blocks) & (key_block > info_ref[1 + 2 * slot + half])
            if step == 0:
                own = lane - blocks - half * HALF
                ahead = ahead | ((own >= 0) & (own < HALF) & (own > token))
            floors.append(jnp.where(ahead, FLOOR_SCORE, 0.0))
    return jnp.concatenate(floors, axis=0).astype(jnp.bfloat16)


def own_kernel(info_ref, q0, q1, q2, q3, w_uk, w_uv, kv, q_ref, floor_ref, sum_ref, top_ref, total_ref, keys):
    y = info_ref[0] // (2 * NX)
    rows = NX * SPAN
    floor = floors_of(info_ref)
    floor_ref[...] = floor
    none = jnp.zeros((rows, WIDE - DL - DR), jnp.bfloat16)

    def fill_queries(h):
        here = slice(h * DQ, (h + 1) * DQ)
        q = jnp.concatenate([q0[:, here], q1[:, here], q2[:, here], q3[:, here]], axis=0)
        q_lat = lax.dot_general(
            q[:, :DN], w_uk[h], (((1,), (1,)), ((), ())), preferred_element_type=jnp.float32
        )
        q_ref[h, :, :DL] = q_lat.astype(jnp.bfloat16)
        q_ref[h, :, DL : DL + DR] = q[:, DN:]
        q_ref[h, :, DL + DR : WIDE] = none

    fill_queries(0)
    fill_queries(1)
    fill_keys(keys, kv, 0, 2 * y)
    ahead = pair_scores(q_ref, floor, keys, 0)
    for p in range(HEADS // 2):
        s = ahead
        values = pair_values(keys, w_uv, p)
        if p + 1 < HEADS // 2:
            fill_queries(2 * p + 2)
            fill_queries(2 * p + 3)
            ahead = pair_scores(q_ref, floor, keys, p + 1)
        top = jnp.max(s, axis=1, keepdims=True)
        weight = jnp.exp2((s - top) * SCALE2)
        total = jnp.sum(weight, axis=1, keepdims=True)
        sums = weigh(weight, values)
        for i in range(2):
            sum_ref[2 * p + i] = sums[i]
        pair = slice(2 * p, 2 * p + 2)
        top_ref[pair] = jnp.broadcast_to(top, (2 * rows, STAT)).reshape(2, rows, STAT)
        total_ref[pair] = jnp.broadcast_to(total, (2 * rows, STAT)).reshape(2, rows, STAT)


def attend_own(info, qs, w_uk, w_uv, kv):
    vmem = pl.BlockSpec(memory_space=pltpu.VMEM)
    smem = pl.BlockSpec(memory_space=pltpu.SMEM)
    rows = NX * SPAN
    return pl.pallas_call(
        own_kernel,
        out_shape=[
            jax.ShapeDtypeStruct((HEADS, rows, WIDE), jnp.bfloat16),
            jax.ShapeDtypeStruct((rows, EXTRA), jnp.bfloat16),
            jax.ShapeDtypeStruct((HEADS, rows, DV), jnp.float32),
            jax.ShapeDtypeStruct((HEADS, rows, STAT), jnp.float32),
            jax.ShapeDtypeStruct((HEADS, rows, STAT), jnp.float32),
        ],
        in_specs=[smem] + [vmem] * 7,
        out_specs=[vmem] * 5,
        scratch_shapes=[pltpu.VMEM((NY * SPAN, WIDE + EXTRA), jnp.bfloat16)],
        compiler_params=pltpu.CompilerParams(vmem_limit_bytes=20 * 1024 * 1024),
        cost_estimate=pl.CostEstimate(flops=6_000_000_000, bytes_accessed=5_000_000, transcendentals=1_000_000),
    )(info, *qs, w_uk, w_uv, kv)


def other_kernel(place_ref, q_ref, floor_ref, kv, sum_ref, top_ref, total_ref, w_uv, out_ref, keys):
    x = (place_ref[0] // 2) % NX
    rows = NX * SPAN
    floor = floor_ref[...]
    fill_keys(keys, kv, NY * SPAN // HALF, None)
    lanes = lax.broadcasted_iota(jnp.int32, (rows, STAT), 1)
    level = jnp.zeros((rows, STAT), jnp.float32)
    ahead = pair_scores(q_ref, floor, keys, 0)
    for p in range(HEADS // 2):
        s = ahead
        values = pair_values(keys, w_uv, p)
        if p + 1 < HEADS // 2:
            ahead = pair_scores(q_ref, floor, keys, p + 1)
        pair = slice(2 * p, 2 * p + 2)
        old_top = top_ref[pair].reshape(2 * rows, STAT)
        old_total = total_ref[pair].reshape(2 * rows, STAT)
        top = jnp.maximum(old_top, jnp.max(s, axis=1, keepdims=True))
        shrink = jnp.exp2((old_top - top) * SCALE2)
        weight = jnp.exp2((s - wide(top, NY * SPAN // STAT)) * SCALE2)
        total = old_total * shrink + jnp.sum(weight, axis=1, keepdims=True)
        sums = weigh(weight, values)
        share = 1.0 / total
        here = top * SCALE2 + jnp.log2(total)
        for i in range(2):
            h = 2 * p + i
            mine = slice(i * rows, (i + 1) * rows)
            value = ((sums[i] + sum_ref[h] * shrink[mine]) * share[mine]).astype(jnp.bfloat16)
            for step in range(NX):
                to = (x + NX - step) % NX
                out_ref[to, :, h * DV : (h + 1) * DV] = value[step * SPAN : (step + 1) * SPAN]
            level = jnp.where(lanes % HEADS == h, here[mine], level)
    high = level.astype(jnp.bfloat16)
    rest = level - high.astype(jnp.float32)
    middle = rest.astype(jnp.bfloat16)
    low = (rest - middle.astype(jnp.float32)).astype(jnp.bfloat16)
    part = lanes // HEADS
    packed = jnp.where(
        part == 0,
        high.astype(jnp.float32),
        jnp.where(part == 1, middle.astype(jnp.float32), jnp.where(part == 2, low.astype(jnp.float32), 0.0)),
    ).astype(jnp.bfloat16)
    for step in range(NX):
        to = (x + NX - step) % NX
        out_ref[to, :, HEADS * DV :] = packed[step * SPAN : (step + 1) * SPAN]


def attend_other(place, q_all, floor, kv, state, w_uv):
    vmem = pl.BlockSpec(memory_space=pltpu.VMEM)
    smem = pl.BlockSpec(memory_space=pltpu.SMEM)
    rows = NX * SPAN
    return pl.pallas_call(
        other_kernel,
        out_shape=jax.ShapeDtypeStruct((NX, SPAN, HEADS * DV + STAT), jnp.bfloat16),
        in_specs=[smem] + [vmem] * 7,
        out_specs=vmem,
        scratch_shapes=[pltpu.VMEM((NY * SPAN, WIDE + EXTRA), jnp.bfloat16)],
        compiler_params=pltpu.CompilerParams(vmem_limit_bytes=20 * 1024 * 1024),
        cost_estimate=pl.CostEstimate(flops=4_000_000_000, bytes_accessed=5_000_000, transcendentals=1_000_000),
    )(place, q_all, floor, kv, *state, w_uv)


def merge_kernel(p_ref, out_ref):
    levels = []
    for x in range(NX):
        pieces = p_ref[x, :, :, HEADS * DV :].astype(jnp.float32).reshape(SPAN, STAT)
        rest = pltpu.roll(pieces, STAT - HEADS, 1) + pltpu.roll(pieces, STAT - 2 * HEADS, 1)
        levels.append(pieces + rest)
    top = functools.reduce(jnp.maximum, levels)
    shares = [jnp.exp2(level - top) for level in levels]
    whole = functools.reduce(jnp.add, shares)
    shares = [share / whole for share in shares]
    tokens = SPAN // NZ
    for z in range(NZ):
        here = slice(z * tokens, (z + 1) * tokens)
        for h in range(HEADS):
            acc = jnp.zeros((tokens, DV), jnp.float32)
            for x in range(NX):
                acc = acc + shares[x][here, h : h + 1] * p_ref[x, z, :, h * DV : (h + 1) * DV].astype(jnp.float32)
            out_ref[:, (z * HEADS + h) * DV : (z * HEADS + h + 1) * DV] = acc.astype(jnp.bfloat16)


def merge(parts):
    vmem = pl.BlockSpec(memory_space=pltpu.VMEM)
    return pl.pallas_call(
        merge_kernel,
        out_shape=jax.ShapeDtypeStruct((SPAN // NZ, NZ * HEADS * DV), jnp.bfloat16),
        in_specs=[vmem],
        out_specs=vmem,
        compiler_params=pltpu.CompilerParams(vmem_limit_bytes=8 * 1024 * 1024),
        cost_estimate=pl.CostEstimate(flops=1_000_000, bytes_accessed=800_000, transcendentals=2000),
    )(parts)


def on_device(queries, latent, rope_key, w_uk, w_uv, block_order):
    place = lax.axis_index(CTX).astype(jnp.int32).reshape(1)
    info = jnp.concatenate([place, block_order])
    both = spread(queries, latent, rope_key)
    both = lax.all_to_all(both, "z", split_axis=0, concat_axis=0, tiled=True).reshape(SPAN, HEADS * DQ + WIDE)
    q_own, kv = pack(both)
    kv_own = lax.all_to_all(kv, "y", split_axis=0, concat_axis=0, tiled=True)
    kv_sib = lax.ppermute(kv_own, "core", CORE_SWAP)
    qs = [q_own] + [lax.ppermute(q_own, "x", along_x(step)) for step in range(1, NX)]
    q_all, floor, *state = attend_own(info, qs, w_uk, w_uv, kv_own)
    partial = attend_other(place, q_all, floor, kv_sib, state, w_uv)
    rows = SPAN // NZ
    partial = partial.reshape(NX * NZ, rows, HEADS * DV + STAT)
    parts = lax.all_to_all(partial, ("x", "z"), split_axis=0, concat_axis=0, tiled=True)
    return merge(parts.reshape(NX, NZ, rows, HEADS * DV + STAT))


def solution(mesh):
    fine = jax.sharding.Mesh(mesh.devices.reshape(NY, NX, 2, NZ), ("y", "x", "core", "z"))
    tokens = P(("y", "x", "core", "z"), None)
    in_specs = (tokens, tokens, tokens, P("z", None, None), P("z", None, None), P())
    return jax.shard_map(on_device, mesh=fine, in_specs=in_specs, out_specs=tokens, check_vma=False)
```

```python
import functools

import jax
import jax.numpy as jnp
from jax import lax
from jax.experimental import pallas as pl
from jax.experimental.pallas import tpu as pltpu
from jax.sharding import PartitionSpec as P

HALF = 32
DL = 512
DR = 64
DN = 128
DV = 128
DQ = DN + DR
WIDE = 640
STAT = 128
EXTRA = 128
NX = 4
NY = 8
NZ = 8
HEADS = 8
SPAN = 64
LANES = 128
PACKED = DL // LANES * SPAN + HALF
FLOOR_SCORE = -1e30
LOG2E = 1.4426950408889634
SCALE2 = DQ ** (-0.5) * LOG2E


def along_x(step):
    return [(x, (x + step) % NX) for x in range(NX)]


CORE_SWAP = [(0, 1), (1, 0)]
CTX = ("y", "x", "core")


def spread_kernel(q_ref, lat_ref, rope_ref, out_ref):
    end = HEADS * DQ
    for z in range(NZ):
        out_ref[z, :, :end] = q_ref[:, z * end : (z + 1) * end]
        out_ref[z, :, end : end + DL] = lat_ref[...]
        out_ref[z, :, end + DL : end + DL + DR] = rope_ref[...]
        out_ref[z, :, end + DL + DR :] = jnp.zeros_like(rope_ref)


def spread(queries, latent, rope_key):
    vmem = pl.BlockSpec(memory_space=pltpu.VMEM)
    return pl.pallas_call(
        spread_kernel,
        out_shape=jax.ShapeDtypeStruct((NZ, SPAN // NZ, HEADS * DQ + WIDE), jnp.bfloat16),
        in_specs=[vmem] * 3,
        out_specs=vmem,
        compiler_params=pltpu.CompilerParams(vmem_limit_bytes=60 * 1024 * 1024),
        cost_estimate=pl.CostEstimate(flops=1_000_000, bytes_accessed=500_000, transcendentals=0),
    )(queries, latent, rope_key)


def pack_kernel(both_ref, floor_ref, q_ref, kv_ref):
    del floor_ref
    q_ref[...] = both_ref[:, : HEADS * DQ]
    rope = both_ref[:, HEADS * DQ + DL : HEADS * DQ + DL + DR]
    for to in range(NY):
        for j in range(DL // LANES):
            col = HEADS * DQ + j * LANES
            kv_ref[to, j * SPAN : (j + 1) * SPAN] = both_ref[:, col : col + LANES]
        kv_ref[to, PACKED - HALF :, :DR] = rope[:HALF]
        kv_ref[to, PACKED - HALF :, DR:] = rope[HALF:]


def pack(both, floor):
    vmem = pl.BlockSpec(memory_space=pltpu.VMEM)
    return pl.pallas_call(
        pack_kernel,
        out_shape=[
            jax.ShapeDtypeStruct((SPAN, HEADS * DQ), jnp.bfloat16),
            jax.ShapeDtypeStruct((NY, PACKED, LANES), jnp.bfloat16),
        ],
        in_specs=[vmem] + [pl.BlockSpec(memory_space=pl.ANY)],
        out_specs=[vmem] * 2,
        compiler_params=pltpu.CompilerParams(vmem_limit_bytes=8 * 1024 * 1024),
        cost_estimate=pl.CostEstimate(flops=4_000_000_000, bytes_accessed=1_000_000, transcendentals=0),
    )(both, floor)


def fill_keys(keys, kv, first, own_block):
    count = NY * SPAN
    blocks = 2 * count // HALF
    for b in range(NY):
        here = slice(b * SPAN, (b + 1) * SPAN)
        for j in range(DL // LANES):
            keys[here, j * LANES : (j + 1) * LANES] = kv[b, j * SPAN : (j + 1) * SPAN]
        keys[b * SPAN : b * SPAN + HALF, DL : DL + DR] = kv[b, PACKED - HALF :, :DR]
        keys[b * SPAN + HALF : (b + 1) * SPAN, DL : DL + DR] = kv[b, PACKED - HALF :, DR:]
    keys[:, DL + DR : WIDE] = jnp.zeros((count, WIDE - DL - DR), jnp.bfloat16)
    key = lax.broadcasted_iota(jnp.int32, (count, EXTRA), 0)
    col = lax.broadcasted_iota(jnp.int32, (count, EXTRA), 1)
    ones = col == key // HALF + first
    if own_block is not None:
        in_own = (key // HALF == own_block) | (key // HALF == own_block + 1)
        ones = ones | (in_own & (col == blocks + key - own_block * HALF))
    keys[:, WIDE:] = jnp.where(ones, 1.0, 0.0).astype(jnp.bfloat16)


def pair_scores(q_ref, floor, keys, p):
    rows = NX * SPAN
    q = jnp.concatenate(
        [q_ref[2 * p : 2 * p + 2].reshape(2 * rows, WIDE), jnp.concatenate([floor, floor], axis=0)], axis=1
    )
    return lax.dot_general(q, keys[...], (((1,), (1,)), ((), ())), preferred_element_type=jnp.float32)


def pair_values(keys, w_uv, p):
    w = jnp.concatenate([w_uv[2 * p], w_uv[2 * p + 1]], axis=1)
    return jnp.dot(keys[:, :DL], w, preferred_element_type=jnp.float32).astype(jnp.bfloat16)


def weigh(weight, values):
    rows = NX * SPAN
    weight = weight.astype(jnp.bfloat16)
    return [
        jnp.dot(weight[i * rows : (i + 1) * rows], values[:, i * DV : (i + 1) * DV], preferred_element_type=jnp.float32)
        for i in range(2)
    ]


def wide(value, count):
    return jnp.concatenate([value] * count, axis=1)


def floors_of(info_ref):
    me = info_ref[0]
    core = me % 2
    x = (me // 2) % NX
    y = me // (2 * NX)
    blocks = 2 * NY * SPAN // HALF
    lane = lax.broadcasted_iota(jnp.int32, (HALF, EXTRA), 1)
    token = lax.broadcasted_iota(jnp.int32, (HALF, EXTRA), 0)
    key_block = jnp.zeros((HALF, EXTRA), jnp.int32)
    for which in range(blocks):
        side_core = core if which < blocks // 2 else 1 - core
        slot = (((which // 2) % NY) * NX + x) * 2 + side_core
        key_block = jnp.where(lane == which, info_ref[1 + 2 * slot + which % 2], key_block)
    floors = []
    for step in range(NX):
        slot = (y * NX + (x - step + NX) % NX) * 2 + core
        for half in range(2):
            ahead = (lane < blocks) & (key_block > info_ref[1 + 2 * slot + half])
            if step == 0:
                own = lane - blocks - half * HALF
                ahead = ahead | ((own >= 0) & (own < HALF) & (own > token))
            floors.append(jnp.where(ahead, FLOOR_SCORE, 0.0))
    return jnp.concatenate(floors, axis=0).astype(jnp.bfloat16)


def floor_kernel(info_ref, floor_ref):
    floor_ref[...] = floors_of(info_ref)


def make_floor(info):
    vmem = pl.BlockSpec(memory_space=pltpu.VMEM)
    smem = pl.BlockSpec(memory_space=pltpu.SMEM)
    return pl.pallas_call(
        floor_kernel,
        out_shape=jax.ShapeDtypeStruct((NX * SPAN, EXTRA), jnp.bfloat16),
        in_specs=[smem],
        out_specs=vmem,
        compiler_params=pltpu.CompilerParams(vmem_limit_bytes=8 * 1024 * 1024),
        cost_estimate=pl.CostEstimate(flops=4_000_000_000, bytes_accessed=500_000, transcendentals=0),
    )(info)


def own_kernel(place_ref, q0, q1, q2, q3, w_uk, w_uv, kv, floor_ref, q_ref, sum_ref, top_ref, total_ref, keys):
    rows = NX * SPAN
    floor = floor_ref[...]
    none = jnp.zeros((rows, WIDE - DL - DR), jnp.bfloat16)

    def fill_queries(h):
        here = slice(h * DQ, (h + 1) * DQ)
        q = jnp.concatenate([q0[:, here], q1[:, here], q2[:, here], q3[:, here]], axis=0)
        q_lat = lax.dot_general(
            q[:, :DN], w_uk[h], (((1,), (1,)), ((), ())), preferred_element_type=jnp.float32
        )
        q_ref[h, :, :DL] = q_lat.astype(jnp.bfloat16)
        q_ref[h, :, DL : DL + DR] = q[:, DN:]
        q_ref[h, :, DL + DR : WIDE] = none

    fill_queries(0)
    fill_queries(1)
    fill_keys(keys, kv, 0, place_ref[0] // (2 * NX) * 2)
    ahead = pair_scores(q_ref, floor, keys, 0)
    for p in range(HEADS // 2):
        s = ahead
        values = pair_values(keys, w_uv, p)
        if p + 1 < HEADS // 2:
            fill_queries(2 * p + 2)
            fill_queries(2 * p + 3)
            ahead = pair_scores(q_ref, floor, keys, p + 1)
        top = jnp.max(s, axis=1, keepdims=True)
        weight = jnp.exp2((s - top) * SCALE2)
        total = jnp.sum(weight, axis=1, keepdims=True)
        sums = weigh(weight, values)
        for i in range(2):
            sum_ref[2 * p + i] = sums[i]
        pair = slice(2 * p, 2 * p + 2)
        top_ref[pair] = jnp.broadcast_to(top, (2 * rows, STAT)).reshape(2, rows, STAT)
        total_ref[pair] = jnp.broadcast_to(total, (2 * rows, STAT)).reshape(2, rows, STAT)


def attend_own(place, qs, w_uk, w_uv, kv, floor):
    vmem = pl.BlockSpec(memory_space=pltpu.VMEM)
    smem = pl.BlockSpec(memory_space=pltpu.SMEM)
    rows = NX * SPAN
    return pl.pallas_call(
        own_kernel,
        out_shape=[
            jax.ShapeDtypeStruct((HEADS, rows, WIDE), jnp.bfloat16),
            jax.ShapeDtypeStruct((HEADS, rows, DV), jnp.float32),
            jax.ShapeDtypeStruct((HEADS, rows, STAT), jnp.float32),
            jax.ShapeDtypeStruct((HEADS, rows, STAT), jnp.float32),
        ],
        in_specs=[smem] + [vmem] * 8,
        out_specs=[vmem] * 4,
        scratch_shapes=[pltpu.VMEM((NY * SPAN, WIDE + EXTRA), jnp.bfloat16)],
        compiler_params=pltpu.CompilerParams(vmem_limit_bytes=20 * 1024 * 1024),
        cost_estimate=pl.CostEstimate(flops=6_000_000_000, bytes_accessed=5_000_000, transcendentals=1_000_000),
    )(place, *qs, w_uk, w_uv, kv, floor)


def other_kernel(place_ref, q_ref, floor_ref, kv, sum_ref, top_ref, total_ref, w_uv, out_ref, keys):
    x = (place_ref[0] // 2) % NX
    rows = NX * SPAN
    floor = floor_ref[...]
    fill_keys(keys, kv, NY * SPAN // HALF, None)
    lanes = lax.broadcasted_iota(jnp.int32, (rows, STAT), 1)
    level = jnp.zeros((rows, STAT), jnp.float32)
    ahead = pair_scores(q_ref, floor, keys, 0)
    for p in range(HEADS // 2):
        s = ahead
        values = pair_values(keys, w_uv, p)
        if p + 1 < HEADS // 2:
            ahead = pair_scores(q_ref, floor, keys, p + 1)
        pair = slice(2 * p, 2 * p + 2)
        old_top = top_ref[pair].reshape(2 * rows, STAT)
        old_total = total_ref[pair].reshape(2 * rows, STAT)
        top = jnp.maximum(old_top, jnp.max(s, axis=1, keepdims=True))
        shrink = jnp.exp2((old_top - top) * SCALE2)
        weight = jnp.exp2((s - wide(top, NY * SPAN // STAT)) * SCALE2)
        total = old_total * shrink + jnp.sum(weight, axis=1, keepdims=True)
        sums = weigh(weight, values)
        share = 1.0 / total
        here = top * SCALE2 + jnp.log2(total)
        for i in range(2):
            h = 2 * p + i
            mine = slice(i * rows, (i + 1) * rows)
            value = ((sums[i] + sum_ref[h] * shrink[mine]) * share[mine]).astype(jnp.bfloat16)
            for step in range(NX):
                to = (x + NX - step) % NX
                out_ref[to, :, h * DV : (h + 1) * DV] = value[step * SPAN : (step + 1) * SPAN]
            level = jnp.where(lanes % HEADS == h, here[mine], level)
    high = level.astype(jnp.bfloat16)
    rest = level - high.astype(jnp.float32)
    middle = rest.astype(jnp.bfloat16)
    low = (rest - middle.astype(jnp.float32)).astype(jnp.bfloat16)
    part = lanes // HEADS
    packed = jnp.where(
        part == 0,
        high.astype(jnp.float32),
        jnp.where(part == 1, middle.astype(jnp.float32), jnp.where(part == 2, low.astype(jnp.float32), 0.0)),
    ).astype(jnp.bfloat16)
    for step in range(NX):
        to = (x + NX - step) % NX
        out_ref[to, :, HEADS * DV :] = packed[step * SPAN : (step + 1) * SPAN]


def attend_other(place, q_all, floor, kv, state, w_uv):
    vmem = pl.BlockSpec(memory_space=pltpu.VMEM)
    smem = pl.BlockSpec(memory_space=pltpu.SMEM)
    rows = NX * SPAN
    return pl.pallas_call(
        other_kernel,
        out_shape=jax.ShapeDtypeStruct((NX, SPAN, HEADS * DV + STAT), jnp.bfloat16),
        in_specs=[smem] + [vmem] * 7,
        out_specs=vmem,
        scratch_shapes=[pltpu.VMEM((NY * SPAN, WIDE + EXTRA), jnp.bfloat16)],
        compiler_params=pltpu.CompilerParams(vmem_limit_bytes=20 * 1024 * 1024),
        cost_estimate=pl.CostEstimate(flops=4_000_000_000, bytes_accessed=5_000_000, transcendentals=1_000_000),
    )(place, q_all, floor, kv, *state, w_uv)


def merge_kernel(p_ref, out_ref, held, sems):
    levels = []
    for x in range(NX):
        pieces = p_ref[x, :, :, HEADS * DV :].astype(jnp.float32).reshape(SPAN, STAT)
        rest = pltpu.roll(pieces, STAT - HEADS, 1) + pltpu.roll(pieces, STAT - 2 * HEADS, 1)
        levels.append(pieces + rest)
    top = functools.reduce(jnp.maximum, levels)
    shares = [jnp.exp2(level - top) for level in levels]
    whole = functools.reduce(jnp.add, shares)
    shares = [share / whole for share in shares]
    tokens = SPAN // NZ
    moves = []
    for z in range(NZ):
        here = slice(z * tokens, (z + 1) * tokens)
        for h in range(HEADS):
            acc = jnp.zeros((tokens, DV), jnp.float32)
            for x in range(NX):
                acc = acc + shares[x][here, h : h + 1] * p_ref[x, z, :, h * DV : (h + 1) * DV].astype(jnp.float32)
            held[:, (z * HEADS + h) * DV : (z * HEADS + h + 1) * DV] = acc.astype(jnp.bfloat16)
        cols = slice(z * HEADS * DV, (z + 1) * HEADS * DV)
        moves.append(pltpu.make_async_copy(held.at[:, cols], out_ref.at[:, cols], sems.at[z]))
        moves[-1].start()
    for move in moves:
        move.wait()


def merge(parts):
    vmem = pl.BlockSpec(memory_space=pltpu.VMEM)
    return pl.pallas_call(
        merge_kernel,
        out_shape=jax.ShapeDtypeStruct((SPAN // NZ, NZ * HEADS * DV), jnp.bfloat16),
        in_specs=[vmem],
        out_specs=pl.BlockSpec(memory_space=pl.ANY),
        scratch_shapes=[
            pltpu.VMEM((SPAN // NZ, NZ * HEADS * DV), jnp.bfloat16),
            pltpu.SemaphoreType.DMA((NZ,)),
        ],
        compiler_params=pltpu.CompilerParams(vmem_limit_bytes=8 * 1024 * 1024),
        cost_estimate=pl.CostEstimate(flops=1_000_000, bytes_accessed=800_000, transcendentals=2000),
    )(parts)


def on_device(queries, latent, rope_key, w_uk, w_uv, block_order):
    place = lax.axis_index(CTX).astype(jnp.int32).reshape(1)
    floor = make_floor(jnp.concatenate([place, block_order]))
    both = spread(queries, latent, rope_key)
    both = lax.all_to_all(both, "z", split_axis=0, concat_axis=0, tiled=True).reshape(SPAN, HEADS * DQ + WIDE)
    q_own, kv = pack(both, floor)
    kv_own = lax.all_to_all(kv, "y", split_axis=0, concat_axis=0, tiled=True)
    kv_sib = lax.ppermute(kv_own, "core", CORE_SWAP)
    qs = [q_own] + [lax.ppermute(q_own, "x", along_x(step)) for step in range(1, NX)]
    q_all, *state = attend_own(place, qs, w_uk, w_uv, kv_own, floor)
    partial = attend_other(place, q_all, floor, kv_sib, state, w_uv)
    rows = SPAN // NZ
    partial = partial.reshape(NX * NZ, rows, HEADS * DV + STAT)
    parts = lax.all_to_all(partial, ("x", "z"), split_axis=0, concat_axis=0, tiled=True)
    return merge(parts.reshape(NX, NZ, rows, HEADS * DV + STAT))


def solution(mesh):
    fine = jax.sharding.Mesh(mesh.devices.reshape(NY, NX, 2, NZ), ("y", "x", "core", "z"))
    tokens = P(("y", "x", "core", "z"), None)
    in_specs = (tokens, tokens, tokens, P("z", None, None), P("z", None, None), P())
    return jax.shard_map(on_device, mesh=fine, in_specs=in_specs, out_specs=tokens, check_vma=False)
```

```python
import functools

import jax
import jax.numpy as jnp
from jax import lax
from jax.experimental import pallas as pl
from jax.experimental.pallas import tpu as pltpu
from jax.sharding import PartitionSpec as P

HALF = 32
DL = 512
DR = 64
DN = 128
DV = 128
DQ = DN + DR
WIDE = 640
STAT = 128
EXTRA = 128
NX = 4
NY = 8
NZ = 8
HEADS = 8
SPAN = 64
LANES = 128
PACKED = DL // LANES * SPAN + HALF
FLOOR_SCORE = -1e30
LOG2E = 1.4426950408889634
SCALE2 = DQ ** (-0.5) * LOG2E


def along_x(step):
    return [(x, (x + step) % NX) for x in range(NX)]


CORE_SWAP = [(0, 1), (1, 0)]
CTX = ("y", "x", "core")


def spread_kernel(q_ref, lat_ref, rope_ref, out_ref, lat, rope, held, sems):
    end = HEADS * DQ
    fetches = [
        pltpu.make_async_copy(lat_ref, lat, sems.at[2 * NZ]),
        pltpu.make_async_copy(rope_ref, rope, sems.at[2 * NZ + 1]),
    ]
    parts = [
        pltpu.make_async_copy(q_ref.at[:, z * end : (z + 1) * end], held.at[z, :, :end], sems.at[z]) for z in range(NZ)
    ]
    for copy in fetches + parts:
        copy.start()
    for copy in fetches:
        copy.wait()
    for z in range(NZ):
        held[z, :, end : end + DL] = lat[...]
        held[z, :, end + DL : end + DL + DR] = rope[...]
        held[z, :, end + DL + DR :] = jnp.zeros_like(rope)
    moves = [pltpu.make_async_copy(held.at[z], out_ref.at[z], sems.at[NZ + z]) for z in range(NZ)]
    for z in range(NZ):
        parts[z].wait()
        moves[z].start()
    for move in moves:
        move.wait()


def spread(queries, latent, rope_key):
    hbm = pl.BlockSpec(memory_space=pl.ANY)
    shape = (NZ, SPAN // NZ, HEADS * DQ + WIDE)
    return pl.pallas_call(
        spread_kernel,
        out_shape=jax.ShapeDtypeStruct(shape, jnp.bfloat16),
        in_specs=[hbm] * 3,
        out_specs=hbm,
        scratch_shapes=[
            pltpu.VMEM(latent.shape, jnp.bfloat16),
            pltpu.VMEM(rope_key.shape, jnp.bfloat16),
            pltpu.VMEM(shape, jnp.bfloat16),
            pltpu.SemaphoreType.DMA((2 * NZ + 2,)),
        ],
        compiler_params=pltpu.CompilerParams(vmem_limit_bytes=60 * 1024 * 1024),
        cost_estimate=pl.CostEstimate(flops=1_000_000, bytes_accessed=500_000, transcendentals=0),
    )(queries, latent, rope_key)


def pack_kernel(both_ref, floor_ref, q_ref, kv_ref, block, sems):
    del floor_ref
    for j in range(DL // LANES):
        col = HEADS * DQ + j * LANES
        block[j * SPAN : (j + 1) * SPAN] = both_ref[:, col : col + LANES]
    rope = both_ref[:, HEADS * DQ + DL : HEADS * DQ + DL + DR]
    block[PACKED - HALF :, :DR] = rope[:HALF]
    block[PACKED - HALF :, DR:] = rope[HALF:]
    moves = [pltpu.make_async_copy(block, kv_ref.at[to], sems.at[to]) for to in range(NY)]
    for move in moves:
        move.start()
    q_ref[...] = both_ref[:, : HEADS * DQ]
    for move in moves:
        move.wait()


def pack(both, floor):
    vmem = pl.BlockSpec(memory_space=pltpu.VMEM)
    hbm = pl.BlockSpec(memory_space=pl.ANY)
    return pl.pallas_call(
        pack_kernel,
        out_shape=[
            jax.ShapeDtypeStruct((SPAN, HEADS * DQ), jnp.bfloat16),
            jax.ShapeDtypeStruct((NY, PACKED, LANES), jnp.bfloat16),
        ],
        in_specs=[vmem, hbm],
        out_specs=[vmem, hbm],
        scratch_shapes=[pltpu.VMEM((PACKED, LANES), jnp.bfloat16), pltpu.SemaphoreType.DMA((NY,))],
        compiler_params=pltpu.CompilerParams(vmem_limit_bytes=8 * 1024 * 1024),
        cost_estimate=pl.CostEstimate(flops=4_000_000_000, bytes_accessed=1_000_000, transcendentals=0),
    )(both, floor)


def fill_keys(keys, kv, first, own_block):
    count = NY * SPAN
    blocks = 2 * count // HALF
    for b in range(NY):
        here = slice(b * SPAN, (b + 1) * SPAN)
        for j in range(DL // LANES):
            keys[here, j * LANES : (j + 1) * LANES] = kv[b, j * SPAN : (j + 1) * SPAN]
        keys[b * SPAN : b * SPAN + HALF, DL : DL + DR] = kv[b, PACKED - HALF :, :DR]
        keys[b * SPAN + HALF : (b + 1) * SPAN, DL : DL + DR] = kv[b, PACKED - HALF :, DR:]
    keys[:, DL + DR : WIDE] = jnp.zeros((count, WIDE - DL - DR), jnp.bfloat16)
    key = lax.broadcasted_iota(jnp.int32, (count, EXTRA), 0)
    col = lax.broadcasted_iota(jnp.int32, (count, EXTRA), 1)
    ones = col == key // HALF + first
    if own_block is not None:
        in_own = (key // HALF == own_block) | (key // HALF == own_block + 1)
        ones = ones | (in_own & (col == blocks + key - own_block * HALF))
    keys[:, WIDE:] = jnp.where(ones, 1.0, 0.0).astype(jnp.bfloat16)


def pair_scores(q_ref, floor, keys, p):
    rows = NX * SPAN
    q = jnp.concatenate(
        [q_ref[2 * p : 2 * p + 2].reshape(2 * rows, WIDE), jnp.concatenate([floor, floor], axis=0)], axis=1
    )
    return lax.dot_general(q, keys[...], (((1,), (1,)), ((), ())), preferred_element_type=jnp.float32)


def pair_values(keys, w_uv, p):
    w = jnp.concatenate([w_uv[2 * p], w_uv[2 * p + 1]], axis=1)
    return jnp.dot(keys[:, :DL], w, preferred_element_type=jnp.float32).astype(jnp.bfloat16)


def weigh(weight, values):
    rows = NX * SPAN
    weight = weight.astype(jnp.bfloat16)
    return [
        jnp.dot(weight[i * rows : (i + 1) * rows], values[:, i * DV : (i + 1) * DV], preferred_element_type=jnp.float32)
        for i in range(2)
    ]


def wide(value, count):
    return jnp.concatenate([value] * count, axis=1)


def floors_of(info_ref):
    me = info_ref[0]
    core = me % 2
    x = (me // 2) % NX
    y = me // (2 * NX)
    blocks = 2 * NY * SPAN // HALF
    lane = lax.broadcasted_iota(jnp.int32, (HALF, EXTRA), 1)
    token = lax.broadcasted_iota(jnp.int32, (HALF, EXTRA), 0)
    key_block = jnp.zeros((HALF, EXTRA), jnp.int32)
    for which in range(blocks):
        side_core = core if which < blocks // 2 else 1 - core
        slot = (((which // 2) % NY) * NX + x) * 2 + side_core
        key_block = jnp.where(lane == which, info_ref[1 + 2 * slot + which % 2], key_block)
    floors = []
    for step in range(NX):
        slot = (y * NX + (x - step + NX) % NX) * 2 + core
        for half in range(2):
            ahead = (lane < blocks) & (key_block > info_ref[1 + 2 * slot + half])
            if step == 0:
                own = lane - blocks - half * HALF
                ahead = ahead | ((own >= 0) & (own < HALF) & (own > token))
            floors.append(jnp.where(ahead, FLOOR_SCORE, 0.0))
    return jnp.concatenate(floors, axis=0).astype(jnp.bfloat16)


def floor_kernel(info_ref, floor_ref):
    floor_ref[...] = floors_of(info_ref)


def make_floor(info):
    vmem = pl.BlockSpec(memory_space=pltpu.VMEM)
    smem = pl.BlockSpec(memory_space=pltpu.SMEM)
    return pl.pallas_call(
        floor_kernel,
        out_shape=jax.ShapeDtypeStruct((NX * SPAN, EXTRA), jnp.bfloat16),
        in_specs=[smem],
        out_specs=vmem,
        compiler_params=pltpu.CompilerParams(vmem_limit_bytes=8 * 1024 * 1024),
        cost_estimate=pl.CostEstimate(flops=4_000_000_000, bytes_accessed=500_000, transcendentals=0),
    )(info)


def own_kernel(place_ref, q0, q1, q2, q3, w_uk, w_uv, kv, floor_ref, q_ref, sum_ref, top_ref, total_ref, keys):
    rows = NX * SPAN
    floor = floor_ref[...]
    none = jnp.zeros((rows, WIDE - DL - DR), jnp.bfloat16)

    def fill_queries(h):
        here = slice(h * DQ, (h + 1) * DQ)
        q = jnp.concatenate([q0[:, here], q1[:, here], q2[:, here], q3[:, here]], axis=0)
        q_lat = lax.dot_general(
            q[:, :DN], w_uk[h], (((1,), (1,)), ((), ())), preferred_element_type=jnp.float32
        )
        q_ref[h, :, :DL] = q_lat.astype(jnp.bfloat16)
        q_ref[h, :, DL : DL + DR] = q[:, DN:]
        q_ref[h, :, DL + DR : WIDE] = none

    fill_queries(0)
    fill_queries(1)
    fill_keys(keys, kv, 0, place_ref[0] // (2 * NX) * 2)
    ahead = pair_scores(q_ref, floor, keys, 0)
    for p in range(HEADS // 2):
        s = ahead
        values = pair_values(keys, w_uv, p)
        if p + 1 < HEADS // 2:
            fill_queries(2 * p + 2)
            fill_queries(2 * p + 3)
            ahead = pair_scores(q_ref, floor, keys, p + 1)
        top = jnp.max(s, axis=1, keepdims=True)
        weight = jnp.exp2((s - top) * SCALE2)
        total = jnp.sum(weight, axis=1, keepdims=True)
        sums = weigh(weight, values)
        for i in range(2):
            sum_ref[2 * p + i] = sums[i]
        pair = slice(2 * p, 2 * p + 2)
        top_ref[pair] = jnp.broadcast_to(top, (2 * rows, STAT)).reshape(2, rows, STAT)
        total_ref[pair] = jnp.broadcast_to(total, (2 * rows, STAT)).reshape(2, rows, STAT)


def attend_own(place, qs, w_uk, w_uv, kv, floor):
    vmem = pl.BlockSpec(memory_space=pltpu.VMEM)
    smem = pl.BlockSpec(memory_space=pltpu.SMEM)
    rows = NX * SPAN
    return pl.pallas_call(
        own_kernel,
        out_shape=[
            jax.ShapeDtypeStruct((HEADS, rows, WIDE), jnp.bfloat16),
            jax.ShapeDtypeStruct((HEADS, rows, DV), jnp.float32),
            jax.ShapeDtypeStruct((HEADS, rows, STAT), jnp.float32),
            jax.ShapeDtypeStruct((HEADS, rows, STAT), jnp.float32),
        ],
        in_specs=[smem] + [vmem] * 8,
        out_specs=[vmem] * 4,
        scratch_shapes=[pltpu.VMEM((NY * SPAN, WIDE + EXTRA), jnp.bfloat16)],
        compiler_params=pltpu.CompilerParams(vmem_limit_bytes=20 * 1024 * 1024),
        cost_estimate=pl.CostEstimate(flops=6_000_000_000, bytes_accessed=5_000_000, transcendentals=1_000_000),
    )(place, *qs, w_uk, w_uv, kv, floor)


def head_scores(q_ref, floor, keys, h):
    q = jnp.concatenate([q_ref[h], floor], axis=1)
    return lax.dot_general(q, keys[...], (((1,), (1,)), ((), ())), preferred_element_type=jnp.float32)


def other_kernel(place_ref, q_ref, floor_ref, kv, sum_ref, top_ref, total_ref, w_uv, out_ref, keys):
    x = (place_ref[0] // 2) % NX
    rows = NX * SPAN
    floor = floor_ref[...]
    fill_keys(keys, kv, NY * SPAN // HALF, None)
    lanes = lax.broadcasted_iota(jnp.int32, (rows, STAT), 1)
    level = jnp.zeros((rows, STAT), jnp.float32)
    ahead = head_scores(q_ref, floor, keys, 0)
    for h in range(HEADS):
        s = ahead
        if h % 2 == 0:
            values = pair_values(keys, w_uv, h // 2)
        if h + 1 < HEADS:
            ahead = head_scores(q_ref, floor, keys, h + 1)
        old_top = top_ref[h]
        top = jnp.maximum(old_top, jnp.max(s, axis=1, keepdims=True))
        shrink = jnp.exp2((old_top - top) * SCALE2)
        weight = jnp.exp2((s - wide(top, NY * SPAN // STAT)) * SCALE2)
        total = total_ref[h] * shrink + jnp.sum(weight, axis=1, keepdims=True)
        value = values[:, h % 2 * DV : (h % 2 + 1) * DV]
        sums = jnp.dot(weight.astype(jnp.bfloat16), value, preferred_element_type=jnp.float32)
        out = ((sums + sum_ref[h] * shrink) * (1.0 / total)).astype(jnp.bfloat16)
        for step in range(NX):
            to = (x + NX - step) % NX
            out_ref[to, :, h * DV : (h + 1) * DV] = out[step * SPAN : (step + 1) * SPAN]
        level = jnp.where(lanes % HEADS == h, top * SCALE2 + jnp.log2(total), level)
    high = level.astype(jnp.bfloat16)
    rest = level - high.astype(jnp.float32)
    middle = rest.astype(jnp.bfloat16)
    low = (rest - middle.astype(jnp.float32)).astype(jnp.bfloat16)
    part = lanes // HEADS
    packed = jnp.where(
        part == 0,
        high.astype(jnp.float32),
        jnp.where(part == 1, middle.astype(jnp.float32), jnp.where(part == 2, low.astype(jnp.float32), 0.0)),
    ).astype(jnp.bfloat16)
    for step in range(NX):
        to = (x + NX - step) % NX
        out_ref[to, :, HEADS * DV :] = packed[step * SPAN : (step + 1) * SPAN]


def attend_other(place, q_all, floor, kv, state, w_uv):
    vmem = pl.BlockSpec(memory_space=pltpu.VMEM)
    smem = pl.BlockSpec(memory_space=pltpu.SMEM)
    rows = NX * SPAN
    return pl.pallas_call(
        other_kernel,
        out_shape=jax.ShapeDtypeStruct((NX, SPAN, HEADS * DV + STAT), jnp.bfloat16),
        in_specs=[smem] + [vmem] * 7,
        out_specs=vmem,
        scratch_shapes=[pltpu.VMEM((NY * SPAN, WIDE + EXTRA), jnp.bfloat16)],
        compiler_params=pltpu.CompilerParams(vmem_limit_bytes=20 * 1024 * 1024),
        cost_estimate=pl.CostEstimate(flops=4_000_000_000, bytes_accessed=5_000_000, transcendentals=1_000_000),
    )(place, q_all, floor, kv, *state, w_uv)


def merge_kernel(p_ref, out_ref, held, sems):
    levels = []
    for x in range(NX):
        pieces = p_ref[x, :, :, HEADS * DV :].astype(jnp.float32).reshape(SPAN, STAT)
        rest = pltpu.roll(pieces, STAT - HEADS, 1) + pltpu.roll(pieces, STAT - 2 * HEADS, 1)
        levels.append(pieces + rest)
    top = functools.reduce(jnp.maximum, levels)
    shares = [jnp.exp2(level - top) for level in levels]
    whole = functools.reduce(jnp.add, shares)
    shares = [share / whole for share in shares]
    tokens = SPAN // NZ
    moves = []
    for z in range(NZ):
        here = slice(z * tokens, (z + 1) * tokens)
        for h in range(HEADS):
            acc = jnp.zeros((tokens, DV), jnp.float32)
            for x in range(NX):
                acc = acc + shares[x][here, h : h + 1] * p_ref[x, z, :, h * DV : (h + 1) * DV].astype(jnp.float32)
            held[:, (z * HEADS + h) * DV : (z * HEADS + h + 1) * DV] = acc.astype(jnp.bfloat16)
        cols = slice(z * HEADS * DV, (z + 1) * HEADS * DV)
        moves.append(pltpu.make_async_copy(held.at[:, cols], out_ref.at[:, cols], sems.at[z]))
        moves[-1].start()
    for move in moves:
        move.wait()


def merge(parts):
    vmem = pl.BlockSpec(memory_space=pltpu.VMEM)
    return pl.pallas_call(
        merge_kernel,
        out_shape=jax.ShapeDtypeStruct((SPAN // NZ, NZ * HEADS * DV), jnp.bfloat16),
        in_specs=[vmem],
        out_specs=pl.BlockSpec(memory_space=pl.ANY),
        scratch_shapes=[
            pltpu.VMEM((SPAN // NZ, NZ * HEADS * DV), jnp.bfloat16),
            pltpu.SemaphoreType.DMA((NZ,)),
        ],
        compiler_params=pltpu.CompilerParams(vmem_limit_bytes=8 * 1024 * 1024),
        cost_estimate=pl.CostEstimate(flops=1_000_000, bytes_accessed=800_000, transcendentals=2000),
    )(parts)


def on_device(queries, latent, rope_key, w_uk, w_uv, block_order):
    place = lax.axis_index(CTX).astype(jnp.int32).reshape(1)
    floor = make_floor(jnp.concatenate([place, block_order]))
    both = spread(queries, latent, rope_key)
    both = lax.all_to_all(both, "z", split_axis=0, concat_axis=0, tiled=True).reshape(SPAN, HEADS * DQ + WIDE)
    q_own, kv = pack(both, floor)
    kv_own = lax.all_to_all(kv, "y", split_axis=0, concat_axis=0, tiled=True)
    kv_sib = lax.ppermute(kv_own, "core", CORE_SWAP)
    qs = [q_own] + [lax.ppermute(q_own, "x", along_x(step)) for step in range(1, NX)]
    q_all, *state = attend_own(place, qs, w_uk, w_uv, kv_own, floor)
    partial = attend_other(place, q_all, floor, kv_sib, state, w_uv)
    rows = SPAN // NZ
    partial = partial.reshape(NX * NZ, rows, HEADS * DV + STAT)
    parts = lax.all_to_all(partial, ("x", "z"), split_axis=0, concat_axis=0, tiled=True)
    return merge(parts.reshape(NX, NZ, rows, HEADS * DV + STAT))


def solution(mesh):
    fine = jax.sharding.Mesh(mesh.devices.reshape(NY, NX, 2, NZ), ("y", "x", "core", "z"))
    tokens = P(("y", "x", "core", "z"), None)
    in_specs = (tokens, tokens, tokens, P("z", None, None), P("z", None, None), P())
    return jax.shard_map(on_device, mesh=fine, in_specs=in_specs, out_specs=tokens, check_vma=False)
```

```python
import functools

import jax
import jax.numpy as jnp
from jax import lax
from jax.experimental import pallas as pl
from jax.experimental.pallas import tpu as pltpu
from jax.sharding import PartitionSpec as P

HALF = 32
DL = 512
DR = 64
DN = 128
DV = 128
DQ = DN + DR
WIDE = 640
STAT = 128
EXTRA = 128
NX = 4
NY = 8
NZ = 8
HEADS = 8
SPAN = 64
LANES = 128
PACKED = DL // LANES * SPAN + HALF
FLOOR_SCORE = -1e30
LOG2E = 1.4426950408889634
SCALE2 = DQ ** (-0.5) * LOG2E


def along_x(step):
    return [(x, (x + step) % NX) for x in range(NX)]


CORE_SWAP = [(0, 1), (1, 0)]
CTX = ("y", "x", "core")


def spread_kernel(q_ref, lat_ref, rope_ref, out_ref):
    end = HEADS * DQ
    for z in range(NZ):
        out_ref[z, :, :end] = q_ref[:, z * end : (z + 1) * end]
        out_ref[z, :, end : end + DL] = lat_ref[...]
        out_ref[z, :, end + DL : end + DL + DR] = rope_ref[...]
        out_ref[z, :, end + DL + DR :] = jnp.zeros_like(rope_ref)


def spread(queries, latent, rope_key):
    vmem = pl.BlockSpec(memory_space=pltpu.VMEM)
    return pl.pallas_call(
        spread_kernel,
        out_shape=jax.ShapeDtypeStruct((NZ, SPAN // NZ, HEADS * DQ + WIDE), jnp.bfloat16),
        in_specs=[vmem] * 3,
        out_specs=vmem,
        compiler_params=pltpu.CompilerParams(vmem_limit_bytes=60 * 1024 * 1024),
        cost_estimate=pl.CostEstimate(flops=1_000_000, bytes_accessed=500_000, transcendentals=0),
    )(queries, latent, rope_key)


def pack_kernel(both_ref, floor_ref, q_ref, kv_ref):
    del floor_ref
    q_ref[...] = both_ref[:, : HEADS * DQ]
    rope = both_ref[:, HEADS * DQ + DL : HEADS * DQ + DL + DR]
    for to in range(NY):
        for j in range(DL // LANES):
            col = HEADS * DQ + j * LANES
            kv_ref[to, j * SPAN : (j + 1) * SPAN] = both_ref[:, col : col + LANES]
        kv_ref[to, PACKED - HALF :, :DR] = rope[:HALF]
        kv_ref[to, PACKED - HALF :, DR:] = rope[HALF:]


def pack(both, floor):
    vmem = pl.BlockSpec(memory_space=pltpu.VMEM)
    return pl.pallas_call(
        pack_kernel,
        out_shape=[
            jax.ShapeDtypeStruct((SPAN, HEADS * DQ), jnp.bfloat16),
            jax.ShapeDtypeStruct((NY, PACKED, LANES), jnp.bfloat16),
        ],
        in_specs=[vmem] + [pl.BlockSpec(memory_space=pl.ANY)],
        out_specs=[vmem] * 2,
        compiler_params=pltpu.CompilerParams(vmem_limit_bytes=8 * 1024 * 1024),
        cost_estimate=pl.CostEstimate(flops=4_000_000_000, bytes_accessed=1_000_000, transcendentals=0),
    )(both, floor)


def fill_keys(keys, kv, first, own_block):
    count = NY * SPAN
    blocks = 2 * count // HALF
    for b in range(NY):
        here = slice(b * SPAN, (b + 1) * SPAN)
        for j in range(DL // LANES):
            keys[here, j * LANES : (j + 1) * LANES] = kv[b, j * SPAN : (j + 1) * SPAN]
        keys[b * SPAN : b * SPAN + HALF, DL : DL + DR] = kv[b, PACKED - HALF :, :DR]
        keys[b * SPAN + HALF : (b + 1) * SPAN, DL : DL + DR] = kv[b, PACKED - HALF :, DR:]
    keys[:, DL + DR : WIDE] = jnp.zeros((count, WIDE - DL - DR), jnp.bfloat16)
    key = lax.broadcasted_iota(jnp.int32, (count, EXTRA), 0)
    col = lax.broadcasted_iota(jnp.int32, (count, EXTRA), 1)
    ones = col == key // HALF + first
    if own_block is not None:
        in_own = (key // HALF == own_block) | (key // HALF == own_block + 1)
        ones = ones | (in_own & (col == blocks + key - own_block * HALF))
    keys[:, WIDE:] = jnp.where(ones, 1.0, 0.0).astype(jnp.bfloat16)


PART = 256


def part_scores(q_ref, floor, keys, h, part):
    q = jnp.concatenate([q_ref[h], floor], axis=1)
    return lax.dot_general(
        q, keys[part * PART : (part + 1) * PART], (((1,), (1,)), ((), ())), preferred_element_type=jnp.float32
    )


def pair_values(keys, w_uv, p):
    w = jnp.concatenate([w_uv[2 * p], w_uv[2 * p + 1]], axis=1)
    return jnp.dot(keys[:, :DL], w, preferred_element_type=jnp.float32).astype(jnp.bfloat16)


def wide(value, count):
    return jnp.concatenate([value] * count, axis=1)


def floors_of(info_ref):
    me = info_ref[0]
    core = me % 2
    x = (me // 2) % NX
    y = me // (2 * NX)
    blocks = 2 * NY * SPAN // HALF
    lane = lax.broadcasted_iota(jnp.int32, (HALF, EXTRA), 1)
    token = lax.broadcasted_iota(jnp.int32, (HALF, EXTRA), 0)
    key_block = jnp.zeros((HALF, EXTRA), jnp.int32)
    for which in range(blocks):
        side_core = core if which < blocks // 2 else 1 - core
        slot = (((which // 2) % NY) * NX + x) * 2 + side_core
        key_block = jnp.where(lane == which, info_ref[1 + 2 * slot + which % 2], key_block)
    floors = []
    for step in range(NX):
        slot = (y * NX + (x - step + NX) % NX) * 2 + core
        for half in range(2):
            ahead = (lane < blocks) & (key_block > info_ref[1 + 2 * slot + half])
            if step == 0:
                own = lane - blocks - half * HALF
                ahead = ahead | ((own >= 0) & (own < HALF) & (own > token))
            floors.append(jnp.where(ahead, FLOOR_SCORE, 0.0))
    return jnp.concatenate(floors, axis=0).astype(jnp.bfloat16)


def floor_kernel(info_ref, floor_ref):
    floor_ref[...] = floors_of(info_ref)


def make_floor(info):
    vmem = pl.BlockSpec(memory_space=pltpu.VMEM)
    smem = pl.BlockSpec(memory_space=pltpu.SMEM)
    return pl.pallas_call(
        floor_kernel,
        out_shape=jax.ShapeDtypeStruct((NX * SPAN, EXTRA), jnp.bfloat16),
        in_specs=[smem],
        out_specs=vmem,
        compiler_params=pltpu.CompilerParams(vmem_limit_bytes=8 * 1024 * 1024),
        cost_estimate=pl.CostEstimate(flops=4_000_000_000, bytes_accessed=500_000, transcendentals=0),
    )(info)


def own_kernel(place_ref, q0, q1, q2, q3, w_uk, w_uv, kv, floor_ref, q_ref, sum_ref, top_ref, total_ref, keys):
    rows = NX * SPAN
    floor = floor_ref[...]
    none = jnp.zeros((rows, WIDE - DL - DR), jnp.bfloat16)

    def fill_queries(h):
        here = slice(h * DQ, (h + 1) * DQ)
        q = jnp.concatenate([q0[:, here], q1[:, here], q2[:, here], q3[:, here]], axis=0)
        q_lat = lax.dot_general(
            q[:, :DN], w_uk[h], (((1,), (1,)), ((), ())), preferred_element_type=jnp.float32
        )
        q_ref[h, :, :DL] = q_lat.astype(jnp.bfloat16)
        q_ref[h, :, DL : DL + DR] = q[:, DN:]
        q_ref[h, :, DL + DR : WIDE] = none

    fill_queries(0)
    fill_queries(1)
    fill_keys(keys, kv, 0, place_ref[0] // (2 * NX) * 2)
    s = [part_scores(q_ref, floor, keys, 0, part) for part in range(2)]
    for h in range(HEADS):
        ahead = []
        if h + 1 < HEADS:
            ahead.append(part_scores(q_ref, floor, keys, h + 1, 0))
        top = jnp.max(jnp.maximum(s[0], s[1]), axis=1, keepdims=True)
        first = jnp.exp2((s[0] - top) * SCALE2)
        if h + 2 < HEADS:
            fill_queries(h + 2)
        if h + 1 < HEADS:
            ahead.append(part_scores(q_ref, floor, keys, h + 1, 1))
        second = jnp.exp2((s[1] - top) * SCALE2)
        if h % 2 == 0:
            values = pair_values(keys, w_uv, h // 2)
        total = jnp.sum(first + second, axis=1, keepdims=True)
        value = values[:, h % 2 * DV : (h % 2 + 1) * DV]
        sum_ref[h] = jnp.dot(
            first.astype(jnp.bfloat16), value[:PART], preferred_element_type=jnp.float32
        ) + jnp.dot(second.astype(jnp.bfloat16), value[PART:], preferred_element_type=jnp.float32)
        top_ref[h] = jnp.broadcast_to(top, (rows, STAT))
        total_ref[h] = jnp.broadcast_to(total, (rows, STAT))
        s = ahead


def attend_own(place, qs, w_uk, w_uv, kv, floor):
    vmem = pl.BlockSpec(memory_space=pltpu.VMEM)
    smem = pl.BlockSpec(memory_space=pltpu.SMEM)
    rows = NX * SPAN
    return pl.pallas_call(
        own_kernel,
        out_shape=[
            jax.ShapeDtypeStruct((HEADS, rows, WIDE), jnp.bfloat16),
            jax.ShapeDtypeStruct((HEADS, rows, DV), jnp.float32),
            jax.ShapeDtypeStruct((HEADS, rows, STAT), jnp.float32),
            jax.ShapeDtypeStruct((HEADS, rows, STAT), jnp.float32),
        ],
        in_specs=[smem] + [vmem] * 8,
        out_specs=[vmem] * 4,
        scratch_shapes=[pltpu.VMEM((NY * SPAN, WIDE + EXTRA), jnp.bfloat16)],
        compiler_params=pltpu.CompilerParams(vmem_limit_bytes=20 * 1024 * 1024),
        cost_estimate=pl.CostEstimate(flops=6_000_000_000, bytes_accessed=5_000_000, transcendentals=1_000_000),
    )(place, *qs, w_uk, w_uv, kv, floor)


def other_kernel(place_ref, q_ref, floor_ref, kv, sum_ref, top_ref, total_ref, w_uv, out_ref, keys):
    x = (place_ref[0] // 2) % NX
    rows = NX * SPAN
    floor = floor_ref[...]
    fill_keys(keys, kv, NY * SPAN // HALF, None)
    lanes = lax.broadcasted_iota(jnp.int32, (rows, STAT), 1)
    level = jnp.zeros((rows, STAT), jnp.float32)
    s = [part_scores(q_ref, floor, keys, 0, part) for part in range(2)]
    for h in range(HEADS):
        ahead = []
        if h + 1 < HEADS:
            ahead.append(part_scores(q_ref, floor, keys, h + 1, 0))
        old_top = top_ref[h]
        top = jnp.maximum(old_top, jnp.max(jnp.maximum(s[0], s[1]), axis=1, keepdims=True))
        shrink = jnp.exp2((old_top - top) * SCALE2)
        first = jnp.exp2((s[0] - wide(top, PART // STAT)) * SCALE2)
        if h + 1 < HEADS:
            ahead.append(part_scores(q_ref, floor, keys, h + 1, 1))
        second = jnp.exp2((s[1] - wide(top, PART // STAT)) * SCALE2)
        if h % 2 == 0:
            values = pair_values(keys, w_uv, h // 2)
        total = total_ref[h] * shrink + jnp.sum(first + second, axis=1, keepdims=True)
        value = values[:, h % 2 * DV : (h % 2 + 1) * DV]
        sums = jnp.dot(first.astype(jnp.bfloat16), value[:PART], preferred_element_type=jnp.float32) + jnp.dot(
            second.astype(jnp.bfloat16), value[PART:], preferred_element_type=jnp.float32
        )
        out = ((sums + sum_ref[h] * shrink) * (1.0 / total)).astype(jnp.bfloat16)
        for step in range(NX):
            to = (x + NX - step) % NX
            out_ref[to, :, h * DV : (h + 1) * DV] = out[step * SPAN : (step + 1) * SPAN]
        level = jnp.where(lanes % HEADS == h, top * SCALE2 + jnp.log2(total), level)
        s = ahead
    high = level.astype(jnp.bfloat16)
    rest = level - high.astype(jnp.float32)
    middle = rest.astype(jnp.bfloat16)
    low = (rest - middle.astype(jnp.float32)).astype(jnp.bfloat16)
    part = lanes // HEADS
    packed = jnp.where(
        part == 0,
        high.astype(jnp.float32),
        jnp.where(part == 1, middle.astype(jnp.float32), jnp.where(part == 2, low.astype(jnp.float32), 0.0)),
    ).astype(jnp.bfloat16)
    for step in range(NX):
        to = (x + NX - step) % NX
        out_ref[to, :, HEADS * DV :] = packed[step * SPAN : (step + 1) * SPAN]


def attend_other(place, q_all, floor, kv, state, w_uv):
    vmem = pl.BlockSpec(memory_space=pltpu.VMEM)
    smem = pl.BlockSpec(memory_space=pltpu.SMEM)
    rows = NX * SPAN
    return pl.pallas_call(
        other_kernel,
        out_shape=jax.ShapeDtypeStruct((NX, SPAN, HEADS * DV + STAT), jnp.bfloat16),
        in_specs=[smem] + [vmem] * 7,
        out_specs=vmem,
        scratch_shapes=[pltpu.VMEM((NY * SPAN, WIDE + EXTRA), jnp.bfloat16)],
        compiler_params=pltpu.CompilerParams(vmem_limit_bytes=20 * 1024 * 1024),
        cost_estimate=pl.CostEstimate(flops=4_000_000_000, bytes_accessed=5_000_000, transcendentals=1_000_000),
    )(place, q_all, floor, kv, *state, w_uv)


def merge_kernel(p_ref, out_ref, held, sems):
    levels = []
    for x in range(NX):
        pieces = p_ref[x, :, :, HEADS * DV :].astype(jnp.float32).reshape(SPAN, STAT)
        rest = pltpu.roll(pieces, STAT - HEADS, 1) + pltpu.roll(pieces, STAT - 2 * HEADS, 1)
        levels.append(pieces + rest)
    top = functools.reduce(jnp.maximum, levels)
    shares = [jnp.exp2(level - top) for level in levels]
    whole = functools.reduce(jnp.add, shares)
    shares = [share / whole for share in shares]
    tokens = SPAN // NZ
    moves = []
    for z in range(NZ):
        here = slice(z * tokens, (z + 1) * tokens)
        for h in range(HEADS):
            acc = jnp.zeros((tokens, DV), jnp.float32)
            for x in range(NX):
                acc = acc + shares[x][here, h : h + 1] * p_ref[x, z, :, h * DV : (h + 1) * DV].astype(jnp.float32)
            held[:, (z * HEADS + h) * DV : (z * HEADS + h + 1) * DV] = acc.astype(jnp.bfloat16)
        cols = slice(z * HEADS * DV, (z + 1) * HEADS * DV)
        moves.append(pltpu.make_async_copy(held.at[:, cols], out_ref.at[:, cols], sems.at[z]))
        moves[-1].start()
    for move in moves:
        move.wait()


def merge(parts):
    vmem = pl.BlockSpec(memory_space=pltpu.VMEM)
    return pl.pallas_call(
        merge_kernel,
        out_shape=jax.ShapeDtypeStruct((SPAN // NZ, NZ * HEADS * DV), jnp.bfloat16),
        in_specs=[vmem],
        out_specs=pl.BlockSpec(memory_space=pl.ANY),
        scratch_shapes=[
            pltpu.VMEM((SPAN // NZ, NZ * HEADS * DV), jnp.bfloat16),
            pltpu.SemaphoreType.DMA((NZ,)),
        ],
        compiler_params=pltpu.CompilerParams(vmem_limit_bytes=8 * 1024 * 1024),
        cost_estimate=pl.CostEstimate(flops=1_000_000, bytes_accessed=800_000, transcendentals=2000),
    )(parts)


def on_device(queries, latent, rope_key, w_uk, w_uv, block_order):
    place = lax.axis_index(CTX).astype(jnp.int32).reshape(1)
    floor = make_floor(jnp.concatenate([place, block_order]))
    both = spread(queries, latent, rope_key)
    both = lax.all_to_all(both, "z", split_axis=0, concat_axis=0, tiled=True).reshape(SPAN, HEADS * DQ + WIDE)
    q_own, kv = pack(both, floor)
    kv_own = lax.all_to_all(kv, "y", split_axis=0, concat_axis=0, tiled=True)
    kv_sib = lax.ppermute(kv_own, "core", CORE_SWAP)
    qs = [q_own] + [lax.ppermute(q_own, "x", along_x(step)) for step in range(1, NX)]
    q_all, *state = attend_own(place, qs, w_uk, w_uv, kv_own, floor)
    partial = attend_other(place, q_all, floor, kv_sib, state, w_uv)
    rows = SPAN // NZ
    partial = partial.reshape(NX * NZ, rows, HEADS * DV + STAT)
    parts = lax.all_to_all(partial, ("x", "z"), split_axis=0, concat_axis=0, tiled=True)
    return merge(parts.reshape(NX, NZ, rows, HEADS * DV + STAT))


def solution(mesh):
    fine = jax.sharding.Mesh(mesh.devices.reshape(NY, NX, 2, NZ), ("y", "x", "core", "z"))
    tokens = P(("y", "x", "core", "z"), None)
    in_specs = (tokens, tokens, tokens, P("z", None, None), P("z", None, None), P())
    return jax.shard_map(on_device, mesh=fine, in_specs=in_specs, out_specs=tokens, check_vma=False)
```

```python
import functools

import jax
import jax.numpy as jnp
from jax import lax
from jax.experimental import pallas as pl
from jax.experimental.pallas import tpu as pltpu
from jax.sharding import PartitionSpec as P

HALF = 32
DL = 512
DR = 64
DN = 128
DV = 128
DQ = DN + DR
WIDE = 640
STAT = 128
EXTRA = 128
NX = 4
NY = 8
NZ = 8
HEADS = 8
SPAN = 64
LANES = 128
PACKED = DL // LANES * SPAN + HALF
FLOOR_SCORE = -1e30
LOG2E = 1.4426950408889634
SCALE2 = DQ ** (-0.5) * LOG2E


def along_x(step):
    return [(x, (x + step) % NX) for x in range(NX)]


CORE_SWAP = [(0, 1), (1, 0)]
CTX = ("y", "x", "core")


def spread_kernel(q_ref, lat_ref, rope_ref, out_ref):
    end = HEADS * DQ
    for z in range(NZ):
        out_ref[z, :, :end] = q_ref[:, z * end : (z + 1) * end]
        out_ref[z, :, end : end + DL] = lat_ref[...]
        out_ref[z, :, end + DL : end + DL + DR] = rope_ref[...]
        out_ref[z, :, end + DL + DR :] = jnp.zeros_like(rope_ref)


def spread(queries, latent, rope_key):
    vmem = pl.BlockSpec(memory_space=pltpu.VMEM)
    return pl.pallas_call(
        spread_kernel,
        out_shape=jax.ShapeDtypeStruct((NZ, SPAN // NZ, HEADS * DQ + WIDE), jnp.bfloat16),
        in_specs=[vmem] * 3,
        out_specs=vmem,
        compiler_params=pltpu.CompilerParams(vmem_limit_bytes=60 * 1024 * 1024),
        cost_estimate=pl.CostEstimate(flops=1_000_000, bytes_accessed=500_000, transcendentals=0),
    )(queries, latent, rope_key)


def pack_kernel(both_ref, floor_ref, q_ref, kv_ref):
    del floor_ref
    q_ref[...] = both_ref[:, : HEADS * DQ]
    rope = both_ref[:, HEADS * DQ + DL : HEADS * DQ + DL + DR]
    for to in range(NY):
        for j in range(DL // LANES):
            col = HEADS * DQ + j * LANES
            kv_ref[to, j * SPAN : (j + 1) * SPAN] = both_ref[:, col : col + LANES]
        kv_ref[to, PACKED - HALF :, :DR] = rope[:HALF]
        kv_ref[to, PACKED - HALF :, DR:] = rope[HALF:]


def pack(both, floor):
    vmem = pl.BlockSpec(memory_space=pltpu.VMEM)
    return pl.pallas_call(
        pack_kernel,
        out_shape=[
            jax.ShapeDtypeStruct((SPAN, HEADS * DQ), jnp.bfloat16),
            jax.ShapeDtypeStruct((NY, PACKED, LANES), jnp.bfloat16),
        ],
        in_specs=[vmem] + [pl.BlockSpec(memory_space=pl.ANY)],
        out_specs=[vmem] * 2,
        compiler_params=pltpu.CompilerParams(vmem_limit_bytes=8 * 1024 * 1024),
        cost_estimate=pl.CostEstimate(flops=4_000_000_000, bytes_accessed=1_000_000, transcendentals=0),
    )(both, floor)


def fill_keys(keys, kv, first, own_block):
    count = NY * SPAN
    blocks = 2 * count // HALF
    for b in range(NY):
        here = slice(b * SPAN, (b + 1) * SPAN)
        for j in range(DL // LANES):
            keys[here, j * LANES : (j + 1) * LANES] = kv[b, j * SPAN : (j + 1) * SPAN]
        keys[b * SPAN : b * SPAN + HALF, DL : DL + DR] = kv[b, PACKED - HALF :, :DR]
        keys[b * SPAN + HALF : (b + 1) * SPAN, DL : DL + DR] = kv[b, PACKED - HALF :, DR:]
    keys[:, DL + DR : WIDE] = jnp.zeros((count, WIDE - DL - DR), jnp.bfloat16)
    key = lax.broadcasted_iota(jnp.int32, (count, EXTRA), 0)
    col = lax.broadcasted_iota(jnp.int32, (count, EXTRA), 1)
    ones = col == key // HALF + first
    if own_block is not None:
        in_own = (key // HALF == own_block) | (key // HALF == own_block + 1)
        ones = ones | (in_own & (col == blocks + key - own_block * HALF))
    keys[:, WIDE:] = jnp.where(ones, 1.0, 0.0).astype(jnp.bfloat16)


def pair_scores(q_ref, floor, keys, p):
    rows = NX * SPAN
    q = jnp.concatenate(
        [q_ref[2 * p : 2 * p + 2].reshape(2 * rows, WIDE), jnp.concatenate([floor, floor], axis=0)], axis=1
    )
    return lax.dot_general(q, keys[...], (((1,), (1,)), ((), ())), preferred_element_type=jnp.float32)


def pair_values(keys, w_uv, p):
    w = jnp.concatenate([w_uv[2 * p], w_uv[2 * p + 1]], axis=1)
    values = jnp.dot(keys[:, :DL], w, preferred_element_type=jnp.float32).astype(jnp.bfloat16)
    ones = jnp.ones((NY * SPAN, STAT), jnp.bfloat16)
    return [jnp.concatenate([values[:, i * DV : (i + 1) * DV], ones], axis=1) for i in range(2)]


def weigh(weight, values):
    rows = NX * SPAN
    weight = weight.astype(jnp.bfloat16)
    both = [
        jnp.dot(weight[i * rows : (i + 1) * rows], values[i], preferred_element_type=jnp.float32) for i in range(2)
    ]
    return [one[:, :DV] for one in both], [one[:, DV:] for one in both]


def wide(value, count):
    return jnp.concatenate([value] * count, axis=1)


def floors_of(info_ref):
    me = info_ref[0]
    core = me % 2
    x = (me // 2) % NX
    y = me // (2 * NX)
    blocks = 2 * NY * SPAN // HALF
    lane = lax.broadcasted_iota(jnp.int32, (HALF, EXTRA), 1)
    token = lax.broadcasted_iota(jnp.int32, (HALF, EXTRA), 0)
    key_block = jnp.zeros((HALF, EXTRA), jnp.int32)
    for which in range(blocks):
        side_core = core if which < blocks // 2 else 1 - core
        slot = (((which // 2) % NY) * NX + x) * 2 + side_core
        key_block = jnp.where(lane == which, info_ref[1 + 2 * slot + which % 2], key_block)
    floors = []
    for step in range(NX):
        slot = (y * NX + (x - step + NX) % NX) * 2 + core
        for half in range(2):
            ahead = (lane < blocks) & (key_block > info_ref[1 + 2 * slot + half])
            if step == 0:
                own = lane - blocks - half * HALF
                ahead = ahead | ((own >= 0) & (own < HALF) & (own > token))
            floors.append(jnp.where(ahead, FLOOR_SCORE, 0.0))
    return jnp.concatenate(floors, axis=0).astype(jnp.bfloat16)


def floor_kernel(info_ref, floor_ref):
    floor_ref[...] = floors_of(info_ref)


def make_floor(info):
    vmem = pl.BlockSpec(memory_space=pltpu.VMEM)
    smem = pl.BlockSpec(memory_space=pltpu.SMEM)
    return pl.pallas_call(
        floor_kernel,
        out_shape=jax.ShapeDtypeStruct((NX * SPAN, EXTRA), jnp.bfloat16),
        in_specs=[smem],
        out_specs=vmem,
        compiler_params=pltpu.CompilerParams(vmem_limit_bytes=8 * 1024 * 1024),
        cost_estimate=pl.CostEstimate(flops=4_000_000_000, bytes_accessed=500_000, transcendentals=0),
    )(info)


def own_kernel(place_ref, q0, q1, q2, q3, w_uk, w_uv, kv, floor_ref, q_ref, sum_ref, top_ref, total_ref, keys):
    rows = NX * SPAN
    floor = floor_ref[...]
    none = jnp.zeros((rows, WIDE - DL - DR), jnp.bfloat16)

    def fill_queries(h):
        here = slice(h * DQ, (h + 1) * DQ)
        q = jnp.concatenate([q0[:, here], q1[:, here], q2[:, here], q3[:, here]], axis=0)
        q_lat = lax.dot_general(
            q[:, :DN], w_uk[h], (((1,), (1,)), ((), ())), preferred_element_type=jnp.float32
        )
        q_ref[h, :, :DL] = q_lat.astype(jnp.bfloat16)
        q_ref[h, :, DL : DL + DR] = q[:, DN:]
        q_ref[h, :, DL + DR : WIDE] = none

    fill_queries(0)
    fill_queries(1)
    fill_keys(keys, kv, 0, place_ref[0] // (2 * NX) * 2)
    ahead = pair_scores(q_ref, floor, keys, 0)
    for p in range(HEADS // 2):
        s = ahead
        values = pair_values(keys, w_uv, p)
        if p + 1 < HEADS // 2:
            fill_queries(2 * p + 2)
            fill_queries(2 * p + 3)
            ahead = pair_scores(q_ref, floor, keys, p + 1)
        top = jnp.max(s, axis=1, keepdims=True)
        weight = jnp.exp2((s - top) * SCALE2)
        sums, totals = weigh(weight, values)
        for i in range(2):
            sum_ref[2 * p + i] = sums[i]
            total_ref[2 * p + i] = totals[i]
        pair = slice(2 * p, 2 * p + 2)
        top_ref[pair] = jnp.broadcast_to(top, (2 * rows, STAT)).reshape(2, rows, STAT)


def attend_own(place, qs, w_uk, w_uv, kv, floor):
    vmem = pl.BlockSpec(memory_space=pltpu.VMEM)
    smem = pl.BlockSpec(memory_space=pltpu.SMEM)
    rows = NX * SPAN
    return pl.pallas_call(
        own_kernel,
        out_shape=[
            jax.ShapeDtypeStruct((HEADS, rows, WIDE), jnp.bfloat16),
            jax.ShapeDtypeStruct((HEADS, rows, DV), jnp.float32),
            jax.ShapeDtypeStruct((HEADS, rows, STAT), jnp.float32),
            jax.ShapeDtypeStruct((HEADS, rows, STAT), jnp.float32),
        ],
        in_specs=[smem] + [vmem] * 8,
        out_specs=[vmem] * 4,
        scratch_shapes=[pltpu.VMEM((NY * SPAN, WIDE + EXTRA), jnp.bfloat16)],
        compiler_params=pltpu.CompilerParams(vmem_limit_bytes=20 * 1024 * 1024),
        cost_estimate=pl.CostEstimate(flops=6_000_000_000, bytes_accessed=5_000_000, transcendentals=1_000_000),
    )(place, *qs, w_uk, w_uv, kv, floor)


def other_kernel(place_ref, q_ref, floor_ref, kv, sum_ref, top_ref, total_ref, w_uv, out_ref, keys):
    x = (place_ref[0] // 2) % NX
    rows = NX * SPAN
    floor = floor_ref[...]
    fill_keys(keys, kv, NY * SPAN // HALF, None)
    lanes = lax.broadcasted_iota(jnp.int32, (rows, STAT), 1)
    level = jnp.zeros((rows, STAT), jnp.float32)
    ahead = pair_scores(q_ref, floor, keys, 0)
    for p in range(HEADS // 2):
        s = ahead
        values = pair_values(keys, w_uv, p)
        if p + 1 < HEADS // 2:
            ahead = pair_scores(q_ref, floor, keys, p + 1)
        pair = slice(2 * p, 2 * p + 2)
        old_top = top_ref[pair].reshape(2 * rows, STAT)
        top = jnp.maximum(old_top, jnp.max(s, axis=1, keepdims=True))
        shrink = jnp.exp2((old_top - top) * SCALE2)
        weight = jnp.exp2((s - wide(top, NY * SPAN // STAT)) * SCALE2)
        sums, totals = weigh(weight, values)
        for i in range(2):
            h = 2 * p + i
            mine = slice(i * rows, (i + 1) * rows)
            total = totals[i] + total_ref[h] * shrink[mine]
            value = ((sums[i] + sum_ref[h] * shrink[mine]) * (1.0 / total)).astype(jnp.bfloat16)
            for step in range(NX):
                to = (x + NX - step) % NX
                out_ref[to, :, h * DV : (h + 1) * DV] = value[step * SPAN : (step + 1) * SPAN]
            level = jnp.where(lanes % HEADS == h, top[mine] * SCALE2 + jnp.log2(total), level)
    high = level.astype(jnp.bfloat16)
    rest = level - high.astype(jnp.float32)
    middle = rest.astype(jnp.bfloat16)
    low = (rest - middle.astype(jnp.float32)).astype(jnp.bfloat16)
    part = lanes // HEADS
    packed = jnp.where(
        part == 0,
        high.astype(jnp.float32),
        jnp.where(part == 1, middle.astype(jnp.float32), jnp.where(part == 2, low.astype(jnp.float32), 0.0)),
    ).astype(jnp.bfloat16)
    for step in range(NX):
        to = (x + NX - step) % NX
        out_ref[to, :, HEADS * DV :] = packed[step * SPAN : (step + 1) * SPAN]


def attend_other(place, q_all, floor, kv, state, w_uv):
    vmem = pl.BlockSpec(memory_space=pltpu.VMEM)
    smem = pl.BlockSpec(memory_space=pltpu.SMEM)
    rows = NX * SPAN
    return pl.pallas_call(
        other_kernel,
        out_shape=jax.ShapeDtypeStruct((NX, SPAN, HEADS * DV + STAT), jnp.bfloat16),
        in_specs=[smem] + [vmem] * 7,
        out_specs=vmem,
        scratch_shapes=[pltpu.VMEM((NY * SPAN, WIDE + EXTRA), jnp.bfloat16)],
        compiler_params=pltpu.CompilerParams(vmem_limit_bytes=20 * 1024 * 1024),
        cost_estimate=pl.CostEstimate(flops=4_000_000_000, bytes_accessed=5_000_000, transcendentals=1_000_000),
    )(place, q_all, floor, kv, *state, w_uv)


def merge_kernel(p_ref, out_ref, held, sems):
    levels = []
    for x in range(NX):
        pieces = p_ref[x, :, :, HEADS * DV :].astype(jnp.float32).reshape(SPAN, STAT)
        rest = pltpu.roll(pieces, STAT - HEADS, 1) + pltpu.roll(pieces, STAT - 2 * HEADS, 1)
        levels.append(pieces + rest)
    top = functools.reduce(jnp.maximum, levels)
    shares = [jnp.exp2(level - top) for level in levels]
    whole = functools.reduce(jnp.add, shares)
    shares = [share / whole for share in shares]
    tokens = SPAN // NZ
    moves = []
    for z in range(NZ):
        here = slice(z * tokens, (z + 1) * tokens)
        for h in range(HEADS):
            acc = jnp.zeros((tokens, DV), jnp.float32)
            for x in range(NX):
                acc = acc + shares[x][here, h : h + 1] * p_ref[x, z, :, h * DV : (h + 1) * DV].astype(jnp.float32)
            held[:, (z * HEADS + h) * DV : (z * HEADS + h + 1) * DV] = acc.astype(jnp.bfloat16)
        cols = slice(z * HEADS * DV, (z + 1) * HEADS * DV)
        moves.append(pltpu.make_async_copy(held.at[:, cols], out_ref.at[:, cols], sems.at[z]))
        moves[-1].start()
    for move in moves:
        move.wait()


def merge(parts):
    vmem = pl.BlockSpec(memory_space=pltpu.VMEM)
    return pl.pallas_call(
        merge_kernel,
        out_shape=jax.ShapeDtypeStruct((SPAN // NZ, NZ * HEADS * DV), jnp.bfloat16),
        in_specs=[vmem],
        out_specs=pl.BlockSpec(memory_space=pl.ANY),
        scratch_shapes=[
            pltpu.VMEM((SPAN // NZ, NZ * HEADS * DV), jnp.bfloat16),
            pltpu.SemaphoreType.DMA((NZ,)),
        ],
        compiler_params=pltpu.CompilerParams(vmem_limit_bytes=8 * 1024 * 1024),
        cost_estimate=pl.CostEstimate(flops=1_000_000, bytes_accessed=800_000, transcendentals=2000),
    )(parts)


def on_device(queries, latent, rope_key, w_uk, w_uv, block_order):
    place = lax.axis_index(CTX).astype(jnp.int32).reshape(1)
    floor = make_floor(jnp.concatenate([place, block_order]))
    both = spread(queries, latent, rope_key)
    both = lax.all_to_all(both, "z", split_axis=0, concat_axis=0, tiled=True).reshape(SPAN, HEADS * DQ + WIDE)
    q_own, kv = pack(both, floor)
    kv_own = lax.all_to_all(kv, "y", split_axis=0, concat_axis=0, tiled=True)
    kv_sib = lax.ppermute(kv_own, "core", CORE_SWAP)
    qs = [q_own] + [lax.ppermute(q_own, "x", along_x(step)) for step in range(1, NX)]
    q_all, *state = attend_own(place, qs, w_uk, w_uv, kv_own, floor)
    partial = attend_other(place, q_all, floor, kv_sib, state, w_uv)
    rows = SPAN // NZ
    partial = partial.reshape(NX * NZ, rows, HEADS * DV + STAT)
    parts = lax.all_to_all(partial, ("x", "z"), split_axis=0, concat_axis=0, tiled=True)
    return merge(parts.reshape(NX, NZ, rows, HEADS * DV + STAT))


def solution(mesh):
    fine = jax.sharding.Mesh(mesh.devices.reshape(NY, NX, 2, NZ), ("y", "x", "core", "z"))
    tokens = P(("y", "x", "core", "z"), None)
    in_specs = (tokens, tokens, tokens, P("z", None, None), P("z", None, None), P())
    return jax.shard_map(on_device, mesh=fine, in_specs=in_specs, out_specs=tokens, check_vma=False)
```

```python
import functools

import jax
import jax.numpy as jnp
from jax import lax
from jax.experimental import pallas as pl
from jax.experimental.pallas import tpu as pltpu
from jax.sharding import PartitionSpec as P

HALF = 32
DL = 512
DR = 64
DN = 128
DV = 128
DQ = DN + DR
WIDE = 640
STAT = 128
EXTRA = 128
NX = 4
NY = 8
NZ = 8
HEADS = 8
SPAN = 64
LANES = 128
PACKED = DL // LANES * SPAN + HALF
FLOOR_SCORE = -1e30
LOG2E = 1.4426950408889634
SCALE2 = DQ ** (-0.5) * LOG2E


def along_x(step):
    return [(x, (x + step) % NX) for x in range(NX)]


CORE_SWAP = [(0, 1), (1, 0)]
CTX = ("y", "x", "core")


def spread_kernel(q_ref, lat_ref, rope_ref, out_ref):
    end = HEADS * DQ
    for z in range(NZ):
        out_ref[z, :, :end] = q_ref[:, z * end : (z + 1) * end]
        out_ref[z, :, end : end + DL] = lat_ref[...]
        out_ref[z, :, end + DL : end + DL + DR] = rope_ref[...]
        out_ref[z, :, end + DL + DR :] = jnp.zeros_like(rope_ref)


def spread(queries, latent, rope_key):
    vmem = pl.BlockSpec(memory_space=pltpu.VMEM)
    return pl.pallas_call(
        spread_kernel,
        out_shape=jax.ShapeDtypeStruct((NZ, SPAN // NZ, HEADS * DQ + WIDE), jnp.bfloat16),
        in_specs=[vmem] * 3,
        out_specs=vmem,
        compiler_params=pltpu.CompilerParams(vmem_limit_bytes=60 * 1024 * 1024),
        cost_estimate=pl.CostEstimate(flops=1_000_000, bytes_accessed=500_000, transcendentals=0),
    )(queries, latent, rope_key)


def pack_kernel(both_ref, floor_ref, q_ref, kv_ref):
    del floor_ref
    q_ref[...] = both_ref[:, : HEADS * DQ]
    rope = both_ref[:, HEADS * DQ + DL : HEADS * DQ + DL + DR]
    for to in range(NY):
        for j in range(DL // LANES):
            col = HEADS * DQ + j * LANES
            kv_ref[to, j * SPAN : (j + 1) * SPAN] = both_ref[:, col : col + LANES]
        kv_ref[to, PACKED - HALF :, :DR] = rope[:HALF]
        kv_ref[to, PACKED - HALF :, DR:] = rope[HALF:]


def pack(both, floor):
    vmem = pl.BlockSpec(memory_space=pltpu.VMEM)
    return pl.pallas_call(
        pack_kernel,
        out_shape=[
            jax.ShapeDtypeStruct((SPAN, HEADS * DQ), jnp.bfloat16),
            jax.ShapeDtypeStruct((NY, PACKED, LANES), jnp.bfloat16),
        ],
        in_specs=[vmem] + [pl.BlockSpec(memory_space=pl.ANY)],
        out_specs=[vmem] * 2,
        compiler_params=pltpu.CompilerParams(vmem_limit_bytes=8 * 1024 * 1024),
        cost_estimate=pl.CostEstimate(flops=4_000_000_000, bytes_accessed=1_000_000, transcendentals=0),
    )(both, floor)


def fill_keys(keys, kv, first, own_block):
    count = NY * SPAN
    blocks = 2 * count // HALF
    for b in range(NY):
        here = slice(b * SPAN, (b + 1) * SPAN)
        for j in range(DL // LANES):
            keys[here, j * LANES : (j + 1) * LANES] = kv[b, j * SPAN : (j + 1) * SPAN]
        keys[b * SPAN : b * SPAN + HALF, DL : DL + DR] = kv[b, PACKED - HALF :, :DR]
        keys[b * SPAN + HALF : (b + 1) * SPAN, DL : DL + DR] = kv[b, PACKED - HALF :, DR:]
    keys[:, DL + DR : WIDE] = jnp.zeros((count, WIDE - DL - DR), jnp.bfloat16)
    key = lax.broadcasted_iota(jnp.int32, (count, EXTRA), 0)
    col = lax.broadcasted_iota(jnp.int32, (count, EXTRA), 1)
    ones = col == key // HALF + first
    if own_block is not None:
        in_own = (key // HALF == own_block) | (key // HALF == own_block + 1)
        ones = ones | (in_own & (col == blocks + key - own_block * HALF))
    keys[:, WIDE:] = jnp.where(ones, 1.0, 0.0).astype(jnp.bfloat16)


def pair_scores(q_ref, floor, keys, p):
    rows = NX * SPAN
    q = jnp.concatenate(
        [q_ref[2 * p : 2 * p + 2].reshape(2 * rows, WIDE), jnp.concatenate([floor, floor], axis=0)], axis=1
    )
    return lax.dot_general(q, keys[...], (((1,), (1,)), ((), ())), preferred_element_type=jnp.float32)


def pair_values(keys, w_uv, p):
    w = jnp.concatenate([w_uv[2 * p], w_uv[2 * p + 1]], axis=1)
    values = jnp.dot(keys[:, :DL], w, preferred_element_type=jnp.float32).astype(jnp.bfloat16)
    ones = jnp.ones((NY * SPAN, STAT), jnp.bfloat16)
    return [jnp.concatenate([values[:, i * DV : (i + 1) * DV], ones], axis=1) for i in range(2)]


def weigh(weight, values):
    rows = NX * SPAN
    weight = weight.astype(jnp.bfloat16)
    both = [
        jnp.dot(weight[i * rows : (i + 1) * rows], values[i], preferred_element_type=jnp.float32) for i in range(2)
    ]
    return [one[:, :DV] for one in both], [one[:, DV:] for one in both]


def wide(value, count):
    return jnp.concatenate([value] * count, axis=1)


def floors_of(info_ref):
    me = info_ref[0]
    core = me % 2
    x = (me // 2) % NX
    y = me // (2 * NX)
    blocks = 2 * NY * SPAN // HALF
    lane = lax.broadcasted_iota(jnp.int32, (HALF, EXTRA), 1)
    token = lax.broadcasted_iota(jnp.int32, (HALF, EXTRA), 0)
    key_block = jnp.zeros((HALF, EXTRA), jnp.int32)
    for which in range(blocks):
        side_core = core if which < blocks // 2 else 1 - core
        slot = (((which // 2) % NY) * NX + x) * 2 + side_core
        key_block = jnp.where(lane == which, info_ref[1 + 2 * slot + which % 2], key_block)
    floors = []
    for step in range(NX):
        slot = (y * NX + (x - step + NX) % NX) * 2 + core
        for half in range(2):
            ahead = (lane < blocks) & (key_block > info_ref[1 + 2 * slot + half])
            if step == 0:
                own = lane - blocks - half * HALF
                ahead = ahead | ((own >= 0) & (own < HALF) & (own > token))
            floors.append(jnp.where(ahead, FLOOR_SCORE, 0.0))
    return jnp.concatenate(floors, axis=0).astype(jnp.bfloat16)


def floor_kernel(info_ref, floor_ref):
    floor_ref[...] = floors_of(info_ref)


def make_floor(info):
    vmem = pl.BlockSpec(memory_space=pltpu.VMEM)
    smem = pl.BlockSpec(memory_space=pltpu.SMEM)
    return pl.pallas_call(
        floor_kernel,
        out_shape=jax.ShapeDtypeStruct((NX * SPAN, EXTRA), jnp.bfloat16),
        in_specs=[smem],
        out_specs=vmem,
        compiler_params=pltpu.CompilerParams(vmem_limit_bytes=8 * 1024 * 1024),
        cost_estimate=pl.CostEstimate(flops=4_000_000_000, bytes_accessed=500_000, transcendentals=0),
    )(info)


def own_kernel(place_ref, q0, q1, q2, q3, w_uk, w_uv, kv, floor_ref, q_ref, sum_ref, top_ref, total_ref, keys):
    rows = NX * SPAN
    floor = floor_ref[...]
    none = jnp.zeros((rows, WIDE - DL - DR), jnp.bfloat16)

    def fill_queries(h):
        here = slice(h * DQ, (h + 1) * DQ)
        q = jnp.concatenate([q0[:, here], q1[:, here], q2[:, here], q3[:, here]], axis=0)
        q_lat = lax.dot_general(
            q[:, :DN], w_uk[h], (((1,), (1,)), ((), ())), preferred_element_type=jnp.float32
        )
        q_ref[h, :, :DL] = q_lat.astype(jnp.bfloat16)
        q_ref[h, :, DL : DL + DR] = q[:, DN:]
        q_ref[h, :, DL + DR : WIDE] = none

    fill_queries(0)
    fill_queries(1)
    fill_keys(keys, kv, 0, place_ref[0] // (2 * NX) * 2)
    ahead = pair_scores(q_ref, floor, keys, 0)
    for p in range(HEADS // 2):
        s = ahead
        values = pair_values(keys, w_uv, p)
        if p + 1 < HEADS // 2:
            fill_queries(2 * p + 2)
            fill_queries(2 * p + 3)
            ahead = pair_scores(q_ref, floor, keys, p + 1)
        top = jnp.max(s, axis=1, keepdims=True)
        weight = jnp.exp2(s * SCALE2 - top * SCALE2)
        sums, totals = weigh(weight, values)
        for i in range(2):
            sum_ref[2 * p + i] = sums[i]
            total_ref[2 * p + i] = totals[i]
        pair = slice(2 * p, 2 * p + 2)
        top_ref[pair] = jnp.broadcast_to(top, (2 * rows, STAT)).reshape(2, rows, STAT)


def attend_own(place, qs, w_uk, w_uv, kv, floor):
    vmem = pl.BlockSpec(memory_space=pltpu.VMEM)
    smem = pl.BlockSpec(memory_space=pltpu.SMEM)
    rows = NX * SPAN
    return pl.pallas_call(
        own_kernel,
        out_shape=[
            jax.ShapeDtypeStruct((HEADS, rows, WIDE), jnp.bfloat16),
            jax.ShapeDtypeStruct((HEADS, rows, DV), jnp.float32),
            jax.ShapeDtypeStruct((HEADS, rows, STAT), jnp.float32),
            jax.ShapeDtypeStruct((HEADS, rows, STAT), jnp.float32),
        ],
        in_specs=[smem] + [vmem] * 8,
        out_specs=[vmem] * 4,
        scratch_shapes=[pltpu.VMEM((NY * SPAN, WIDE + EXTRA), jnp.bfloat16)],
        compiler_params=pltpu.CompilerParams(vmem_limit_bytes=20 * 1024 * 1024),
        cost_estimate=pl.CostEstimate(flops=6_000_000_000, bytes_accessed=5_000_000, transcendentals=1_000_000),
    )(place, *qs, w_uk, w_uv, kv, floor)


def other_kernel(place_ref, q_ref, floor_ref, kv, sum_ref, top_ref, total_ref, w_uv, out_ref, keys):
    x = (place_ref[0] // 2) % NX
    rows = NX * SPAN
    floor = floor_ref[...]
    fill_keys(keys, kv, NY * SPAN // HALF, None)
    lanes = lax.broadcasted_iota(jnp.int32, (rows, STAT), 1)
    level = jnp.zeros((rows, STAT), jnp.float32)
    ahead = pair_scores(q_ref, floor, keys, 0)
    for p in range(HEADS // 2):
        s = ahead
        values = pair_values(keys, w_uv, p)
        if p + 1 < HEADS // 2:
            ahead = pair_scores(q_ref, floor, keys, p + 1)
        pair = slice(2 * p, 2 * p + 2)
        old_top = top_ref[pair].reshape(2 * rows, STAT)
        top = jnp.maximum(old_top, jnp.max(s, axis=1, keepdims=True))
        shrink = jnp.exp2((old_top - top) * SCALE2)
        weight = jnp.exp2(s * SCALE2 - wide(top * SCALE2, NY * SPAN // STAT))
        sums, totals = weigh(weight, values)
        for i in range(2):
            h = 2 * p + i
            mine = slice(i * rows, (i + 1) * rows)
            total = totals[i] + total_ref[h] * shrink[mine]
            value = ((sums[i] + sum_ref[h] * shrink[mine]) * (1.0 / total)).astype(jnp.bfloat16)
            for step in range(NX):
                to = (x + NX - step) % NX
                out_ref[to, :, h * DV : (h + 1) * DV] = value[step * SPAN : (step + 1) * SPAN]
            level = jnp.where(lanes % HEADS == h, top[mine] * SCALE2 + jnp.log2(total), level)
    high = level.astype(jnp.bfloat16)
    rest = level - high.astype(jnp.float32)
    middle = rest.astype(jnp.bfloat16)
    low = (rest - middle.astype(jnp.float32)).astype(jnp.bfloat16)
    part = lanes // HEADS
    packed = jnp.where(
        part == 0,
        high.astype(jnp.float32),
        jnp.where(part == 1, middle.astype(jnp.float32), jnp.where(part == 2, low.astype(jnp.float32), 0.0)),
    ).astype(jnp.bfloat16)
    for step in range(NX):
        to = (x + NX - step) % NX
        out_ref[to, :, HEADS * DV :] = packed[step * SPAN : (step + 1) * SPAN]


def attend_other(place, q_all, floor, kv, state, w_uv):
    vmem = pl.BlockSpec(memory_space=pltpu.VMEM)
    smem = pl.BlockSpec(memory_space=pltpu.SMEM)
    rows = NX * SPAN
    return pl.pallas_call(
        other_kernel,
        out_shape=jax.ShapeDtypeStruct((NX, SPAN, HEADS * DV + STAT), jnp.bfloat16),
        in_specs=[smem] + [vmem] * 7,
        out_specs=vmem,
        scratch_shapes=[pltpu.VMEM((NY * SPAN, WIDE + EXTRA), jnp.bfloat16)],
        compiler_params=pltpu.CompilerParams(vmem_limit_bytes=20 * 1024 * 1024),
        cost_estimate=pl.CostEstimate(flops=4_000_000_000, bytes_accessed=5_000_000, transcendentals=1_000_000),
    )(place, q_all, floor, kv, *state, w_uv)


def merge_kernel(p_ref, out_ref, held, sems):
    levels = []
    for x in range(NX):
        pieces = p_ref[x, :, :, HEADS * DV :].astype(jnp.float32).reshape(SPAN, STAT)
        rest = pltpu.roll(pieces, STAT - HEADS, 1) + pltpu.roll(pieces, STAT - 2 * HEADS, 1)
        levels.append(pieces + rest)
    top = functools.reduce(jnp.maximum, levels)
    shares = [jnp.exp2(level - top) for level in levels]
    whole = functools.reduce(jnp.add, shares)
    shares = [share / whole for share in shares]
    tokens = SPAN // NZ
    moves = []
    for z in range(NZ):
        here = slice(z * tokens, (z + 1) * tokens)
        for h in range(HEADS):
            acc = jnp.zeros((tokens, DV), jnp.float32)
            for x in range(NX):
                acc = acc + shares[x][here, h : h + 1] * p_ref[x, z, :, h * DV : (h + 1) * DV].astype(jnp.float32)
            held[:, (z * HEADS + h) * DV : (z * HEADS + h + 1) * DV] = acc.astype(jnp.bfloat16)
        cols = slice(z * HEADS * DV, (z + 1) * HEADS * DV)
        moves.append(pltpu.make_async_copy(held.at[:, cols], out_ref.at[:, cols], sems.at[z]))
        moves[-1].start()
    for move in moves:
        move.wait()


def merge(parts):
    vmem = pl.BlockSpec(memory_space=pltpu.VMEM)
    return pl.pallas_call(
        merge_kernel,
        out_shape=jax.ShapeDtypeStruct((SPAN // NZ, NZ * HEADS * DV), jnp.bfloat16),
        in_specs=[vmem],
        out_specs=pl.BlockSpec(memory_space=pl.ANY),
        scratch_shapes=[
            pltpu.VMEM((SPAN // NZ, NZ * HEADS * DV), jnp.bfloat16),
            pltpu.SemaphoreType.DMA((NZ,)),
        ],
        compiler_params=pltpu.CompilerParams(vmem_limit_bytes=8 * 1024 * 1024),
        cost_estimate=pl.CostEstimate(flops=1_000_000, bytes_accessed=800_000, transcendentals=2000),
    )(parts)


def on_device(queries, latent, rope_key, w_uk, w_uv, block_order):
    place = lax.axis_index(CTX).astype(jnp.int32).reshape(1)
    floor = make_floor(jnp.concatenate([place, block_order]))
    both = spread(queries, latent, rope_key)
    both = lax.all_to_all(both, "z", split_axis=0, concat_axis=0, tiled=True).reshape(SPAN, HEADS * DQ + WIDE)
    q_own, kv = pack(both, floor)
    kv_own = lax.all_to_all(kv, "y", split_axis=0, concat_axis=0, tiled=True)
    kv_sib = lax.ppermute(kv_own, "core", CORE_SWAP)
    qs = [q_own] + [lax.ppermute(q_own, "x", along_x(step)) for step in range(1, NX)]
    q_all, *state = attend_own(place, qs, w_uk, w_uv, kv_own, floor)
    partial = attend_other(place, q_all, floor, kv_sib, state, w_uv)
    rows = SPAN // NZ
    partial = partial.reshape(NX * NZ, rows, HEADS * DV + STAT)
    parts = lax.all_to_all(partial, ("x", "z"), split_axis=0, concat_axis=0, tiled=True)
    return merge(parts.reshape(NX, NZ, rows, HEADS * DV + STAT))


def solution(mesh):
    fine = jax.sharding.Mesh(mesh.devices.reshape(NY, NX, 2, NZ), ("y", "x", "core", "z"))
    tokens = P(("y", "x", "core", "z"), None)
    in_specs = (tokens, tokens, tokens, P("z", None, None), P("z", None, None), P())
    return jax.shard_map(on_device, mesh=fine, in_specs=in_specs, out_specs=tokens, check_vma=False)
```

```python
import functools

import jax
import jax.numpy as jnp
from jax import lax
from jax.experimental import pallas as pl
from jax.experimental.pallas import tpu as pltpu
from jax.sharding import PartitionSpec as P

HALF = 32
DL = 512
DR = 64
DN = 128
DV = 128
DQ = DN + DR
WIDE = 640
STAT = 128
EXTRA = 128
NX = 4
NY = 8
NZ = 8
HEADS = 8
SPAN = 64
LANES = 128
PACKED = DL // LANES * SPAN + HALF
FLOOR_SCORE = -1e30
LOG2E = 1.4426950408889634
SCALE2 = DQ ** (-0.5) * LOG2E


def along_x(step):
    return [(x, (x + step) % NX) for x in range(NX)]


CORE_SWAP = [(0, 1), (1, 0)]
CTX = ("y", "x", "core")


def spread_kernel(q_ref, lat_ref, rope_ref, out_ref):
    end = HEADS * DQ
    for z in range(NZ):
        out_ref[z, :, :end] = q_ref[:, z * end : (z + 1) * end]
        out_ref[z, :, end : end + DL] = lat_ref[...]
        out_ref[z, :, end + DL : end + DL + DR] = rope_ref[...]
        out_ref[z, :, end + DL + DR :] = jnp.zeros_like(rope_ref)


def spread(queries, latent, rope_key):
    vmem = pl.BlockSpec(memory_space=pltpu.VMEM)
    return pl.pallas_call(
        spread_kernel,
        out_shape=jax.ShapeDtypeStruct((NZ, SPAN // NZ, HEADS * DQ + WIDE), jnp.bfloat16),
        in_specs=[vmem] * 3,
        out_specs=vmem,
        compiler_params=pltpu.CompilerParams(vmem_limit_bytes=60 * 1024 * 1024),
        cost_estimate=pl.CostEstimate(flops=1_000_000, bytes_accessed=500_000, transcendentals=0),
    )(queries, latent, rope_key)


def pack_kernel(both_ref, floor_ref, q_ref, kv_ref):
    del floor_ref
    q_ref[...] = both_ref[:, : HEADS * DQ]
    rope = both_ref[:, HEADS * DQ + DL : HEADS * DQ + DL + DR]
    for to in range(NY):
        for j in range(DL // LANES):
            col = HEADS * DQ + j * LANES
            kv_ref[to, j * SPAN : (j + 1) * SPAN] = both_ref[:, col : col + LANES]
        kv_ref[to, PACKED - HALF :, :DR] = rope[:HALF]
        kv_ref[to, PACKED - HALF :, DR:] = rope[HALF:]


def pack(both, floor):
    vmem = pl.BlockSpec(memory_space=pltpu.VMEM)
    return pl.pallas_call(
        pack_kernel,
        out_shape=[
            jax.ShapeDtypeStruct((SPAN, HEADS * DQ), jnp.bfloat16),
            jax.ShapeDtypeStruct((NY, PACKED, LANES), jnp.bfloat16),
        ],
        in_specs=[vmem] + [pl.BlockSpec(memory_space=pl.ANY)],
        out_specs=[vmem] * 2,
        compiler_params=pltpu.CompilerParams(vmem_limit_bytes=8 * 1024 * 1024),
        cost_estimate=pl.CostEstimate(flops=4_000_000_000, bytes_accessed=1_000_000, transcendentals=0),
    )(both, floor)


def fill_keys(keys, kv, first, own_block):
    count = NY * SPAN
    blocks = 2 * count // HALF
    for b in range(NY):
        here = slice(b * SPAN, (b + 1) * SPAN)
        for j in range(DL // LANES):
            keys[here, j * LANES : (j + 1) * LANES] = kv[b, j * SPAN : (j + 1) * SPAN]
        keys[b * SPAN : b * SPAN + HALF, DL : DL + DR] = kv[b, PACKED - HALF :, :DR]
        keys[b * SPAN + HALF : (b + 1) * SPAN, DL : DL + DR] = kv[b, PACKED - HALF :, DR:]
    keys[:, DL + DR : WIDE] = jnp.zeros((count, WIDE - DL - DR), jnp.bfloat16)
    key = lax.broadcasted_iota(jnp.int32, (count, EXTRA), 0)
    col = lax.broadcasted_iota(jnp.int32, (count, EXTRA), 1)
    ones = col == key // HALF + first
    if own_block is not None:
        in_own = (key // HALF == own_block) | (key // HALF == own_block + 1)
        ones = ones | (in_own & (col == blocks + key - own_block * HALF))
    keys[:, WIDE:] = jnp.where(ones, 1.0, 0.0).astype(jnp.bfloat16)


def pair_scores(q_ref, floor, keys, p):
    rows = NX * SPAN
    q = jnp.concatenate(
        [q_ref[2 * p : 2 * p + 2].reshape(2 * rows, WIDE), jnp.concatenate([floor, floor], axis=0)], axis=1
    )
    return lax.dot_general(q, keys[...], (((1,), (1,)), ((), ())), preferred_element_type=jnp.float32)


def pair_values(keys, w_uv, p):
    w = jnp.concatenate([w_uv[2 * p], w_uv[2 * p + 1]], axis=1)
    values = jnp.dot(keys[:, :DL], w, preferred_element_type=jnp.float32).astype(jnp.bfloat16)
    ones = jnp.ones((NY * SPAN, STAT), jnp.bfloat16)
    return [jnp.concatenate([values[:, i * DV : (i + 1) * DV], ones], axis=1) for i in range(2)]


def weigh(weight, values):
    rows = NX * SPAN
    weight = weight.astype(jnp.bfloat16)
    both = [
        jnp.dot(weight[i * rows : (i + 1) * rows], values[i], preferred_element_type=jnp.float32) for i in range(2)
    ]
    return [one[:, :DV] for one in both], [one[:, DV:] for one in both]


def wide(value, count):
    return jnp.concatenate([value] * count, axis=1)


def floors_of(info_ref):
    me = info_ref[0]
    core = me % 2
    x = (me // 2) % NX
    y = me // (2 * NX)
    blocks = 2 * NY * SPAN // HALF
    lane = lax.broadcasted_iota(jnp.int32, (HALF, EXTRA), 1)
    token = lax.broadcasted_iota(jnp.int32, (HALF, EXTRA), 0)
    key_block = jnp.zeros((HALF, EXTRA), jnp.int32)
    for which in range(blocks):
        side_core = core if which < blocks // 2 else 1 - core
        slot = (((which // 2) % NY) * NX + x) * 2 + side_core
        key_block = jnp.where(lane == which, info_ref[1 + 2 * slot + which % 2], key_block)
    floors = []
    for step in range(NX):
        slot = (y * NX + (x - step + NX) % NX) * 2 + core
        for half in range(2):
            ahead = (lane < blocks) & (key_block > info_ref[1 + 2 * slot + half])
            if step == 0:
                own = lane - blocks - half * HALF
                ahead = ahead | ((own >= 0) & (own < HALF) & (own > token))
            floors.append(jnp.where(ahead, FLOOR_SCORE, 0.0))
    return jnp.concatenate(floors, axis=0).astype(jnp.bfloat16)


def floor_kernel(info_ref, floor_ref):
    floor_ref[...] = floors_of(info_ref)


def make_floor(info):
    vmem = pl.BlockSpec(memory_space=pltpu.VMEM)
    smem = pl.BlockSpec(memory_space=pltpu.SMEM)
    return pl.pallas_call(
        floor_kernel,
        out_shape=jax.ShapeDtypeStruct((NX * SPAN, EXTRA), jnp.bfloat16),
        in_specs=[smem],
        out_specs=vmem,
        compiler_params=pltpu.CompilerParams(vmem_limit_bytes=8 * 1024 * 1024),
        cost_estimate=pl.CostEstimate(flops=4_000_000_000, bytes_accessed=500_000, transcendentals=0),
    )(info)


def own_kernel(place_ref, q0, q3, q2, q1, w_uk, w_uv, kv, floor_ref, q_ref, sum_ref, top_ref, total_ref, keys):
    rows = NX * SPAN
    floor = floor_ref[...]
    none = jnp.zeros((rows, WIDE - DL - DR), jnp.bfloat16)

    def fill_queries(h):
        here = slice(h * DQ, (h + 1) * DQ)
        q = jnp.concatenate([q0[:, here], q1[:, here], q2[:, here], q3[:, here]], axis=0)
        q_lat = lax.dot_general(
            q[:, :DN], w_uk[h], (((1,), (1,)), ((), ())), preferred_element_type=jnp.float32
        )
        q_ref[h, :, :DL] = q_lat.astype(jnp.bfloat16)
        q_ref[h, :, DL : DL + DR] = q[:, DN:]
        q_ref[h, :, DL + DR : WIDE] = none

    fill_queries(0)
    fill_queries(1)
    fill_keys(keys, kv, 0, place_ref[0] // (2 * NX) * 2)
    ahead = pair_scores(q_ref, floor, keys, 0)
    for p in range(HEADS // 2):
        s = ahead
        values = pair_values(keys, w_uv, p)
        if p + 1 < HEADS // 2:
            fill_queries(2 * p + 2)
            fill_queries(2 * p + 3)
            ahead = pair_scores(q_ref, floor, keys, p + 1)
        top = jnp.max(s, axis=1, keepdims=True)
        weight = jnp.exp2((s - top) * SCALE2)
        sums, totals = weigh(weight, values)
        for i in range(2):
            sum_ref[2 * p + i] = sums[i]
            total_ref[2 * p + i] = totals[i]
        pair = slice(2 * p, 2 * p + 2)
        top_ref[pair] = jnp.broadcast_to(top, (2 * rows, STAT)).reshape(2, rows, STAT)


def attend_own(place, qs, w_uk, w_uv, kv, floor):
    vmem = pl.BlockSpec(memory_space=pltpu.VMEM)
    smem = pl.BlockSpec(memory_space=pltpu.SMEM)
    rows = NX * SPAN
    return pl.pallas_call(
        own_kernel,
        out_shape=[
            jax.ShapeDtypeStruct((HEADS, rows, WIDE), jnp.bfloat16),
            jax.ShapeDtypeStruct((HEADS, rows, DV), jnp.float32),
            jax.ShapeDtypeStruct((HEADS, rows, STAT), jnp.float32),
            jax.ShapeDtypeStruct((HEADS, rows, STAT), jnp.float32),
        ],
        in_specs=[smem] + [vmem] * 8,
        out_specs=[vmem] * 4,
        scratch_shapes=[pltpu.VMEM((NY * SPAN, WIDE + EXTRA), jnp.bfloat16)],
        compiler_params=pltpu.CompilerParams(vmem_limit_bytes=20 * 1024 * 1024),
        cost_estimate=pl.CostEstimate(flops=6_000_000_000, bytes_accessed=5_000_000, transcendentals=1_000_000),
    )(place, qs[0], qs[3], qs[2], qs[1], w_uk, w_uv, kv, floor)


def other_kernel(place_ref, q_ref, floor_ref, kv, sum_ref, top_ref, total_ref, w_uv, out_ref, keys):
    x = (place_ref[0] // 2) % NX
    rows = NX * SPAN
    floor = floor_ref[...]
    fill_keys(keys, kv, NY * SPAN // HALF, None)
    lanes = lax.broadcasted_iota(jnp.int32, (rows, STAT), 1)
    level = jnp.zeros((rows, STAT), jnp.float32)
    ahead = pair_scores(q_ref, floor, keys, 0)
    for p in range(HEADS // 2):
        s = ahead
        values = pair_values(keys, w_uv, p)
        if p + 1 < HEADS // 2:
            ahead = pair_scores(q_ref, floor, keys, p + 1)
        pair = slice(2 * p, 2 * p + 2)
        old_top = top_ref[pair].reshape(2 * rows, STAT)
        top = jnp.maximum(old_top, jnp.max(s, axis=1, keepdims=True))
        shrink = jnp.exp2((old_top - top) * SCALE2)
        weight = jnp.exp2((s - wide(top, NY * SPAN // STAT)) * SCALE2)
        sums, totals = weigh(weight, values)
        for i in range(2):
            h = 2 * p + i
            mine = slice(i * rows, (i + 1) * rows)
            total = totals[i] + total_ref[h] * shrink[mine]
            value = ((sums[i] + sum_ref[h] * shrink[mine]) * (1.0 / total)).astype(jnp.bfloat16)
            for step in range(NX):
                to = (x + NX - step) % NX
                out_ref[to, :, h * DV : (h + 1) * DV] = value[step * SPAN : (step + 1) * SPAN]
            level = jnp.where(lanes % HEADS == h, top[mine] * SCALE2 + jnp.log2(total), level)
    high = level.astype(jnp.bfloat16)
    rest = level - high.astype(jnp.float32)
    middle = rest.astype(jnp.bfloat16)
    low = (rest - middle.astype(jnp.float32)).astype(jnp.bfloat16)
    part = lanes // HEADS
    packed = jnp.where(
        part == 0,
        high.astype(jnp.float32),
        jnp.where(part == 1, middle.astype(jnp.float32), jnp.where(part == 2, low.astype(jnp.float32), 0.0)),
    ).astype(jnp.bfloat16)
    for step in range(NX):
        to = (x + NX - step) % NX
        out_ref[to, :, HEADS * DV :] = packed[step * SPAN : (step + 1) * SPAN]


def attend_other(place, q_all, floor, kv, state, w_uv):
    vmem = pl.BlockSpec(memory_space=pltpu.VMEM)
    smem = pl.BlockSpec(memory_space=pltpu.SMEM)
    rows = NX * SPAN
    return pl.pallas_call(
        other_kernel,
        out_shape=jax.ShapeDtypeStruct((NX, SPAN, HEADS * DV + STAT), jnp.bfloat16),
        in_specs=[smem] + [vmem] * 7,
        out_specs=vmem,
        scratch_shapes=[pltpu.VMEM((NY * SPAN, WIDE + EXTRA), jnp.bfloat16)],
        compiler_params=pltpu.CompilerParams(vmem_limit_bytes=20 * 1024 * 1024),
        cost_estimate=pl.CostEstimate(flops=4_000_000_000, bytes_accessed=5_000_000, transcendentals=1_000_000),
    )(place, q_all, floor, kv, *state, w_uv)


def merge_kernel(p_ref, out_ref, held, sems):
    levels = []
    for x in range(NX):
        pieces = p_ref[x, :, :, HEADS * DV :].astype(jnp.float32).reshape(SPAN, STAT)
        rest = pltpu.roll(pieces, STAT - HEADS, 1) + pltpu.roll(pieces, STAT - 2 * HEADS, 1)
        levels.append(pieces + rest)
    top = functools.reduce(jnp.maximum, levels)
    shares = [jnp.exp2(level - top) for level in levels]
    whole = functools.reduce(jnp.add, shares)
    shares = [share / whole for share in shares]
    lane = lax.broadcasted_iota(jnp.int32, (STAT, HEADS * DV), 0)
    col = lax.broadcasted_iota(jnp.int32, (STAT, HEADS * DV), 1)
    spread_ones = jnp.where(col // DV == lane, 1.0, 0.0).astype(jnp.bfloat16)
    share = jnp.concatenate(shares, axis=0)
    high = share.astype(jnp.bfloat16)
    rest = share - high.astype(jnp.float32)
    middle = rest.astype(jnp.bfloat16)
    low = (rest - middle.astype(jnp.float32)).astype(jnp.bfloat16)
    pieces = jnp.concatenate([high, middle, low], axis=0)
    broad = jnp.dot(pieces, spread_ones, preferred_element_type=jnp.float32)
    count = NX * SPAN
    broad = broad[:count] + broad[count : 2 * count] + broad[2 * count :]
    tokens = SPAN // NZ
    moves = []
    for z in range(NZ):
        acc = jnp.zeros((tokens, HEADS * DV), jnp.float32)
        for x in range(NX):
            here = slice(x * SPAN + z * tokens, x * SPAN + (z + 1) * tokens)
            acc = acc + broad[here] * p_ref[x, z, :, : HEADS * DV].astype(jnp.float32)
        cols = slice(z * HEADS * DV, (z + 1) * HEADS * DV)
        held[:, cols] = acc.astype(jnp.bfloat16)
        moves.append(pltpu.make_async_copy(held.at[:, cols], out_ref.at[:, cols], sems.at[z]))
        moves[-1].start()
    for move in moves:
        move.wait()


def merge(parts):
    vmem = pl.BlockSpec(memory_space=pltpu.VMEM)
    return pl.pallas_call(
        merge_kernel,
        out_shape=jax.ShapeDtypeStruct((SPAN // NZ, NZ * HEADS * DV), jnp.bfloat16),
        in_specs=[vmem],
        out_specs=pl.BlockSpec(memory_space=pl.ANY),
        scratch_shapes=[
            pltpu.VMEM((SPAN // NZ, NZ * HEADS * DV), jnp.bfloat16),
            pltpu.SemaphoreType.DMA((NZ,)),
        ],
        compiler_params=pltpu.CompilerParams(vmem_limit_bytes=8 * 1024 * 1024),
        cost_estimate=pl.CostEstimate(flops=1_000_000, bytes_accessed=800_000, transcendentals=2000),
    )(parts)


def on_device(queries, latent, rope_key, w_uk, w_uv, block_order):
    place = lax.axis_index(CTX).astype(jnp.int32).reshape(1)
    floor = make_floor(jnp.concatenate([place, block_order]))
    both = spread(queries, latent, rope_key)
    both = lax.all_to_all(both, "z", split_axis=0, concat_axis=0, tiled=True).reshape(SPAN, HEADS * DQ + WIDE)
    q_own, kv = pack(both, floor)
    kv_own = lax.all_to_all(kv, "y", split_axis=0, concat_axis=0, tiled=True)
    kv_sib = lax.ppermute(kv_own, "core", CORE_SWAP)
    qs = [q_own] + [lax.ppermute(q_own, "x", along_x(step)) for step in range(1, NX)]
    q_all, *state = attend_own(place, qs, w_uk, w_uv, kv_own, floor)
    partial = attend_other(place, q_all, floor, kv_sib, state, w_uv)
    rows = SPAN // NZ
    partial = partial.reshape(NX * NZ, rows, HEADS * DV + STAT)
    parts = lax.all_to_all(partial, ("x", "z"), split_axis=0, concat_axis=0, tiled=True)
    return merge(parts.reshape(NX, NZ, rows, HEADS * DV + STAT))


def solution(mesh):
    fine = jax.sharding.Mesh(mesh.devices.reshape(NY, NX, 2, NZ), ("y", "x", "core", "z"))
    tokens = P(("y", "x", "core", "z"), None)
    in_specs = (tokens, tokens, tokens, P("z", None, None), P("z", None, None), P())
    return jax.shard_map(on_device, mesh=fine, in_specs=in_specs, out_specs=tokens, check_vma=False)
```

```python
import functools

import jax
import jax.numpy as jnp
from jax import lax
from jax.experimental import pallas as pl
from jax.experimental.pallas import tpu as pltpu
from jax.sharding import PartitionSpec as P

HALF = 32
DL = 512
DR = 64
DN = 128
DV = 128
DQ = DN + DR
WIDE = 640
STAT = 128
EXTRA = 128
NX = 4
NY = 8
NZ = 8
HEADS = 8
SPAN = 64
LANES = 128
PACKED = DL // LANES * SPAN + HALF
FLOOR_SCORE = -1e30
LOG2E = 1.4426950408889634
SCALE2 = DQ ** (-0.5) * LOG2E


def along_x(step):
    return [(x, (x + step) % NX) for x in range(NX)]


CORE_SWAP = [(0, 1), (1, 0)]
CTX = ("y", "x", "core")


def spread_kernel(q_ref, lat_ref, rope_ref, out_ref):
    end = HEADS * DQ
    for z in range(NZ):
        out_ref[z, :, :end] = q_ref[:, z * end : (z + 1) * end]
        out_ref[z, :, end : end + DL] = lat_ref[...]
        out_ref[z, :, end + DL : end + DL + DR] = rope_ref[...]
        out_ref[z, :, end + DL + DR :] = jnp.zeros_like(rope_ref)


def spread(queries, latent, rope_key):
    vmem = pl.BlockSpec(memory_space=pltpu.VMEM)
    return pl.pallas_call(
        spread_kernel,
        out_shape=jax.ShapeDtypeStruct((NZ, SPAN // NZ, HEADS * DQ + WIDE), jnp.bfloat16),
        in_specs=[vmem] * 3,
        out_specs=vmem,
        compiler_params=pltpu.CompilerParams(vmem_limit_bytes=60 * 1024 * 1024),
        cost_estimate=pl.CostEstimate(flops=1_000_000, bytes_accessed=500_000, transcendentals=0),
    )(queries, latent, rope_key)


def pack_kernel(both_ref, floor_ref, q_ref, kv_ref):
    del floor_ref
    q_ref[...] = both_ref[:, : HEADS * DQ]
    rope = both_ref[:, HEADS * DQ + DL : HEADS * DQ + DL + DR]
    for to in range(NY):
        for j in range(DL // LANES):
            col = HEADS * DQ + j * LANES
            kv_ref[to, j * SPAN : (j + 1) * SPAN] = both_ref[:, col : col + LANES]
        kv_ref[to, PACKED - HALF :, :DR] = rope[:HALF]
        kv_ref[to, PACKED - HALF :, DR:] = rope[HALF:]


def pack(both, floor):
    vmem = pl.BlockSpec(memory_space=pltpu.VMEM)
    return pl.pallas_call(
        pack_kernel,
        out_shape=[
            jax.ShapeDtypeStruct((SPAN, HEADS * DQ), jnp.bfloat16),
            jax.ShapeDtypeStruct((NY, PACKED, LANES), jnp.bfloat16),
        ],
        in_specs=[vmem] + [pl.BlockSpec(memory_space=pl.ANY)],
        out_specs=[vmem] * 2,
        compiler_params=pltpu.CompilerParams(vmem_limit_bytes=8 * 1024 * 1024),
        cost_estimate=pl.CostEstimate(flops=4_000_000_000, bytes_accessed=1_000_000, transcendentals=0),
    )(both, floor)


def fill_keys(keys, kv, first, own_block):
    count = NY * SPAN
    blocks = 2 * count // HALF
    for b in range(NY):
        here = slice(b * SPAN, (b + 1) * SPAN)
        for j in range(DL // LANES):
            keys[here, j * LANES : (j + 1) * LANES] = kv[b, j * SPAN : (j + 1) * SPAN]
        keys[b * SPAN : b * SPAN + HALF, DL : DL + DR] = kv[b, PACKED - HALF :, :DR]
        keys[b * SPAN + HALF : (b + 1) * SPAN, DL : DL + DR] = kv[b, PACKED - HALF :, DR:]
    keys[:, DL + DR : WIDE] = jnp.zeros((count, WIDE - DL - DR), jnp.bfloat16)
    lane = lax.broadcasted_iota(jnp.int32, (HALF, EXTRA), 1)
    for block in range(count // HALF):
        ones = jnp.where(lane == block + first, 1.0, 0.0).astype(jnp.bfloat16)
        keys[block * HALF : (block + 1) * HALF, WIDE:] = ones
    if own_block is not None:
        row = lax.broadcasted_iota(jnp.int32, (HALF, EXTRA), 0)
        for half in range(2):
            block = own_block + half
            here = (lane == block + first) | (lane == blocks + half * HALF + row)
            rows = pl.ds(pl.multiple_of(block * HALF, HALF), HALF)
            keys[rows, WIDE:] = jnp.where(here, 1.0, 0.0).astype(jnp.bfloat16)


def pair_scores(q_ref, floor, keys, p):
    rows = NX * SPAN
    q = jnp.concatenate(
        [q_ref[2 * p : 2 * p + 2].reshape(2 * rows, WIDE), jnp.concatenate([floor, floor], axis=0)], axis=1
    )
    return lax.dot_general(q, keys[...], (((1,), (1,)), ((), ())), preferred_element_type=jnp.float32)


def pair_values(keys, w_uv, p):
    w = jnp.concatenate([w_uv[2 * p], w_uv[2 * p + 1]], axis=1)
    values = jnp.dot(keys[:, :DL], w, preferred_element_type=jnp.float32).astype(jnp.bfloat16)
    ones = jnp.ones((NY * SPAN, STAT), jnp.bfloat16)
    return [jnp.concatenate([values[:, i * DV : (i + 1) * DV], ones], axis=1) for i in range(2)]


def weigh(weight, values):
    rows = NX * SPAN
    weight = weight.astype(jnp.bfloat16)
    both = [
        jnp.dot(weight[i * rows : (i + 1) * rows], values[i], preferred_element_type=jnp.float32) for i in range(2)
    ]
    return [one[:, :DV] for one in both], [one[:, DV:] for one in both]


def wide(value, count):
    return jnp.concatenate([value] * count, axis=1)


def floors_of(info_ref):
    me = info_ref[0]
    core = me % 2
    x = (me // 2) % NX
    y = me // (2 * NX)
    blocks = 2 * NY * SPAN // HALF
    lane = lax.broadcasted_iota(jnp.int32, (HALF, EXTRA), 1)
    token = lax.broadcasted_iota(jnp.int32, (HALF, EXTRA), 0)
    key_block = jnp.zeros((HALF, EXTRA), jnp.int32)
    for which in range(blocks):
        side_core = core if which < blocks // 2 else 1 - core
        slot = (((which // 2) % NY) * NX + x) * 2 + side_core
        key_block = jnp.where(lane == which, info_ref[1 + 2 * slot + which % 2], key_block)
    floors = []
    for step in range(NX):
        slot = (y * NX + (x - step + NX) % NX) * 2 + core
        for half in range(2):
            ahead = (lane < blocks) & (key_block > info_ref[1 + 2 * slot + half])
            if step == 0:
                own = lane - blocks - half * HALF
                ahead = ahead | ((own >= 0) & (own < HALF) & (own > token))
            floors.append(jnp.where(ahead, FLOOR_SCORE, 0.0))
    return jnp.concatenate(floors, axis=0).astype(jnp.bfloat16)


def floor_kernel(info_ref, floor_ref):
    floor_ref[...] = floors_of(info_ref)


def make_floor(info):
    vmem = pl.BlockSpec(memory_space=pltpu.VMEM)
    smem = pl.BlockSpec(memory_space=pltpu.SMEM)
    return pl.pallas_call(
        floor_kernel,
        out_shape=jax.ShapeDtypeStruct((NX * SPAN, EXTRA), jnp.bfloat16),
        in_specs=[smem],
        out_specs=vmem,
        compiler_params=pltpu.CompilerParams(vmem_limit_bytes=8 * 1024 * 1024),
        cost_estimate=pl.CostEstimate(flops=4_000_000_000, bytes_accessed=500_000, transcendentals=0),
    )(info)


def own_kernel(place_ref, q0, q1, q2, q3, w_uk, w_uv, kv, floor_ref, q_ref, sum_ref, top_ref, total_ref, keys):
    rows = NX * SPAN
    floor = floor_ref[...]
    none = jnp.zeros((rows, WIDE - DL - DR), jnp.bfloat16)

    def fill_queries(h):
        here = slice(h * DQ, (h + 1) * DQ)
        q = jnp.concatenate([q0[:, here], q1[:, here], q2[:, here], q3[:, here]], axis=0)
        q_lat = lax.dot_general(
            q[:, :DN], w_uk[h], (((1,), (1,)), ((), ())), preferred_element_type=jnp.float32
        )
        q_ref[h, :, :DL] = q_lat.astype(jnp.bfloat16)
        q_ref[h, :, DL : DL + DR] = q[:, DN:]
        q_ref[h, :, DL + DR : WIDE] = none

    fill_queries(0)
    fill_queries(1)
    fill_keys(keys, kv, 0, place_ref[0] // (2 * NX) * 2)
    ahead = pair_scores(q_ref, floor, keys, 0)
    for p in range(HEADS // 2):
        s = ahead
        values = pair_values(keys, w_uv, p)
        if p + 1 < HEADS // 2:
            fill_queries(2 * p + 2)
            fill_queries(2 * p + 3)
            ahead = pair_scores(q_ref, floor, keys, p + 1)
        top = jnp.max(s, axis=1, keepdims=True)
        weight = jnp.exp2((s - top) * SCALE2)
        sums, totals = weigh(weight, values)
        for i in range(2):
            sum_ref[2 * p + i] = sums[i]
            total_ref[2 * p + i] = totals[i]
        pair = slice(2 * p, 2 * p + 2)
        top_ref[pair] = jnp.broadcast_to(top, (2 * rows, STAT)).reshape(2, rows, STAT)


def attend_own(place, qs, w_uk, w_uv, kv, floor):
    vmem = pl.BlockSpec(memory_space=pltpu.VMEM)
    smem = pl.BlockSpec(memory_space=pltpu.SMEM)
    rows = NX * SPAN
    return pl.pallas_call(
        own_kernel,
        out_shape=[
            jax.ShapeDtypeStruct((HEADS, rows, WIDE), jnp.bfloat16),
            jax.ShapeDtypeStruct((HEADS, rows, DV), jnp.float32),
            jax.ShapeDtypeStruct((HEADS, rows, STAT), jnp.float32),
            jax.ShapeDtypeStruct((HEADS, rows, STAT), jnp.float32),
        ],
        in_specs=[smem] + [vmem] * 8,
        out_specs=[vmem] * 4,
        scratch_shapes=[pltpu.VMEM((NY * SPAN, WIDE + EXTRA), jnp.bfloat16)],
        compiler_params=pltpu.CompilerParams(vmem_limit_bytes=20 * 1024 * 1024),
        cost_estimate=pl.CostEstimate(flops=6_000_000_000, bytes_accessed=5_000_000, transcendentals=1_000_000),
    )(place, *qs, w_uk, w_uv, kv, floor)


def other_kernel(place_ref, q_ref, floor_ref, kv, sum_ref, top_ref, total_ref, w_uv, out_ref, keys):
    x = (place_ref[0] // 2) % NX
    rows = NX * SPAN
    floor = floor_ref[...]
    fill_keys(keys, kv, NY * SPAN // HALF, None)
    lanes = lax.broadcasted_iota(jnp.int32, (rows, STAT), 1)
    level = jnp.zeros((rows, STAT), jnp.float32)
    ahead = pair_scores(q_ref, floor, keys, 0)
    for p in range(HEADS // 2):
        s = ahead
        values = pair_values(keys, w_uv, p)
        if p + 1 < HEADS // 2:
            ahead = pair_scores(q_ref, floor, keys, p + 1)
        pair = slice(2 * p, 2 * p + 2)
        old_top = top_ref[pair].reshape(2 * rows, STAT)
        top = jnp.maximum(old_top, jnp.max(s, axis=1, keepdims=True))
        shrink = jnp.exp2((old_top - top) * SCALE2)
        weight = jnp.exp2((s - wide(top, NY * SPAN // STAT)) * SCALE2)
        sums, totals = weigh(weight, values)
        for i in range(2):
            h = 2 * p + i
            mine = slice(i * rows, (i + 1) * rows)
            total = totals[i] + total_ref[h] * shrink[mine]
            value = ((sums[i] + sum_ref[h] * shrink[mine]) * (1.0 / total)).astype(jnp.bfloat16)
            for step in range(NX):
                to = (x + NX - step) % NX
                out_ref[to, :, h * DV : (h + 1) * DV] = value[step * SPAN : (step + 1) * SPAN]
            level = jnp.where(lanes % HEADS == h, top[mine] * SCALE2 + jnp.log2(total), level)
    high = level.astype(jnp.bfloat16)
    rest = level - high.astype(jnp.float32)
    middle = rest.astype(jnp.bfloat16)
    low = (rest - middle.astype(jnp.float32)).astype(jnp.bfloat16)
    part = lanes // HEADS
    packed = jnp.where(
        part == 0,
        high.astype(jnp.float32),
        jnp.where(part == 1, middle.astype(jnp.float32), jnp.where(part == 2, low.astype(jnp.float32), 0.0)),
    ).astype(jnp.bfloat16)
    for step in range(NX):
        to = (x + NX - step) % NX
        out_ref[to, :, HEADS * DV :] = packed[step * SPAN : (step + 1) * SPAN]


def attend_other(place, q_all, floor, kv, state, w_uv):
    vmem = pl.BlockSpec(memory_space=pltpu.VMEM)
    smem = pl.BlockSpec(memory_space=pltpu.SMEM)
    rows = NX * SPAN
    return pl.pallas_call(
        other_kernel,
        out_shape=jax.ShapeDtypeStruct((NX, SPAN, HEADS * DV + STAT), jnp.bfloat16),
        in_specs=[smem] + [vmem] * 7,
        out_specs=vmem,
        scratch_shapes=[pltpu.VMEM((NY * SPAN, WIDE + EXTRA), jnp.bfloat16)],
        compiler_params=pltpu.CompilerParams(vmem_limit_bytes=20 * 1024 * 1024),
        cost_estimate=pl.CostEstimate(flops=4_000_000_000, bytes_accessed=5_000_000, transcendentals=1_000_000),
    )(place, q_all, floor, kv, *state, w_uv)


def merge_kernel(p_ref, out_ref, held, sems):
    levels = []
    for x in range(NX):
        pieces = p_ref[x, :, :, HEADS * DV :].astype(jnp.float32).reshape(SPAN, STAT)
        rest = pltpu.roll(pieces, STAT - HEADS, 1) + pltpu.roll(pieces, STAT - 2 * HEADS, 1)
        levels.append(pieces + rest)
    top = functools.reduce(jnp.maximum, levels)
    shares = [jnp.exp2(level - top) for level in levels]
    whole = functools.reduce(jnp.add, shares)
    shares = [share / whole for share in shares]
    tokens = SPAN // NZ
    moves = []
    for z in range(NZ):
        here = slice(z * tokens, (z + 1) * tokens)
        for h in range(HEADS):
            acc = jnp.zeros((tokens, DV), jnp.float32)
            for x in range(NX):
                acc = acc + shares[x][here, h : h + 1] * p_ref[x, z, :, h * DV : (h + 1) * DV].astype(jnp.float32)
            held[:, (z * HEADS + h) * DV : (z * HEADS + h + 1) * DV] = acc.astype(jnp.bfloat16)
        cols = slice(z * HEADS * DV, (z + 1) * HEADS * DV)
        moves.append(pltpu.make_async_copy(held.at[:, cols], out_ref.at[:, cols], sems.at[z]))
        moves[-1].start()
    for move in moves:
        move.wait()


def merge(parts):
    vmem = pl.BlockSpec(memory_space=pltpu.VMEM)
    return pl.pallas_call(
        merge_kernel,
        out_shape=jax.ShapeDtypeStruct((SPAN // NZ, NZ * HEADS * DV), jnp.bfloat16),
        in_specs=[vmem],
        out_specs=pl.BlockSpec(memory_space=pl.ANY),
        scratch_shapes=[
            pltpu.VMEM((SPAN // NZ, NZ * HEADS * DV), jnp.bfloat16),
            pltpu.SemaphoreType.DMA((NZ,)),
        ],
        compiler_params=pltpu.CompilerParams(vmem_limit_bytes=8 * 1024 * 1024),
        cost_estimate=pl.CostEstimate(flops=1_000_000, bytes_accessed=800_000, transcendentals=2000),
    )(parts)


def on_device(queries, latent, rope_key, w_uk, w_uv, block_order):
    place = lax.axis_index(CTX).astype(jnp.int32).reshape(1)
    floor = make_floor(jnp.concatenate([place, block_order]))
    both = spread(queries, latent, rope_key)
    both = lax.all_to_all(both, "z", split_axis=0, concat_axis=0, tiled=True).reshape(SPAN, HEADS * DQ + WIDE)
    q_own, kv = pack(both, floor)
    kv_own = lax.all_to_all(kv, "y", split_axis=0, concat_axis=0, tiled=True)
    kv_sib = lax.ppermute(kv_own, "core", CORE_SWAP)
    qs = [q_own] + [lax.ppermute(q_own, "x", along_x(step)) for step in range(1, NX)]
    q_all, *state = attend_own(place, qs, w_uk, w_uv, kv_own, floor)
    partial = attend_other(place, q_all, floor, kv_sib, state, w_uv)
    rows = SPAN // NZ
    partial = partial.reshape(NX * NZ, rows, HEADS * DV + STAT)
    parts = lax.all_to_all(partial, ("x", "z"), split_axis=0, concat_axis=0, tiled=True)
    return merge(parts.reshape(NX, NZ, rows, HEADS * DV + STAT))


def solution(mesh):
    fine = jax.sharding.Mesh(mesh.devices.reshape(NY, NX, 2, NZ), ("y", "x", "core", "z"))
    tokens = P(("y", "x", "core", "z"), None)
    in_specs = (tokens, tokens, tokens, P("z", None, None), P("z", None, None), P())
    return jax.shard_map(on_device, mesh=fine, in_specs=in_specs, out_specs=tokens, check_vma=False)
```

```python
import functools

import jax
import jax.numpy as jnp
from jax import lax
from jax.experimental import pallas as pl
from jax.experimental.pallas import tpu as pltpu
from jax.sharding import PartitionSpec as P

HALF = 32
DL = 512
DR = 64
DN = 128
DV = 128
DQ = DN + DR
WIDE = 640
STAT = 128
EXTRA = 128
NX = 4
NY = 8
NZ = 8
HEADS = 8
SPAN = 64
LANES = 128
PACKED = DL // LANES * SPAN + HALF
FLOOR_SCORE = -1e30
LOG2E = 1.4426950408889634
SCALE2 = DQ ** (-0.5) * LOG2E


def along_x(step):
    return [(x, (x + step) % NX) for x in range(NX)]


CORE_SWAP = [(0, 1), (1, 0)]
CTX = ("y", "x", "core")


def spread_kernel(q_ref, lat_ref, rope_ref, out_ref):
    end = HEADS * DQ
    for z in range(NZ):
        out_ref[z, :, :end] = q_ref[:, z * end : (z + 1) * end]
        out_ref[z, :, end : end + DL] = lat_ref[...]
        out_ref[z, :, end + DL : end + DL + DR] = rope_ref[...]
        out_ref[z, :, end + DL + DR :] = jnp.zeros_like(rope_ref)


def spread(queries, latent, rope_key):
    vmem = pl.BlockSpec(memory_space=pltpu.VMEM)
    return pl.pallas_call(
        spread_kernel,
        out_shape=jax.ShapeDtypeStruct((NZ, SPAN // NZ, HEADS * DQ + WIDE), jnp.bfloat16),
        in_specs=[vmem] * 3,
        out_specs=vmem,
        compiler_params=pltpu.CompilerParams(vmem_limit_bytes=60 * 1024 * 1024),
        cost_estimate=pl.CostEstimate(flops=1_000_000, bytes_accessed=500_000, transcendentals=0),
    )(queries, latent, rope_key)


def pack_kernel(both_ref, floor_ref, q_ref, kv_ref):
    del floor_ref
    q_ref[...] = both_ref[:, : HEADS * DQ]
    rope = both_ref[:, HEADS * DQ + DL : HEADS * DQ + DL + DR]
    for to in range(NY):
        for j in range(DL // LANES):
            col = HEADS * DQ + j * LANES
            kv_ref[to, j * SPAN : (j + 1) * SPAN] = both_ref[:, col : col + LANES]
        kv_ref[to, PACKED - HALF :, :DR] = rope[:HALF]
        kv_ref[to, PACKED - HALF :, DR:] = rope[HALF:]


def pack(both, floor):
    vmem = pl.BlockSpec(memory_space=pltpu.VMEM)
    return pl.pallas_call(
        pack_kernel,
        out_shape=[
            jax.ShapeDtypeStruct((SPAN, HEADS * DQ), jnp.bfloat16),
            jax.ShapeDtypeStruct((NY, PACKED, LANES), jnp.bfloat16),
        ],
        in_specs=[vmem] + [pl.BlockSpec(memory_space=pl.ANY)],
        out_specs=[vmem] * 2,
        compiler_params=pltpu.CompilerParams(vmem_limit_bytes=8 * 1024 * 1024),
        cost_estimate=pl.CostEstimate(flops=4_000_000_000, bytes_accessed=1_000_000, transcendentals=0),
    )(both, floor)


def fill_keys(keys, kv, first, own_block):
    count = NY * SPAN
    blocks = 2 * count // HALF
    for b in range(NY):
        here = slice(b * SPAN, (b + 1) * SPAN)
        for j in range(DL // LANES):
            keys[here, j * LANES : (j + 1) * LANES] = kv[b, j * SPAN : (j + 1) * SPAN]
        keys[b * SPAN : b * SPAN + HALF, DL : DL + DR] = kv[b, PACKED - HALF :, :DR]
        keys[b * SPAN + HALF : (b + 1) * SPAN, DL : DL + DR] = kv[b, PACKED - HALF :, DR:]
    keys[:, DL + DR : WIDE] = jnp.zeros((count, WIDE - DL - DR), jnp.bfloat16)
    key = lax.broadcasted_iota(jnp.int32, (count, EXTRA), 0)
    col = lax.broadcasted_iota(jnp.int32, (count, EXTRA), 1)
    ones = col == key // HALF + first
    if own_block is not None:
        in_own = (key // HALF == own_block) | (key // HALF == own_block + 1)
        ones = ones | (in_own & (col == blocks + key - own_block * HALF))
    keys[:, WIDE:] = jnp.where(ones, 1.0, 0.0).astype(jnp.bfloat16)


def pair_scores(q_ref, floor, keys, p):
    rows = NX * SPAN
    q = jnp.concatenate(
        [q_ref[pl.ds(2 * p, 2)].reshape(2 * rows, WIDE), jnp.concatenate([floor, floor], axis=0)], axis=1
    )
    return lax.dot_general(q, keys[...], (((1,), (1,)), ((), ())), preferred_element_type=jnp.float32)


def pair_values(keys, w_uv, p):
    w = jnp.concatenate([w_uv[2 * p], w_uv[2 * p + 1]], axis=1)
    values = jnp.dot(keys[:, :DL], w, preferred_element_type=jnp.float32).astype(jnp.bfloat16)
    ones = jnp.ones((NY * SPAN, STAT), jnp.bfloat16)
    return [jnp.concatenate([values[:, i * DV : (i + 1) * DV], ones], axis=1) for i in range(2)]


def weigh(weight, values):
    rows = NX * SPAN
    weight = weight.astype(jnp.bfloat16)
    both = [
        jnp.dot(weight[i * rows : (i + 1) * rows], values[i], preferred_element_type=jnp.float32) for i in range(2)
    ]
    return [one[:, :DV] for one in both], [one[:, DV:] for one in both]


def wide(value, count):
    return jnp.concatenate([value] * count, axis=1)


def floors_of(info_ref):
    me = info_ref[0]
    core = me % 2
    x = (me // 2) % NX
    y = me // (2 * NX)
    blocks = 2 * NY * SPAN // HALF
    lane = lax.broadcasted_iota(jnp.int32, (HALF, EXTRA), 1)
    token = lax.broadcasted_iota(jnp.int32, (HALF, EXTRA), 0)
    key_block = jnp.zeros((HALF, EXTRA), jnp.int32)
    for which in range(blocks):
        side_core = core if which < blocks // 2 else 1 - core
        slot = (((which // 2) % NY) * NX + x) * 2 + side_core
        key_block = jnp.where(lane == which, info_ref[1 + 2 * slot + which % 2], key_block)
    floors = []
    for step in range(NX):
        slot = (y * NX + (x - step + NX) % NX) * 2 + core
        for half in range(2):
            ahead = (lane < blocks) & (key_block > info_ref[1 + 2 * slot + half])
            if step == 0:
                own = lane - blocks - half * HALF
                ahead = ahead | ((own >= 0) & (own < HALF) & (own > token))
            floors.append(jnp.where(ahead, FLOOR_SCORE, 0.0))
    return jnp.concatenate(floors, axis=0).astype(jnp.bfloat16)


def floor_kernel(info_ref, floor_ref):
    floor_ref[...] = floors_of(info_ref)


def make_floor(info):
    vmem = pl.BlockSpec(memory_space=pltpu.VMEM)
    smem = pl.BlockSpec(memory_space=pltpu.SMEM)
    return pl.pallas_call(
        floor_kernel,
        out_shape=jax.ShapeDtypeStruct((NX * SPAN, EXTRA), jnp.bfloat16),
        in_specs=[smem],
        out_specs=vmem,
        compiler_params=pltpu.CompilerParams(vmem_limit_bytes=8 * 1024 * 1024),
        cost_estimate=pl.CostEstimate(flops=4_000_000_000, bytes_accessed=500_000, transcendentals=0),
    )(info)


def own_kernel(place_ref, q0, q1, q2, q3, w_uk, w_uv, kv, floor_ref, q_ref, sum_ref, top_ref, total_ref, keys):
    rows = NX * SPAN
    floor = floor_ref[...]
    none = jnp.zeros((rows, WIDE - DL - DR), jnp.bfloat16)

    def fill_queries(h):
        here = slice(h * DQ, (h + 1) * DQ)
        q = jnp.concatenate([q0[:, here], q1[:, here], q2[:, here], q3[:, here]], axis=0)
        q_lat = lax.dot_general(
            q[:, :DN], w_uk[h], (((1,), (1,)), ((), ())), preferred_element_type=jnp.float32
        )
        q_ref[h, :, :DL] = q_lat.astype(jnp.bfloat16)
        q_ref[h, :, DL : DL + DR] = q[:, DN:]
        q_ref[h, :, DL + DR : WIDE] = none

    for h in range(HEADS):
        fill_queries(h)
    fill_keys(keys, kv, 0, place_ref[0] // (2 * NX) * 2)

    def step(i, carry):
        scores = [pair_scores(q_ref, floor, keys, 2 * i + j) for j in range(2)]
        for j, s in enumerate(scores):
            p = 2 * i + j
            values = pair_values(keys, w_uv, p)
            top = jnp.max(s, axis=1, keepdims=True)
            weight = jnp.exp2((s - top) * SCALE2)
            sums, totals = weigh(weight, values)
            for k in range(2):
                sum_ref[2 * p + k] = sums[k]
                total_ref[2 * p + k] = totals[k]
            top_ref[pl.ds(2 * p, 2)] = jnp.broadcast_to(top, (2 * rows, STAT)).reshape(2, rows, STAT)
        return carry

    lax.fori_loop(0, HEADS // 4, step, 0)


def attend_own(place, qs, w_uk, w_uv, kv, floor):
    vmem = pl.BlockSpec(memory_space=pltpu.VMEM)
    smem = pl.BlockSpec(memory_space=pltpu.SMEM)
    rows = NX * SPAN
    return pl.pallas_call(
        own_kernel,
        out_shape=[
            jax.ShapeDtypeStruct((HEADS, rows, WIDE), jnp.bfloat16),
            jax.ShapeDtypeStruct((HEADS, rows, DV), jnp.float32),
            jax.ShapeDtypeStruct((HEADS, rows, STAT), jnp.float32),
            jax.ShapeDtypeStruct((HEADS, rows, STAT), jnp.float32),
        ],
        in_specs=[smem] + [vmem] * 8,
        out_specs=[vmem] * 4,
        scratch_shapes=[pltpu.VMEM((NY * SPAN, WIDE + EXTRA), jnp.bfloat16)],
        compiler_params=pltpu.CompilerParams(vmem_limit_bytes=20 * 1024 * 1024),
        cost_estimate=pl.CostEstimate(flops=6_000_000_000, bytes_accessed=5_000_000, transcendentals=1_000_000),
    )(place, *qs, w_uk, w_uv, kv, floor)


def other_kernel(place_ref, q_ref, floor_ref, kv, sum_ref, top_ref, total_ref, w_uv, out_ref, keys):
    x = (place_ref[0] // 2) % NX
    rows = NX * SPAN
    floor = floor_ref[...]
    fill_keys(keys, kv, NY * SPAN // HALF, None)
    lanes = lax.broadcasted_iota(jnp.int32, (rows, STAT), 1)

    def step(i, level):
        scores = [pair_scores(q_ref, floor, keys, 2 * i + j) for j in range(2)]
        for j, s in enumerate(scores):
            p = 2 * i + j
            values = pair_values(keys, w_uv, p)
            old_top = top_ref[pl.ds(2 * p, 2)].reshape(2 * rows, STAT)
            top = jnp.maximum(old_top, jnp.max(s, axis=1, keepdims=True))
            shrink = jnp.exp2((old_top - top) * SCALE2)
            weight = jnp.exp2((s - wide(top, NY * SPAN // STAT)) * SCALE2)
            sums, totals = weigh(weight, values)
            for k in range(2):
                h = 2 * p + k
                mine = slice(k * rows, (k + 1) * rows)
                total = totals[k] + total_ref[h] * shrink[mine]
                value = ((sums[k] + sum_ref[h] * shrink[mine]) * (1.0 / total)).astype(jnp.bfloat16)
                cols = pl.ds(pl.multiple_of(h * DV, DV), DV)
                for member in range(NX):
                    to = (x + NX - member) % NX
                    out_ref[to, :, cols] = value[member * SPAN : (member + 1) * SPAN]
                level = jnp.where(lanes % HEADS == h, top[mine] * SCALE2 + jnp.log2(total), level)
        return level

    level = lax.fori_loop(0, HEADS // 4, step, jnp.zeros((rows, STAT), jnp.float32))
    high = level.astype(jnp.bfloat16)
    rest = level - high.astype(jnp.float32)
    middle = rest.astype(jnp.bfloat16)
    low = (rest - middle.astype(jnp.float32)).astype(jnp.bfloat16)
    part = lanes // HEADS
    packed = jnp.where(
        part == 0,
        high.astype(jnp.float32),
        jnp.where(part == 1, middle.astype(jnp.float32), jnp.where(part == 2, low.astype(jnp.float32), 0.0)),
    ).astype(jnp.bfloat16)
    for step in range(NX):
        to = (x + NX - step) % NX
        out_ref[to, :, HEADS * DV :] = packed[step * SPAN : (step + 1) * SPAN]


def attend_other(place, q_all, floor, kv, state, w_uv):
    vmem = pl.BlockSpec(memory_space=pltpu.VMEM)
    smem = pl.BlockSpec(memory_space=pltpu.SMEM)
    rows = NX * SPAN
    return pl.pallas_call(
        other_kernel,
        out_shape=jax.ShapeDtypeStruct((NX, SPAN, HEADS * DV + STAT), jnp.bfloat16),
        in_specs=[smem] + [vmem] * 7,
        out_specs=vmem,
        scratch_shapes=[pltpu.VMEM((NY * SPAN, WIDE + EXTRA), jnp.bfloat16)],
        compiler_params=pltpu.CompilerParams(vmem_limit_bytes=20 * 1024 * 1024),
        cost_estimate=pl.CostEstimate(flops=4_000_000_000, bytes_accessed=5_000_000, transcendentals=1_000_000),
    )(place, q_all, floor, kv, *state, w_uv)


def merge_kernel(p_ref, out_ref, held, sems):
    levels = []
    for x in range(NX):
        pieces = p_ref[x, :, :, HEADS * DV :].astype(jnp.float32).reshape(SPAN, STAT)
        rest = pltpu.roll(pieces, STAT - HEADS, 1) + pltpu.roll(pieces, STAT - 2 * HEADS, 1)
        levels.append(pieces + rest)
    top = functools.reduce(jnp.maximum, levels)
    shares = [jnp.exp2(level - top) for level in levels]
    whole = functools.reduce(jnp.add, shares)
    shares = [share / whole for share in shares]
    tokens = SPAN // NZ
    moves = []
    for z in range(NZ):
        here = slice(z * tokens, (z + 1) * tokens)
        for h in range(HEADS):
            acc = jnp.zeros((tokens, DV), jnp.float32)
            for x in range(NX):
                acc = acc + shares[x][here, h : h + 1] * p_ref[x, z, :, h * DV : (h + 1) * DV].astype(jnp.float32)
            held[:, (z * HEADS + h) * DV : (z * HEADS + h + 1) * DV] = acc.astype(jnp.bfloat16)
        cols = slice(z * HEADS * DV, (z + 1) * HEADS * DV)
        moves.append(pltpu.make_async_copy(held.at[:, cols], out_ref.at[:, cols], sems.at[z]))
        moves[-1].start()
    for move in moves:
        move.wait()


def merge(parts):
    vmem = pl.BlockSpec(memory_space=pltpu.VMEM)
    return pl.pallas_call(
        merge_kernel,
        out_shape=jax.ShapeDtypeStruct((SPAN // NZ, NZ * HEADS * DV), jnp.bfloat16),
        in_specs=[vmem],
        out_specs=pl.BlockSpec(memory_space=pl.ANY),
        scratch_shapes=[
            pltpu.VMEM((SPAN // NZ, NZ * HEADS * DV), jnp.bfloat16),
            pltpu.SemaphoreType.DMA((NZ,)),
        ],
        compiler_params=pltpu.CompilerParams(vmem_limit_bytes=8 * 1024 * 1024),
        cost_estimate=pl.CostEstimate(flops=1_000_000, bytes_accessed=800_000, transcendentals=2000),
    )(parts)


def on_device(queries, latent, rope_key, w_uk, w_uv, block_order):
    place = lax.axis_index(CTX).astype(jnp.int32).reshape(1)
    floor = make_floor(jnp.concatenate([place, block_order]))
    both = spread(queries, latent, rope_key)
    both = lax.all_to_all(both, "z", split_axis=0, concat_axis=0, tiled=True).reshape(SPAN, HEADS * DQ + WIDE)
    q_own, kv = pack(both, floor)
    kv_own = lax.all_to_all(kv, "y", split_axis=0, concat_axis=0, tiled=True)
    kv_sib = lax.ppermute(kv_own, "core", CORE_SWAP)
    qs = [q_own] + [lax.ppermute(q_own, "x", along_x(step)) for step in range(1, NX)]
    q_all, *state = attend_own(place, qs, w_uk, w_uv, kv_own, floor)
    partial = attend_other(place, q_all, floor, kv_sib, state, w_uv)
    rows = SPAN // NZ
    partial = partial.reshape(NX * NZ, rows, HEADS * DV + STAT)
    parts = lax.all_to_all(partial, ("x", "z"), split_axis=0, concat_axis=0, tiled=True)
    return merge(parts.reshape(NX, NZ, rows, HEADS * DV + STAT))


def solution(mesh):
    fine = jax.sharding.Mesh(mesh.devices.reshape(NY, NX, 2, NZ), ("y", "x", "core", "z"))
    tokens = P(("y", "x", "core", "z"), None)
    in_specs = (tokens, tokens, tokens, P("z", None, None), P("z", None, None), P())
    return jax.shard_map(on_device, mesh=fine, in_specs=in_specs, out_specs=tokens, check_vma=False)
```

```python
import functools

import jax
import jax.numpy as jnp
from jax import lax
from jax.experimental import pallas as pl
from jax.experimental.pallas import tpu as pltpu
from jax.sharding import PartitionSpec as P

HALF = 32
DL = 512
DR = 64
DN = 128
DV = 128
DQ = DN + DR
WIDE = 640
STAT = 128
EXTRA = 128
NX = 4
NY = 8
NZ = 8
HEADS = 8
SPAN = 64
LANES = 128
PACKED = DL // LANES * SPAN + HALF
FLOOR_SCORE = -1e30
LOG2E = 1.4426950408889634
SCALE2 = DQ ** (-0.5) * LOG2E


def along_x(step):
    return [(x, (x + step) % NX) for x in range(NX)]


CORE_SWAP = [(0, 1), (1, 0)]
CTX = ("y", "x", "core")


def spread_kernel(q_ref, lat_ref, rope_ref, out_ref):
    end = HEADS * DQ
    for z in range(NZ):
        out_ref[z, :, :end] = q_ref[:, z * end : (z + 1) * end]
        out_ref[z, :, end : end + DL] = lat_ref[...]
        out_ref[z, :, end + DL : end + DL + DR] = rope_ref[...]
        out_ref[z, :, end + DL + DR :] = jnp.zeros_like(rope_ref)


def spread(queries, latent, rope_key):
    vmem = pl.BlockSpec(memory_space=pltpu.VMEM)
    return pl.pallas_call(
        spread_kernel,
        out_shape=jax.ShapeDtypeStruct((NZ, SPAN // NZ, HEADS * DQ + WIDE), jnp.bfloat16),
        in_specs=[vmem] * 3,
        out_specs=vmem,
        compiler_params=pltpu.CompilerParams(vmem_limit_bytes=60 * 1024 * 1024),
        cost_estimate=pl.CostEstimate(flops=1_000_000, bytes_accessed=500_000, transcendentals=0),
    )(queries, latent, rope_key)


def pack_kernel(both_ref, floor_ref, q_ref, kv_ref):
    del floor_ref
    q_ref[...] = both_ref[:, : HEADS * DQ]
    rope = both_ref[:, HEADS * DQ + DL : HEADS * DQ + DL + DR]
    for to in range(NY):
        for j in range(DL // LANES):
            col = HEADS * DQ + j * LANES
            kv_ref[to, j * SPAN : (j + 1) * SPAN] = both_ref[:, col : col + LANES]
        kv_ref[to, PACKED - HALF :, :DR] = rope[:HALF]
        kv_ref[to, PACKED - HALF :, DR:] = rope[HALF:]


def pack(both, floor):
    vmem = pl.BlockSpec(memory_space=pltpu.VMEM)
    return pl.pallas_call(
        pack_kernel,
        out_shape=[
            jax.ShapeDtypeStruct((SPAN, HEADS * DQ), jnp.bfloat16),
            jax.ShapeDtypeStruct((NY, PACKED, LANES), jnp.bfloat16),
        ],
        in_specs=[vmem] + [pl.BlockSpec(memory_space=pl.ANY)],
        out_specs=[vmem] * 2,
        compiler_params=pltpu.CompilerParams(vmem_limit_bytes=8 * 1024 * 1024),
        cost_estimate=pl.CostEstimate(flops=4_000_000_000, bytes_accessed=1_000_000, transcendentals=0),
    )(both, floor)


def fill_keys(keys, kv, first, own_block):
    count = NY * SPAN
    blocks = 2 * count // HALF
    for b in range(NY):
        here = slice(b * SPAN, (b + 1) * SPAN)
        for j in range(DL // LANES):
            keys[here, j * LANES : (j + 1) * LANES] = kv[b, j * SPAN : (j + 1) * SPAN]
        keys[b * SPAN : b * SPAN + HALF, DL : DL + DR] = kv[b, PACKED - HALF :, :DR]
        keys[b * SPAN + HALF : (b + 1) * SPAN, DL : DL + DR] = kv[b, PACKED - HALF :, DR:]
    keys[:, DL + DR : WIDE] = jnp.zeros((count, WIDE - DL - DR), jnp.bfloat16)
    key = lax.broadcasted_iota(jnp.int32, (count, EXTRA), 0)
    col = lax.broadcasted_iota(jnp.int32, (count, EXTRA), 1)
    ones = col == key // HALF + first
    if own_block is not None:
        in_own = (key // HALF == own_block) | (key // HALF == own_block + 1)
        ones = ones | (in_own & (col == blocks + key - own_block * HALF))
    keys[:, WIDE:] = jnp.where(ones, 1.0, 0.0).astype(jnp.bfloat16)


def pair_scores(q_ref, floor, keys, p):
    rows = NX * SPAN
    q = jnp.concatenate(
        [q_ref[2 * p : 2 * p + 2].reshape(2 * rows, WIDE), jnp.concatenate([floor, floor], axis=0)], axis=1
    )
    return lax.dot_general(q, keys[...], (((1,), (1,)), ((), ())), preferred_element_type=jnp.float32)


def pair_values(keys, w_uv, p):
    w = jnp.concatenate([w_uv[2 * p], w_uv[2 * p + 1]], axis=1)
    values = jnp.dot(keys[:, :DL], w, preferred_element_type=jnp.float32).astype(jnp.bfloat16)
    ones = jnp.ones((NY * SPAN, STAT), jnp.bfloat16)
    return [jnp.concatenate([values[:, i * DV : (i + 1) * DV], ones], axis=1) for i in range(2)]


def weigh(weight, values):
    rows = NX * SPAN
    weight = weight.astype(jnp.bfloat16)
    both = [
        jnp.dot(weight[i * rows : (i + 1) * rows], values[i], preferred_element_type=jnp.float32) for i in range(2)
    ]
    return [one[:, :DV] for one in both], [one[:, DV:] for one in both]


def wide(value, count):
    return jnp.concatenate([value] * count, axis=1)


def floors_of(info_ref):
    me = info_ref[0]
    core = me % 2
    x = (me // 2) % NX
    y = me // (2 * NX)
    blocks = 2 * NY * SPAN // HALF
    lane = lax.broadcasted_iota(jnp.int32, (HALF, EXTRA), 1)
    token = lax.broadcasted_iota(jnp.int32, (HALF, EXTRA), 0)
    key_block = jnp.zeros((HALF, EXTRA), jnp.int32)
    for which in range(blocks):
        side_core = core if which < blocks // 2 else 1 - core
        slot = (((which // 2) % NY) * NX + x) * 2 + side_core
        key_block = jnp.where(lane == which, info_ref[1 + 2 * slot + which % 2], key_block)
    floors = []
    for step in range(NX):
        slot = (y * NX + (x - step + NX) % NX) * 2 + core
        for half in range(2):
            ahead = (lane < blocks) & (key_block > info_ref[1 + 2 * slot + half])
            if step == 0:
                own = lane - blocks - half * HALF
                ahead = ahead | ((own >= 0) & (own < HALF) & (own > token))
            floors.append(jnp.where(ahead, FLOOR_SCORE, 0.0))
    return jnp.concatenate(floors, axis=0).astype(jnp.bfloat16)


def floor_kernel(info_ref, floor_ref):
    floor_ref[...] = floors_of(info_ref)


def make_floor(info):
    vmem = pl.BlockSpec(memory_space=pltpu.VMEM)
    smem = pl.BlockSpec(memory_space=pltpu.SMEM)
    return pl.pallas_call(
        floor_kernel,
        out_shape=jax.ShapeDtypeStruct((NX * SPAN, EXTRA), jnp.bfloat16),
        in_specs=[smem],
        out_specs=vmem,
        compiler_params=pltpu.CompilerParams(vmem_limit_bytes=8 * 1024 * 1024),
        cost_estimate=pl.CostEstimate(flops=4_000_000_000, bytes_accessed=500_000, transcendentals=0),
    )(info)


def own_kernel(place_ref, q0, q1, q2, q3, w_uk, w_uv, kv, floor_ref, q_ref, sum_ref, top_ref, total_ref, keys):
    rows = NX * SPAN
    floor = floor_ref[...]
    none = jnp.zeros((rows, WIDE - DL - DR), jnp.bfloat16)

    def fill_queries(h):
        here = slice(h * DQ, (h + 1) * DQ)
        q = jnp.concatenate([q0[:, here], q1[:, here], q2[:, here], q3[:, here]], axis=0)
        q_lat = lax.dot_general(
            q[:, :DN], w_uk[h], (((1,), (1,)), ((), ())), preferred_element_type=jnp.float32
        )
        q_ref[h, :, :DL] = q_lat.astype(jnp.bfloat16)
        q_ref[h, :, DL : DL + DR] = q[:, DN:]
        q_ref[h, :, DL + DR : WIDE] = none

    fill_queries(0)
    fill_queries(1)
    fill_keys(keys, kv, 0, place_ref[0] // (2 * NX) * 2)
    ahead = [pair_scores(q_ref, floor, keys, 0)]
    fill_queries(2)
    fill_queries(3)
    ahead.append(pair_scores(q_ref, floor, keys, 1))
    later = pair_values(keys, w_uv, 0)
    for p in range(HEADS // 2):
        s, values = ahead.pop(0), later
        if p + 2 < HEADS // 2:
            fill_queries(2 * p + 4)
            fill_queries(2 * p + 5)
            ahead.append(pair_scores(q_ref, floor, keys, p + 2))
        if p + 1 < HEADS // 2:
            later = pair_values(keys, w_uv, p + 1)
        top = jnp.max(s, axis=1, keepdims=True)
        weight = jnp.exp2((s - top) * SCALE2)
        sums, totals = weigh(weight, values)
        for i in range(2):
            sum_ref[2 * p + i] = sums[i]
            total_ref[2 * p + i] = totals[i]
        pair = slice(2 * p, 2 * p + 2)
        top_ref[pair] = jnp.broadcast_to(top, (2 * rows, STAT)).reshape(2, rows, STAT)


def attend_own(place, qs, w_uk, w_uv, kv, floor):
    vmem = pl.BlockSpec(memory_space=pltpu.VMEM)
    smem = pl.BlockSpec(memory_space=pltpu.SMEM)
    rows = NX * SPAN
    return pl.pallas_call(
        own_kernel,
        out_shape=[
            jax.ShapeDtypeStruct((HEADS, rows, WIDE), jnp.bfloat16),
            jax.ShapeDtypeStruct((HEADS, rows, DV), jnp.float32),
            jax.ShapeDtypeStruct((HEADS, rows, STAT), jnp.float32),
            jax.ShapeDtypeStruct((HEADS, rows, STAT), jnp.float32),
        ],
        in_specs=[smem] + [vmem] * 8,
        out_specs=[vmem] * 4,
        scratch_shapes=[pltpu.VMEM((NY * SPAN, WIDE + EXTRA), jnp.bfloat16)],
        compiler_params=pltpu.CompilerParams(vmem_limit_bytes=20 * 1024 * 1024),
        cost_estimate=pl.CostEstimate(flops=6_000_000_000, bytes_accessed=5_000_000, transcendentals=1_000_000),
    )(place, *qs, w_uk, w_uv, kv, floor)


def other_kernel(place_ref, q_ref, floor_ref, kv, sum_ref, top_ref, total_ref, w_uv, out_ref, keys):
    x = (place_ref[0] // 2) % NX
    rows = NX * SPAN
    floor = floor_ref[...]
    fill_keys(keys, kv, NY * SPAN // HALF, None)
    lanes = lax.broadcasted_iota(jnp.int32, (rows, STAT), 1)
    level = jnp.zeros((rows, STAT), jnp.float32)
    ahead = [pair_scores(q_ref, floor, keys, p) for p in range(2)]
    later = pair_values(keys, w_uv, 0)
    for p in range(HEADS // 2):
        s, values = ahead.pop(0), later
        if p + 2 < HEADS // 2:
            ahead.append(pair_scores(q_ref, floor, keys, p + 2))
        if p + 1 < HEADS // 2:
            later = pair_values(keys, w_uv, p + 1)
        pair = slice(2 * p, 2 * p + 2)
        old_top = top_ref[pair].reshape(2 * rows, STAT)
        top = jnp.maximum(old_top, jnp.max(s, axis=1, keepdims=True))
        shrink = jnp.exp2((old_top - top) * SCALE2)
        weight = jnp.exp2((s - wide(top, NY * SPAN // STAT)) * SCALE2)
        sums, totals = weigh(weight, values)
        for i in range(2):
            h = 2 * p + i
            mine = slice(i * rows, (i + 1) * rows)
            total = totals[i] + total_ref[h] * shrink[mine]
            value = ((sums[i] + sum_ref[h] * shrink[mine]) * (1.0 / total)).astype(jnp.bfloat16)
            for step in range(NX):
                to = (x + NX - step) % NX
                out_ref[to, :, h * DV : (h + 1) * DV] = value[step * SPAN : (step + 1) * SPAN]
            level = jnp.where(lanes % HEADS == h, top[mine] * SCALE2 + jnp.log2(total), level)
    high = level.astype(jnp.bfloat16)
    rest = level - high.astype(jnp.float32)
    middle = rest.astype(jnp.bfloat16)
    low = (rest - middle.astype(jnp.float32)).astype(jnp.bfloat16)
    part = lanes // HEADS
    packed = jnp.where(
        part == 0,
        high.astype(jnp.float32),
        jnp.where(part == 1, middle.astype(jnp.float32), jnp.where(part == 2, low.astype(jnp.float32), 0.0)),
    ).astype(jnp.bfloat16)
    for step in range(NX):
        to = (x + NX - step) % NX
        out_ref[to, :, HEADS * DV :] = packed[step * SPAN : (step + 1) * SPAN]


def attend_other(place, q_all, floor, kv, state, w_uv):
    vmem = pl.BlockSpec(memory_space=pltpu.VMEM)
    smem = pl.BlockSpec(memory_space=pltpu.SMEM)
    rows = NX * SPAN
    return pl.pallas_call(
        other_kernel,
        out_shape=jax.ShapeDtypeStruct((NX, SPAN, HEADS * DV + STAT), jnp.bfloat16),
        in_specs=[smem] + [vmem] * 7,
        out_specs=vmem,
        scratch_shapes=[pltpu.VMEM((NY * SPAN, WIDE + EXTRA), jnp.bfloat16)],
        compiler_params=pltpu.CompilerParams(vmem_limit_bytes=20 * 1024 * 1024),
        cost_estimate=pl.CostEstimate(flops=4_000_000_000, bytes_accessed=5_000_000, transcendentals=1_000_000),
    )(place, q_all, floor, kv, *state, w_uv)


def merge_kernel(p_ref, out_ref, held, sems):
    levels = []
    for x in range(NX):
        pieces = p_ref[x, :, :, HEADS * DV :].astype(jnp.float32).reshape(SPAN, STAT)
        rest = pltpu.roll(pieces, STAT - HEADS, 1) + pltpu.roll(pieces, STAT - 2 * HEADS, 1)
        levels.append(pieces + rest)
    top = functools.reduce(jnp.maximum, levels)
    shares = [jnp.exp2(level - top) for level in levels]
    whole = functools.reduce(jnp.add, shares)
    shares = [share / whole for share in shares]
    tokens = SPAN // NZ
    moves = []
    for z in range(NZ):
        here = slice(z * tokens, (z + 1) * tokens)
        for h in range(HEADS):
            acc = jnp.zeros((tokens, DV), jnp.float32)
            for x in range(NX):
                acc = acc + shares[x][here, h : h + 1] * p_ref[x, z, :, h * DV : (h + 1) * DV].astype(jnp.float32)
            held[:, (z * HEADS + h) * DV : (z * HEADS + h + 1) * DV] = acc.astype(jnp.bfloat16)
        cols = slice(z * HEADS * DV, (z + 1) * HEADS * DV)
        moves.append(pltpu.make_async_copy(held.at[:, cols], out_ref.at[:, cols], sems.at[z]))
        moves[-1].start()
    for move in moves:
        move.wait()


def merge(parts):
    vmem = pl.BlockSpec(memory_space=pltpu.VMEM)
    return pl.pallas_call(
        merge_kernel,
        out_shape=jax.ShapeDtypeStruct((SPAN // NZ, NZ * HEADS * DV), jnp.bfloat16),
        in_specs=[vmem],
        out_specs=pl.BlockSpec(memory_space=pl.ANY),
        scratch_shapes=[
            pltpu.VMEM((SPAN // NZ, NZ * HEADS * DV), jnp.bfloat16),
            pltpu.SemaphoreType.DMA((NZ,)),
        ],
        compiler_params=pltpu.CompilerParams(vmem_limit_bytes=8 * 1024 * 1024),
        cost_estimate=pl.CostEstimate(flops=1_000_000, bytes_accessed=800_000, transcendentals=2000),
    )(parts)


def on_device(queries, latent, rope_key, w_uk, w_uv, block_order):
    place = lax.axis_index(CTX).astype(jnp.int32).reshape(1)
    floor = make_floor(jnp.concatenate([place, block_order]))
    both = spread(queries, latent, rope_key)
    both = lax.all_to_all(both, "z", split_axis=0, concat_axis=0, tiled=True).reshape(SPAN, HEADS * DQ + WIDE)
    q_own, kv = pack(both, floor)
    kv_own = lax.all_to_all(kv, "y", split_axis=0, concat_axis=0, tiled=True)
    kv_sib = lax.ppermute(kv_own, "core", CORE_SWAP)
    qs = [q_own] + [lax.ppermute(q_own, "x", along_x(step)) for step in range(1, NX)]
    q_all, *state = attend_own(place, qs, w_uk, w_uv, kv_own, floor)
    partial = attend_other(place, q_all, floor, kv_sib, state, w_uv)
    rows = SPAN // NZ
    partial = partial.reshape(NX * NZ, rows, HEADS * DV + STAT)
    parts = lax.all_to_all(partial, ("x", "z"), split_axis=0, concat_axis=0, tiled=True)
    return merge(parts.reshape(NX, NZ, rows, HEADS * DV + STAT))


def solution(mesh):
    fine = jax.sharding.Mesh(mesh.devices.reshape(NY, NX, 2, NZ), ("y", "x", "core", "z"))
    tokens = P(("y", "x", "core", "z"), None)
    in_specs = (tokens, tokens, tokens, P("z", None, None), P("z", None, None), P())
    return jax.shard_map(on_device, mesh=fine, in_specs=in_specs, out_specs=tokens, check_vma=False)
```

```python
import functools

import jax
import jax.numpy as jnp
from jax import lax
from jax.experimental import pallas as pl
from jax.experimental.pallas import tpu as pltpu
from jax.sharding import PartitionSpec as P

HALF = 32
DL = 512
DR = 64
DN = 128
DV = 128
DQ = DN + DR
WIDE = 640
STAT = 128
EXTRA = 128
NX = 4
NY = 8
NZ = 8
HEADS = 8
SPAN = 64
LANES = 128
PACKED = DL // LANES * SPAN + HALF
FLOOR_SCORE = -1e30
LOG2E = 1.4426950408889634
SCALE2 = DQ ** (-0.5) * LOG2E


def along_x(step):
    return [(x, (x + step) % NX) for x in range(NX)]


CORE_SWAP = [(0, 1), (1, 0)]
CTX = ("y", "x", "core")


def spread_kernel(q_ref, lat_ref, rope_ref, out_ref):
    end = HEADS * DQ
    for z in range(NZ):
        out_ref[z, :, :end] = q_ref[:, z * end : (z + 1) * end]
        out_ref[z, :, end : end + DL] = lat_ref[...]
        out_ref[z, :, end + DL : end + DL + DR] = rope_ref[...]
        out_ref[z, :, end + DL + DR :] = jnp.zeros_like(rope_ref)


def spread(queries, latent, rope_key):
    vmem = pl.BlockSpec(memory_space=pltpu.VMEM)
    return pl.pallas_call(
        spread_kernel,
        out_shape=jax.ShapeDtypeStruct((NZ, SPAN // NZ, HEADS * DQ + WIDE), jnp.bfloat16),
        in_specs=[vmem] * 3,
        out_specs=vmem,
        compiler_params=pltpu.CompilerParams(vmem_limit_bytes=60 * 1024 * 1024),
        cost_estimate=pl.CostEstimate(flops=1_000_000, bytes_accessed=500_000, transcendentals=0),
    )(queries, latent, rope_key)


def pack_kernel(both_ref, floor_ref, q_ref, kv_ref):
    del floor_ref
    q_ref[...] = both_ref[:, : HEADS * DQ]
    rope = both_ref[:, HEADS * DQ + DL : HEADS * DQ + DL + DR]
    for to in range(NY):
        for j in range(DL // LANES):
            col = HEADS * DQ + j * LANES
            kv_ref[to, j * SPAN : (j + 1) * SPAN] = both_ref[:, col : col + LANES]
        kv_ref[to, PACKED - HALF :, :DR] = rope[:HALF]
        kv_ref[to, PACKED - HALF :, DR:] = rope[HALF:]


def pack(both, floor):
    vmem = pl.BlockSpec(memory_space=pltpu.VMEM)
    return pl.pallas_call(
        pack_kernel,
        out_shape=[
            jax.ShapeDtypeStruct((SPAN, HEADS * DQ), jnp.bfloat16),
            jax.ShapeDtypeStruct((NY, PACKED, LANES), jnp.bfloat16),
        ],
        in_specs=[vmem] + [pl.BlockSpec(memory_space=pl.ANY)],
        out_specs=[vmem] * 2,
        compiler_params=pltpu.CompilerParams(vmem_limit_bytes=8 * 1024 * 1024),
        cost_estimate=pl.CostEstimate(flops=4_000_000_000, bytes_accessed=1_000_000, transcendentals=0),
    )(both, floor)


def fill_keys(keys, kv, first, own_block):
    count = NY * SPAN
    blocks = 2 * count // HALF
    for b in range(NY):
        here = slice(b * SPAN, (b + 1) * SPAN)
        for j in range(DL // LANES):
            keys[here, j * LANES : (j + 1) * LANES] = kv[b, j * SPAN : (j + 1) * SPAN]
        keys[b * SPAN : b * SPAN + HALF, DL : DL + DR] = kv[b, PACKED - HALF :, :DR]
        keys[b * SPAN + HALF : (b + 1) * SPAN, DL : DL + DR] = kv[b, PACKED - HALF :, DR:]
    keys[:, DL + DR : WIDE] = jnp.zeros((count, WIDE - DL - DR), jnp.bfloat16)
    key = lax.broadcasted_iota(jnp.int32, (count, EXTRA), 0)
    col = lax.broadcasted_iota(jnp.int32, (count, EXTRA), 1)
    ones = col == key // HALF + first
    if own_block is not None:
        in_own = (key // HALF == own_block) | (key // HALF == own_block + 1)
        ones = ones | (in_own & (col == blocks + key - own_block * HALF))
    keys[:, WIDE:] = jnp.where(ones, 1.0, 0.0).astype(jnp.bfloat16)


def pair_scores(q_ref, floor, keys, p):
    rows = NX * SPAN
    q = jnp.concatenate(
        [q_ref[2 * p : 2 * p + 2].reshape(2 * rows, WIDE), jnp.concatenate([floor, floor], axis=0)], axis=1
    )
    return lax.dot_general(q, keys[...], (((1,), (1,)), ((), ())), preferred_element_type=jnp.float32)


def pair_values(keys, w_uv, p):
    w = jnp.concatenate([w_uv[2 * p], w_uv[2 * p + 1]], axis=1)
    values = jnp.dot(keys[:, :DL], w, preferred_element_type=jnp.float32).astype(jnp.bfloat16)
    ones = jnp.ones((NY * SPAN, STAT), jnp.bfloat16)
    return [jnp.concatenate([values[:, i * DV : (i + 1) * DV], ones], axis=1) for i in range(2)]


def weigh(weight, values):
    rows = NX * SPAN
    weight = weight.astype(jnp.bfloat16)
    both = [
        jnp.dot(weight[i * rows : (i + 1) * rows], values[i], preferred_element_type=jnp.float32) for i in range(2)
    ]
    return [one[:, :DV] for one in both], [one[:, DV:] for one in both]


def wide(value, count):
    return jnp.concatenate([value] * count, axis=1)


def floors_of(info_ref):
    me = info_ref[0]
    core = me % 2
    x = (me // 2) % NX
    y = me // (2 * NX)
    blocks = 2 * NY * SPAN // HALF
    lane = lax.broadcasted_iota(jnp.int32, (HALF, EXTRA), 1)
    token = lax.broadcasted_iota(jnp.int32, (HALF, EXTRA), 0)
    key_block = jnp.zeros((HALF, EXTRA), jnp.int32)
    for which in range(blocks):
        side_core = core if which < blocks // 2 else 1 - core
        slot = (((which // 2) % NY) * NX + x) * 2 + side_core
        key_block = jnp.where(lane == which, info_ref[1 + 2 * slot + which % 2], key_block)
    floors = []
    for step in range(NX):
        slot = (y * NX + (x - step + NX) % NX) * 2 + core
        for half in range(2):
            ahead = (lane < blocks) & (key_block > info_ref[1 + 2 * slot + half])
            if step == 0:
                own = lane - blocks - half * HALF
                ahead = ahead | ((own >= 0) & (own < HALF) & (own > token))
            floors.append(jnp.where(ahead, FLOOR_SCORE, 0.0))
    return jnp.concatenate(floors, axis=0).astype(jnp.bfloat16)


def floor_kernel(info_ref, floor_ref):
    floor_ref[...] = floors_of(info_ref)


def make_floor(info):
    vmem = pl.BlockSpec(memory_space=pltpu.VMEM)
    smem = pl.BlockSpec(memory_space=pltpu.SMEM)
    return pl.pallas_call(
        floor_kernel,
        out_shape=jax.ShapeDtypeStruct((NX * SPAN, EXTRA), jnp.bfloat16),
        in_specs=[smem],
        out_specs=vmem,
        compiler_params=pltpu.CompilerParams(vmem_limit_bytes=8 * 1024 * 1024),
        cost_estimate=pl.CostEstimate(flops=4_000_000_000, bytes_accessed=500_000, transcendentals=0),
    )(info)


def own_kernel(place_ref, q0, q1, q2, q3, w_uk, w_uv, kv, floor_ref, q_ref, sum_ref, top_ref, total_ref, keys):
    rows = NX * SPAN
    floor = floor_ref[...]
    none = jnp.zeros((rows, WIDE - DL - DR), jnp.bfloat16)

    def fill_queries(h):
        here = slice(h * DQ, (h + 1) * DQ)
        q = jnp.concatenate([q0[:, here], q1[:, here], q2[:, here], q3[:, here]], axis=0)
        q_lat = lax.dot_general(
            q[:, :DN], w_uk[h], (((1,), (1,)), ((), ())), preferred_element_type=jnp.float32
        )
        q_ref[h, :, :DL] = q_lat.astype(jnp.bfloat16)
        q_ref[h, :, DL : DL + DR] = q[:, DN:]
        q_ref[h, :, DL + DR : WIDE] = none

    fill_queries(0)
    fill_queries(1)
    fill_keys(keys, kv, 0, place_ref[0] // (2 * NX) * 2)
    ahead = [pair_scores(q_ref, floor, keys, 0)]
    fill_queries(2)
    fill_queries(3)
    ahead.append(pair_scores(q_ref, floor, keys, 1))
    fill_queries(4)
    fill_queries(5)
    ahead.append(pair_scores(q_ref, floor, keys, 2))
    later = [pair_values(keys, w_uv, p) for p in range(2)]
    for p in range(HEADS // 2):
        s, values = ahead.pop(0), later.pop(0)
        if p + 3 < HEADS // 2:
            fill_queries(2 * p + 6)
            fill_queries(2 * p + 7)
            ahead.append(pair_scores(q_ref, floor, keys, p + 3))
        if p + 2 < HEADS // 2:
            later.append(pair_values(keys, w_uv, p + 2))
        top = jnp.max(s, axis=1, keepdims=True)
        weight = jnp.exp2((s - top) * SCALE2)
        sums, totals = weigh(weight, values)
        for i in range(2):
            sum_ref[2 * p + i] = sums[i]
            total_ref[2 * p + i] = totals[i]
        pair = slice(2 * p, 2 * p + 2)
        top_ref[pair] = jnp.broadcast_to(top, (2 * rows, STAT)).reshape(2, rows, STAT)


def attend_own(place, qs, w_uk, w_uv, kv, floor):
    vmem = pl.BlockSpec(memory_space=pltpu.VMEM)
    smem = pl.BlockSpec(memory_space=pltpu.SMEM)
    rows = NX * SPAN
    return pl.pallas_call(
        own_kernel,
        out_shape=[
            jax.ShapeDtypeStruct((HEADS, rows, WIDE), jnp.bfloat16),
            jax.ShapeDtypeStruct((HEADS, rows, DV), jnp.float32),
            jax.ShapeDtypeStruct((HEADS, rows, STAT), jnp.float32),
            jax.ShapeDtypeStruct((HEADS, rows, STAT), jnp.float32),
        ],
        in_specs=[smem] + [vmem] * 8,
        out_specs=[vmem] * 4,
        scratch_shapes=[pltpu.VMEM((NY * SPAN, WIDE + EXTRA), jnp.bfloat16)],
        compiler_params=pltpu.CompilerParams(vmem_limit_bytes=20 * 1024 * 1024),
        cost_estimate=pl.CostEstimate(flops=6_000_000_000, bytes_accessed=5_000_000, transcendentals=1_000_000),
    )(place, *qs, w_uk, w_uv, kv, floor)


def other_kernel(place_ref, q_ref, floor_ref, kv, sum_ref, top_ref, total_ref, w_uv, out_ref, keys):
    x = (place_ref[0] // 2) % NX
    rows = NX * SPAN
    floor = floor_ref[...]
    fill_keys(keys, kv, NY * SPAN // HALF, None)
    lanes = lax.broadcasted_iota(jnp.int32, (rows, STAT), 1)
    level = jnp.zeros((rows, STAT), jnp.float32)
    ahead = [pair_scores(q_ref, floor, keys, p) for p in range(3)]
    later = [pair_values(keys, w_uv, p) for p in range(2)]
    for p in range(HEADS // 2):
        s, values = ahead.pop(0), later.pop(0)
        if p + 3 < HEADS // 2:
            ahead.append(pair_scores(q_ref, floor, keys, p + 3))
        if p + 2 < HEADS // 2:
            later.append(pair_values(keys, w_uv, p + 2))
        pair = slice(2 * p, 2 * p + 2)
        old_top = top_ref[pair].reshape(2 * rows, STAT)
        top = jnp.maximum(old_top, jnp.max(s, axis=1, keepdims=True))
        shrink = jnp.exp2((old_top - top) * SCALE2)
        weight = jnp.exp2((s - wide(top, NY * SPAN // STAT)) * SCALE2)
        sums, totals = weigh(weight, values)
        for i in range(2):
            h = 2 * p + i
            mine = slice(i * rows, (i + 1) * rows)
            total = totals[i] + total_ref[h] * shrink[mine]
            value = ((sums[i] + sum_ref[h] * shrink[mine]) * (1.0 / total)).astype(jnp.bfloat16)
            for step in range(NX):
                to = (x + NX - step) % NX
                out_ref[to, :, h * DV : (h + 1) * DV] = value[step * SPAN : (step + 1) * SPAN]
            level = jnp.where(lanes % HEADS == h, top[mine] * SCALE2 + jnp.log2(total), level)
    high = level.astype(jnp.bfloat16)
    rest = level - high.astype(jnp.float32)
    middle = rest.astype(jnp.bfloat16)
    low = (rest - middle.astype(jnp.float32)).astype(jnp.bfloat16)
    part = lanes // HEADS
    packed = jnp.where(
        part == 0,
        high.astype(jnp.float32),
        jnp.where(part == 1, middle.astype(jnp.float32), jnp.where(part == 2, low.astype(jnp.float32), 0.0)),
    ).astype(jnp.bfloat16)
    for step in range(NX):
        to = (x + NX - step) % NX
        out_ref[to, :, HEADS * DV :] = packed[step * SPAN : (step + 1) * SPAN]


def attend_other(place, q_all, floor, kv, state, w_uv):
    vmem = pl.BlockSpec(memory_space=pltpu.VMEM)
    smem = pl.BlockSpec(memory_space=pltpu.SMEM)
    rows = NX * SPAN
    return pl.pallas_call(
        other_kernel,
        out_shape=jax.ShapeDtypeStruct((NX, SPAN, HEADS * DV + STAT), jnp.bfloat16),
        in_specs=[smem] + [vmem] * 7,
        out_specs=vmem,
        scratch_shapes=[pltpu.VMEM((NY * SPAN, WIDE + EXTRA), jnp.bfloat16)],
        compiler_params=pltpu.CompilerParams(vmem_limit_bytes=20 * 1024 * 1024),
        cost_estimate=pl.CostEstimate(flops=4_000_000_000, bytes_accessed=5_000_000, transcendentals=1_000_000),
    )(place, q_all, floor, kv, *state, w_uv)


def merge_kernel(p_ref, out_ref, held, sems):
    levels = []
    for x in range(NX):
        pieces = p_ref[x, :, :, HEADS * DV :].astype(jnp.float32).reshape(SPAN, STAT)
        rest = pltpu.roll(pieces, STAT - HEADS, 1) + pltpu.roll(pieces, STAT - 2 * HEADS, 1)
        levels.append(pieces + rest)
    top = functools.reduce(jnp.maximum, levels)
    shares = [jnp.exp2(level - top) for level in levels]
    whole = functools.reduce(jnp.add, shares)
    shares = [share / whole for share in shares]
    tokens = SPAN // NZ
    moves = []
    for z in range(NZ):
        here = slice(z * tokens, (z + 1) * tokens)
        for h in range(HEADS):
            acc = jnp.zeros((tokens, DV), jnp.float32)
            for x in range(NX):
                acc = acc + shares[x][here, h : h + 1] * p_ref[x, z, :, h * DV : (h + 1) * DV].astype(jnp.float32)
            held[:, (z * HEADS + h) * DV : (z * HEADS + h + 1) * DV] = acc.astype(jnp.bfloat16)
        cols = slice(z * HEADS * DV, (z + 1) * HEADS * DV)
        moves.append(pltpu.make_async_copy(held.at[:, cols], out_ref.at[:, cols], sems.at[z]))
        moves[-1].start()
    for move in moves:
        move.wait()


def merge(parts):
    vmem = pl.BlockSpec(memory_space=pltpu.VMEM)
    return pl.pallas_call(
        merge_kernel,
        out_shape=jax.ShapeDtypeStruct((SPAN // NZ, NZ * HEADS * DV), jnp.bfloat16),
        in_specs=[vmem],
        out_specs=pl.BlockSpec(memory_space=pl.ANY),
        scratch_shapes=[
            pltpu.VMEM((SPAN // NZ, NZ * HEADS * DV), jnp.bfloat16),
            pltpu.SemaphoreType.DMA((NZ,)),
        ],
        compiler_params=pltpu.CompilerParams(vmem_limit_bytes=8 * 1024 * 1024),
        cost_estimate=pl.CostEstimate(flops=1_000_000, bytes_accessed=800_000, transcendentals=2000),
    )(parts)


def on_device(queries, latent, rope_key, w_uk, w_uv, block_order):
    place = lax.axis_index(CTX).astype(jnp.int32).reshape(1)
    floor = make_floor(jnp.concatenate([place, block_order]))
    both = spread(queries, latent, rope_key)
    both = lax.all_to_all(both, "z", split_axis=0, concat_axis=0, tiled=True).reshape(SPAN, HEADS * DQ + WIDE)
    q_own, kv = pack(both, floor)
    kv_own = lax.all_to_all(kv, "y", split_axis=0, concat_axis=0, tiled=True)
    kv_sib = lax.ppermute(kv_own, "core", CORE_SWAP)
    qs = [q_own] + [lax.ppermute(q_own, "x", along_x(step)) for step in range(1, NX)]
    q_all, *state = attend_own(place, qs, w_uk, w_uv, kv_own, floor)
    partial = attend_other(place, q_all, floor, kv_sib, state, w_uv)
    rows = SPAN // NZ
    partial = partial.reshape(NX * NZ, rows, HEADS * DV + STAT)
    parts = lax.all_to_all(partial, ("x", "z"), split_axis=0, concat_axis=0, tiled=True)
    return merge(parts.reshape(NX, NZ, rows, HEADS * DV + STAT))


def solution(mesh):
    fine = jax.sharding.Mesh(mesh.devices.reshape(NY, NX, 2, NZ), ("y", "x", "core", "z"))
    tokens = P(("y", "x", "core", "z"), None)
    in_specs = (tokens, tokens, tokens, P("z", None, None), P("z", None, None), P())
    return jax.shard_map(on_device, mesh=fine, in_specs=in_specs, out_specs=tokens, check_vma=False)
```
